32 devices in a mesh: panel: 2 (over y), dom: 4 (over z), blk: 2 (over x), dir: 2 (over core).
Axes of the slice: x: 2, y: 2, z: 4, core: 2. Of those that a mesh axis runs over, the one named last changes fastest.
Arguments:
- panel_vectors: bfloat16 [3072, 2048], P('dom', ('panel', 'blk')), parts along dimension 1, may hold values from -6 to 6
- force_blocks: float32 [16, 9, 1024], P(None, None, 'dom'), may hold values from -1 to 1
- bond_vectors: float32 [2, 16, 1024], P('dir', None, 'dom'), may hold values from -4 to 4
- neighbours: int32 [16, 1024], P(None, 'dom'), may hold values from 0 to 511
- boundary_low: int32 [512], P('dom'), may hold values from 0 to 255
- boundary_high: int32 [512], P('dom'), may hold values from 0 to 255
Outputs:
- coupling: float32 [2, 2048, 1024], P('dir', ('panel', 'dom'), 'blk'), parts along dimension 1
The draws below stay inside these ranges and needn't reach their ends.
There are 2 independent parts, one for each index of `panel`. The reference program is written for one: setup_inputs(seed, part) draws one part's arguments, and reference() takes and returns one part's arrays. A program takes and returns all parts, laid end to end along the dimension named above; an argument that names none is the same for every part. Nothing has to cross between parts.
Inputs may be any that keep to these rules, and one draw needn't show every extreme that they name: `neighbours`: an entry below 256 names an atom of the same domain; from 256 to 383 the listed boundary atoms of the domain below; from 384 on those of the domain above. `boundary_low`: local atom numbers within the domain that owns the block; repeats may occur. `boundary_high`: local atom numbers within the domain that owns the block; repeats may occur.
All inputs are finite; a program needn't handle non-finite values.
Results may differ from the reference program's by a relative error of at most 0.0029.
Values may be sent and summed in bfloat16 or wider, within the bound.
No kernel may reach another device: no remote copies, remote signals or barrier semaphores. Data moves between devices by JAX's collectives and lax.ppermute only.
A program may use at most 64 MiB of HBM per device.

```python
import jax
import jax.numpy as jnp
from jax import lax

AD = 256
M = 1024
K = 16
BND = 128
ATOMS = 1024
N_DOM = 4


def set_ends(entries, stream_key, least, top_value):
    longest = entries.shape.index(max(entries.shape))
    spots = []
    for shift in (0, 1):
        where = [jax.random.randint(jax.random.fold_in(stream_key, axis), (), 0, length) for axis, length in enumerate(entries.shape)]
        where[longest] = (where[longest] + shift) % entries.shape[longest]
        spots.append(tuple(where))
    return entries.at[spots[0]].set(least).at[spots[1]].set(top_value)


def block_levels(rng, shape, shards, smallest, high):
    level = 1.0
    for position, blocks in shards:
        draws = jax.random.uniform(jax.random.fold_in(jax.random.fold_in(rng, 6), position), (blocks,), jnp.float32, smallest / len(shards), high / len(shards))
        level = level * jnp.repeat(jnp.exp(draws), shape[position] // blocks).reshape((-1,) + (1,) * (len(shape) - 1 - position))
    return level


def noise(key, extent, spread, reach, shards=(), kind=jnp.bfloat16):
    drawn = spread * jax.random.normal(key, extent, jnp.float32)
    if shards:
        drawn = drawn * block_levels(key, extent, shards, -0.22, 0.18)
    return jnp.clip(drawn, -reach, reach).astype(kind)


def setup_inputs(seed: int = 0, part: int = 0) -> dict:
    streams_of = jax.random.split(jax.random.key(seed), 7)
    own_keys = jax.random.split(jax.random.fold_in(streams_of[6], part), 7)
    return {
        "panel_vectors": noise(own_keys[0], (3 * ATOMS, M), 1.0, 6.0, ((0, 4), (1, 2))),
        "force_blocks": noise(streams_of[1], (K, 9, ATOMS), 0.15, 1.0, ((2, 4),), jnp.float32),
        "bond_vectors": noise(streams_of[2], (2, K, ATOMS), 1.0, 4.0, ((0, 2), (2, 4)), jnp.float32),
        "neighbours": set_ends(jax.random.randint(streams_of[3], (K, ATOMS), 0, AD + 2 * BND), jax.random.fold_in(streams_of[3], 1), 0, (AD + 2 * BND) - 1).astype(jnp.int32),
        "boundary_low": set_ends(jax.random.randint(streams_of[4], (BND * N_DOM,), 0, AD), jax.random.fold_in(streams_of[4], 1), 0, AD - 1).astype(jnp.int32),
        "boundary_high": set_ends(jax.random.randint(streams_of[5], (BND * N_DOM,), 0, AD), jax.random.fold_in(streams_of[5], 1), 0, AD - 1).astype(jnp.int32),
    }


def flux_of(ext, forces, bond, nbrs):
    weights = forces * bond[:, None, :]
    atoms = nbrs.shape[1]

    def step(total, k):
        gathered = ext[nbrs[k]].astype(jnp.float32)
        blocks = weights[k].reshape(3, 3, atoms).transpose(2, 0, 1)
        return total + jnp.sum(blocks[:, :, :, None] * gathered[:, None, :, :], axis=2), None

    init = jnp.zeros((atoms, 3, ext.shape[2]), jnp.float32)
    total, unused = lax.scan(step, init, jnp.arange(K, dtype=jnp.int32))
    return total


def reference(panel_vectors, force_blocks, bond_vectors, neighbours, boundary_low, boundary_high):
    stacked = panel_vectors.reshape(N_DOM, AD, 3, M)

    def domain(d, coupling):
        prev = jnp.mod(d - 1 + N_DOM, N_DOM).astype(jnp.int32)
        nextd = jnp.mod(d + 1, N_DOM).astype(jnp.int32)
        own = lax.dynamic_slice_in_dim(stacked, d, 1, 0)[0]
        low_src = lax.dynamic_slice_in_dim(stacked, prev, 1, 0)[0]
        high_src = lax.dynamic_slice_in_dim(stacked, nextd, 1, 0)[0]
        upper_list = lax.dynamic_slice_in_dim(boundary_high, (prev * BND).astype(jnp.int32), BND, 0)
        lower_list = lax.dynamic_slice_in_dim(boundary_low, (nextd * BND).astype(jnp.int32), BND, 0)
        ext = jnp.concatenate([own, low_src[upper_list], high_src[lower_list]], axis=0)
        start = (d * AD).astype(jnp.int32)
        forces = lax.dynamic_slice_in_dim(force_blocks, start, AD, 2)
        bonds = lax.dynamic_slice_in_dim(bond_vectors, start, AD, 2)
        nbrs = lax.dynamic_slice_in_dim(neighbours, start, AD, 1)
        own_rows = own.reshape(3 * AD, M)
        parts = []
        for c in range(2):
            flux = flux_of(ext, forces, bonds[c], nbrs).astype(jnp.bfloat16).reshape(3 * AD, M)
            parts.append(jnp.dot(own_rows.T, flux, preferred_element_type=jnp.float32))
        return coupling + jnp.stack(parts, axis=0)

    coupling = lax.fori_loop(0, N_DOM, domain, jnp.zeros((2, M, M), jnp.float32))
    return coupling * ((3.0 * ATOMS) ** -0.5)
```

```python
import jax
import jax.numpy as jnp
from jax import lax
from jax.experimental import pallas as pl
from jax.experimental.pallas import tpu as pltpu
from jax.sharding import PartitionSpec as P

GROUP = 16
BF16 = jnp.bfloat16
F32 = jnp.float32


def params(mib=24):
    return pltpu.CompilerParams(vmem_limit_bytes=mib * 1024 * 1024)


def dot(a, b, contract=((1,), (0,))):
    return lax.dot_general(a, b, (contract, ((), ())), preferred_element_type=F32)


def one_hot(mask):
    return jnp.where(mask, 1.0, 0.0).astype(BF16)


def prep_kernel(half_ref, v_ref, low_ref, high_ref, own_ref, send_low_ref, send_high_ref, turned_ref):
    rows, cols = v_ref.shape
    atoms = rows // 3
    half = cols // 2
    v = v_ref[:, pl.ds(pl.multiple_of(half_ref[0] * half, 128), half)]
    lane = lax.broadcasted_iota(jnp.int32, (atoms, rows), 1)
    atom = lax.broadcasted_iota(jnp.int32, (atoms, rows), 0)
    for b in range(3):
        picked = dot(one_hot(lane == 3 * atom + b), v)
        own_ref[b * atoms : (b + 1) * atoms, :] = picked.astype(BF16)
        turned_ref[:, b * atoms : (b + 1) * atoms] = picked.T.astype(BF16)
    for list_ref, out_ref in ((low_ref, send_low_ref), (high_ref, send_high_ref)):
        count = list_ref.shape[1]
        named = jnp.broadcast_to(list_ref[...], (128, count)).T
        lane = lax.broadcasted_iota(jnp.int32, (count, 128), 1)
        for b in range(3):
            wanted = 3 * named + b
            hot = jnp.concatenate(
                [one_hot(lane + t * 128 == wanted) for t in range(rows // 128)], axis=1
            )
            out_ref[b * count : (b + 1) * count, :] = dot(hot, v).astype(BF16)


def weights_kernel(force_ref, bond_ref, near_ref, hi_ref, lo_ref, table_ref):
    steps, nine, atoms = force_ref.shape
    groups = atoms // GROUP
    extent = hi_ref.shape[1] // 3
    lane = lax.broadcasted_iota(jnp.int32, (24, atoms), 1)
    rows = []
    for k in range(steps):
        force = force_ref[k]
        near = near_ref[k : k + 1, :].astype(F32)
        rows.append(
            jnp.concatenate(
                [
                    force * bond_ref[0, k : k + 1, :],
                    force * bond_ref[1, k : k + 1, :],
                    jnp.broadcast_to(near, (6, atoms)),
                ],
                axis=0,
            )
        )
    bit = 1
    while bit < steps:
        taken = ((lane // GROUP) & bit) != 0
        turned = list(rows)
        for p in range(steps):
            if p & bit:
                continue
            q = p | bit
            turned[p] = jnp.where(taken, pltpu.roll(rows[q], GROUP * bit, 1), rows[p])
            turned[q] = jnp.where(taken, rows[q], pltpu.roll(rows[p], atoms - GROUP * bit, 1))
        rows = turned
        bit *= 2
    for g in range(groups):
        table_ref[g] = rows[g]

    mask = (
        lax.broadcasted_iota(jnp.int32, (GROUP, atoms), 1) % GROUP
        == lax.broadcasted_iota(jnp.int32, (GROUP, atoms), 0)
    )
    target = lax.broadcasted_iota(jnp.int32, (extent, atoms), 0).astype(F32)

    def group(g, carry):
        table = table_ref[g]
        hot = one_hot(target == table[18:19, :])
        spread = jnp.concatenate(
            [jnp.where(mask, table[r : r + 1, :], 0.0) for r in range(18)], axis=0
        )
        top = spread.astype(BF16)
        rest = (spread - top.astype(F32)).astype(BF16)
        both = ((1,), (1,))
        dense = dot(top, hot, both) + dot(rest, hot, both)
        hi = dense.astype(BF16)
        lo = (dense - hi.astype(F32)).astype(BF16)
        for e in range(2):
            for a in range(3):
                at = pl.ds(pl.multiple_of((e * 3 + a) * atoms + g * GROUP, GROUP), GROUP)
                for b in range(3):
                    r = (e * 9 + 3 * a + b) * GROUP
                    span = slice(b * extent, (b + 1) * extent)
                    hi_ref[at, span] = hi[r : r + GROUP]
                    lo_ref[at, span] = lo[r : r + GROUP]
        return carry

    lax.fori_loop(0, groups, group, 0)


def couple_kernel(hi_ref, lo_ref, own_ref, below_ref, above_ref, turned_ref, out_ref, ext_ref, flux_ref):
    rows, half = own_ref.shape
    atoms = rows // 3
    count = below_ref.shape[0] // 3
    extent = atoms + 2 * count
    for b in range(3):
        at = b * extent
        ext_ref[at : at + atoms] = own_ref[b * atoms : (b + 1) * atoms]
        ext_ref[at + atoms : at + atoms + count] = below_ref[b * count : (b + 1) * count]
        ext_ref[at + atoms + count : at + extent] = above_ref[b * count : (b + 1) * count]
    ext = ext_ref[...]
    for e in range(2):
        for a in range(3):
            at = (e * 3 + a) * atoms
            flux = dot(hi_ref[at : at + atoms, :], ext) + dot(lo_ref[at : at + atoms, :], ext)
            flux_ref[a * atoms : (a + 1) * atoms, e * half : (e + 1) * half] = flux.astype(BF16)
    flux = flux_ref[...]
    modes = turned_ref.shape[0]
    block = out_ref.shape[1]
    chunk = max(block, min(256, modes))
    for at in range(0, modes, chunk):
        term = dot(turned_ref[at : at + chunk, :], flux).astype(BF16)
        for s in range(chunk // block):
            for e in range(2):
                out_ref[2 * (at // block + s) + e] = term[
                    s * block : (s + 1) * block, e * half : (e + 1) * half
                ]


def sum_kernel(scale, terms_ref, out_ref):
    pairs, block, half = terms_ref.shape
    for c in range(2):
        total = terms_ref[c].astype(F32)
        for d in range(1, pairs // 2):
            total = total + terms_ref[2 * d + c].astype(F32)
        out_ref[0, :, c * half : (c + 1) * half] = total * scale


def shift(value, axis, by):
    length = lax.axis_size(axis)
    return lax.ppermute(value, axis, [(i, (i + by) % length) for i in range(length)])


def shape(dims, dtype):
    return jax.ShapeDtypeStruct(dims, dtype)


def per_device(panel_vectors, force_blocks, bond_vectors, neighbours, boundary_low, boundary_high):
    rows, cols = panel_vectors.shape
    atoms = rows // 3
    half = cols // 2
    count = boundary_low.shape[0]
    extent = atoms + 2 * count
    domains = lax.axis_size("dom")
    modes = cols * lax.axis_size("blk")
    block = modes // domains
    vmem = pl.BlockSpec(memory_space=pltpu.VMEM)
    smem = pl.BlockSpec(memory_space=pltpu.SMEM)

    own, send_low, send_high, turned = pl.pallas_call(
        prep_kernel,
        out_shape=(
            shape((rows, half), BF16),
            shape((3 * count, half), BF16),
            shape((3 * count, half), BF16),
            shape((half, rows), BF16),
        ),
        in_specs=[smem, vmem, vmem, vmem],
        out_specs=(vmem,) * 4,
        compiler_params=params(),
        name="prep",
    )(
        lax.axis_index("dir").reshape(1),
        panel_vectors,
        boundary_low.reshape(1, count),
        boundary_high.reshape(1, count),
    )
    below = shift(send_high, "dom", 1)
    above = shift(send_low, "dom", -1)
    turned_all = lax.all_gather(turned, ("blk", "dir"), axis=0, tiled=True)
    bonds = lax.all_gather(bond_vectors, "dir", axis=0, tiled=True)

    hi, lo = pl.pallas_call(
        weights_kernel,
        out_shape=(shape((2 * rows, 3 * extent), BF16),) * 2,
        in_specs=[vmem] * 3,
        out_specs=(vmem,) * 2,
        scratch_shapes=[pltpu.VMEM((atoms // GROUP, 24, atoms), F32)],
        compiler_params=params(32),
        cost_estimate=pl.CostEstimate(
            flops=8 * 10**9, bytes_accessed=10**7, transcendentals=0
        ),
        name="weights",
    )(force_blocks, bonds, neighbours)

    terms = pl.pallas_call(
        couple_kernel,
        out_shape=shape((2 * domains, block, half), BF16),
        in_specs=[vmem] * 6,
        out_specs=vmem,
        scratch_shapes=[
            pltpu.VMEM((3 * extent, half), BF16),
            pltpu.VMEM((rows, 2 * half), BF16),
        ],
        compiler_params=params(32),
        name="couple",
    )(hi, lo, own, below, above, turned_all)

    terms = lax.all_to_all(terms, ("dom", "dir"), split_axis=0, concat_axis=0, tiled=True)

    scale = (3.0 * atoms * domains) ** (-0.5)
    return pl.pallas_call(
        lambda *refs: sum_kernel(scale, *refs),
        out_shape=shape((1, block, cols), F32),
        in_specs=[vmem],
        out_specs=vmem,
        compiler_params=params(),
        name="total",
    )(terms)


def solution(mesh):
    in_specs = (
        P("dom", ("panel", "blk")),
        P(None, None, "dom"),
        P("dir", None, "dom"),
        P(None, "dom"),
        P("dom"),
        P("dom"),
    )
    out_specs = P("dir", ("panel", "dom"), "blk")
    return jax.shard_map(
        per_device, mesh=mesh, in_specs=in_specs, out_specs=out_specs, check_vma=False
    )
```

```python
import jax
import jax.numpy as jnp
from jax import lax
from jax.experimental import pallas as pl
from jax.experimental.pallas import tpu as pltpu
from jax.sharding import PartitionSpec as P

GROUP = 16
BF16 = jnp.bfloat16
F32 = jnp.float32


def params(mib=24):
    return pltpu.CompilerParams(vmem_limit_bytes=mib * 1024 * 1024)


def dot(a, b, contract=((1,), (0,))):
    return lax.dot_general(a, b, (contract, ((), ())), preferred_element_type=F32)


def one_hot(mask):
    return jnp.where(mask, 1.0, 0.0).astype(BF16)


def fetch(sources, targets, sems):
    copies = [
        pltpu.make_async_copy(source, target, sems.at[i])
        for i, (source, target) in enumerate(zip(sources, targets))
    ]
    for copy in copies:
        copy.start()
    for copy in copies:
        copy.wait()


def prep_kernel(
    v_hbm, low_hbm, high_hbm, force_hbm, bond_hbm, near_hbm,
    own_ref, send_low_ref, send_high_ref, turned_ref, source_ref,
    v_ref, low_ref, high_ref, near_ref, sems,
):
    rows, half = v_ref.shape
    atoms = rows // 3
    columns = pl.ds(pl.multiple_of(lax.axis_index("dir") * half, 128), half)
    fetch(
        (v_hbm.at[:, columns], low_hbm, high_hbm, force_hbm, bond_hbm, near_hbm),
        (v_ref, low_ref, high_ref, source_ref.at[0:9], source_ref.at[9:10], near_ref),
        sems,
    )
    source_ref[10] = near_ref[...].astype(F32)
    v = v_ref[...]
    lane = lax.broadcasted_iota(jnp.int32, (atoms, rows), 1)
    atom = lax.broadcasted_iota(jnp.int32, (atoms, rows), 0)
    for b in range(3):
        picked = dot(one_hot(lane == 3 * atom + b), v)
        own_ref[b * atoms : (b + 1) * atoms, :] = picked.astype(BF16)
        turned_ref[:, b * atoms : (b + 1) * atoms] = picked.T.astype(BF16)
    for list_ref, out_ref in ((low_ref, send_low_ref), (high_ref, send_high_ref)):
        count = list_ref.shape[1]
        named = jnp.broadcast_to(list_ref[...], (128, count)).T
        lane = lax.broadcasted_iota(jnp.int32, (count, 128), 1)
        for b in range(3):
            wanted = 3 * named + b
            hot = jnp.concatenate(
                [one_hot(lane + t * 128 == wanted) for t in range(rows // 128)], axis=1
            )
            out_ref[b * count : (b + 1) * count, :] = dot(hot, v).astype(BF16)


def weights_kernel(
    source_ref, other_ref,
    own_hi_ref, own_lo_ref, hi_ref, lo_ref, table_ref,
):
    _, steps, atoms = source_ref.shape
    groups = atoms // GROUP
    halo = hi_ref.shape[1] // 3
    extent = atoms + halo
    first = lax.axis_index("dir") == 0
    mine, other = source_ref[9], other_ref[0]
    bonds = (jnp.where(first, mine, other), jnp.where(first, other, mine))
    lane = lax.broadcasted_iota(jnp.int32, (24, atoms), 1)
    rows = []
    for k in range(steps):
        force = source_ref[0:9, k, :]
        near = source_ref[10, k : k + 1, :]
        rows.append(
            jnp.concatenate(
                [force * bonds[0][k : k + 1, :], force * bonds[1][k : k + 1, :]]
                + [jnp.broadcast_to(near, (6, atoms))],
                axis=0,
            )
        )
    bit = 1
    while bit < steps:
        taken = ((lane // GROUP) & bit) != 0
        turned = list(rows)
        for p in range(steps):
            if p & bit:
                continue
            q = p | bit
            turned[p] = jnp.where(taken, pltpu.roll(rows[q], GROUP * bit, 1), rows[p])
            turned[q] = jnp.where(taken, rows[q], pltpu.roll(rows[p], atoms - GROUP * bit, 1))
        rows = turned
        bit *= 2
    for g in range(groups):
        table_ref[g] = rows[g]

    mask = (
        lax.broadcasted_iota(jnp.int32, (GROUP, atoms), 1) % GROUP
        == lax.broadcasted_iota(jnp.int32, (GROUP, atoms), 0)
    )
    target = lax.broadcasted_iota(jnp.int32, (extent, atoms), 0).astype(F32)

    def group(g, carry):
        table = table_ref[g]
        hot = one_hot(target == table[18:19, :])
        spread = jnp.concatenate(
            [jnp.where(mask, table[r : r + 1, :], 0.0) for r in range(18)], axis=0
        )
        top = spread.astype(BF16)
        rest = (spread - top.astype(F32)).astype(BF16)
        both = ((1,), (1,))
        dense = dot(top, hot, both) + dot(rest, hot, both)
        hi = dense.astype(BF16)
        lo = (dense - hi.astype(F32)).astype(BF16)
        for e in range(2):
            for a in range(3):
                at = pl.ds(pl.multiple_of((e * 3 + a) * atoms + g * GROUP, GROUP), GROUP)
                for b in range(3):
                    r = (e * 9 + 3 * a + b) * GROUP
                    near, far = slice(b * atoms, (b + 1) * atoms), slice(b * halo, (b + 1) * halo)
                    own_hi_ref[at, near] = hi[r : r + GROUP, :atoms]
                    own_lo_ref[at, near] = lo[r : r + GROUP, :atoms]
                    hi_ref[at, far] = hi[r : r + GROUP, atoms:]
                    lo_ref[at, far] = lo[r : r + GROUP, atoms:]
        return carry

    lax.fori_loop(0, groups, group, 0)


def own_kernel(hi_ref, lo_ref, own_ref, below_ref, above_ref, *refs):
    quarters = len(refs) // 2 - 1
    flux_ref, halo_ref = refs[quarters : quarters + 2]
    own = own_ref[...]
    part = own.shape[0] // 3
    for at in range(0, hi_ref.shape[0], part):
        rows = slice(at, at + part)
        flux_ref[rows, :] = dot(hi_ref[rows, :], own) + dot(lo_ref[rows, :], own)
    count = below_ref.shape[0] // 3
    for b in range(3):
        at = 2 * b * count
        halo_ref[at : at + count] = below_ref[b * count : (b + 1) * count]
        halo_ref[at + count : at + 2 * count] = above_ref[b * count : (b + 1) * count]
    for got_ref, given_ref in zip(refs[:quarters], refs[quarters + 2 :]):
        given_ref[...] = got_ref[...]


def flux_kernel(part_ref, hi_ref, lo_ref, halo_ref, flux_ref):
    half = part_ref.shape[1]
    atoms = flux_ref.shape[0] // 3
    halo = halo_ref[...]
    for e in range(2):
        for a in range(3):
            at = slice((e * 3 + a) * atoms, (e * 3 + a + 1) * atoms)
            flux = part_ref[at, :] + (dot(hi_ref[at, :], halo) + dot(lo_ref[at, :], halo))
            flux_ref[a * atoms : (a + 1) * atoms, e * half : (e + 1) * half] = flux.astype(BF16)


def couple_kernel(flux_ref, *refs):
    *quarter_refs, out_ref = refs
    half = quarter_refs[0].shape[0]
    block = out_ref.shape[1]
    tiles = len(quarter_refs) // 2
    me, core = lax.axis_index("blk"), lax.axis_index("dir")
    flux = flux_ref[...]
    for j in range(tiles):
        tile = lax.rem(me - j + tiles, tiles)
        for s in range(2):
            quarter = 2 * tile + (core if s == 0 else 1 - core)
            term = dot(quarter_refs[2 * j + s][...], flux).astype(BF16)
            for t in range(half // block):
                for e in range(2):
                    at = 2 * (quarter * (half // block) + t) + e
                    out_ref[at] = term[t * block : (t + 1) * block, e * half : (e + 1) * half]


def sum_kernel(scale, terms_ref, out_ref):
    pairs, block, half = terms_ref.shape
    for c in range(2):
        total = terms_ref[c].astype(F32)
        for d in range(1, pairs // 2):
            total = total + terms_ref[2 * d + c].astype(F32)
        out_ref[0, :, c * half : (c + 1) * half] = total * scale


def shift(value, axis, by):
    length = lax.axis_size(axis)
    return lax.ppermute(value, axis, [(i, (i + by) % length) for i in range(length)])


def shape(dims, dtype):
    return jax.ShapeDtypeStruct(dims, dtype)


def per_device(panel_vectors, force_blocks, bond_vectors, neighbours, boundary_low, boundary_high):
    rows, cols = panel_vectors.shape
    atoms = rows // 3
    half = cols // 2
    count = boundary_low.shape[0]
    domains, tiles = lax.axis_size("dom"), lax.axis_size("blk")
    block = cols * tiles // domains
    vmem = pl.BlockSpec(memory_space=pltpu.VMEM)
    hbm = pl.BlockSpec(memory_space=pltpu.HBM)

    other_bonds = shift(bond_vectors, "dir", 1)
    lists = [boundary_low.reshape(1, count), boundary_high.reshape(1, count)]
    forces = force_blocks.transpose(1, 0, 2)
    own, send_low, send_high, turned, sources = pl.pallas_call(
        prep_kernel,
        out_shape=(
            shape((rows, half), BF16),
            shape((3 * count, half), BF16),
            shape((3 * count, half), BF16),
            shape((half, rows), BF16),
            shape((11, *neighbours.shape), F32),
        ),
        in_specs=[hbm] * 6,
        out_specs=(vmem,) * 5,
        scratch_shapes=[
            pltpu.VMEM((rows, half), BF16),
            pltpu.VMEM((1, count), jnp.int32),
            pltpu.VMEM((1, count), jnp.int32),
            pltpu.VMEM(neighbours.shape, jnp.int32),
            pltpu.SemaphoreType.DMA((6,)),
        ],
        compiler_params=params(58),
        name="prep",
    )(panel_vectors, *lists, forces, bond_vectors, neighbours)
    below = shift(send_high, "dom", 1)
    above = shift(send_low, "dom", -1)
    quarters = [shift(turned, "blk", j) for j in range(1, tiles)]
    turned_other = shift(turned, "dir", 1)

    *own_weights, hi, lo = pl.pallas_call(
        weights_kernel,
        out_shape=(
            shape((2 * rows, rows), BF16),
            shape((2 * rows, rows), BF16),
            shape((2 * rows, 6 * count), BF16),
            shape((2 * rows, 6 * count), BF16),
        ),
        in_specs=[vmem] * 2,
        out_specs=(vmem,) * 4,
        scratch_shapes=[pltpu.VMEM((atoms // GROUP, 24, atoms), F32)],
        compiler_params=params(32),
        cost_estimate=pl.CostEstimate(
            flops=7 * 10**9, bytes_accessed=10**7, transcendentals=0
        ),
        name="weights",
    )(sources, other_bonds)

    partial_flux, halo, *quarters = pl.pallas_call(
        own_kernel,
        out_shape=[shape((2 * rows, half), F32), shape((6 * count, half), BF16)]
        + [shape(turned.shape, BF16)] * len(quarters),
        in_specs=[vmem] * (5 + len(quarters)),
        out_specs=[vmem] * (2 + len(quarters)),
        compiler_params=params(16),
        cost_estimate=pl.CostEstimate(
            flops=2 * 10**9, bytes_accessed=10**6, transcendentals=0
        ),
        name="own",
    )(*own_weights, own, below, above, *quarters)
    given = [turned, turned_other]
    for quarter in quarters:
        given += [quarter, shift(quarter, "dir", 1)]

    flux = pl.pallas_call(
        flux_kernel,
        out_shape=shape((rows, 2 * half), BF16),
        in_specs=[vmem] * 4,
        out_specs=vmem,
        compiler_params=params(16),
        cost_estimate=pl.CostEstimate(
            flops=2 * 10**9, bytes_accessed=10**6, transcendentals=0
        ),
        name="flux",
    )(partial_flux, hi, lo, halo)

    terms = pl.pallas_call(
        couple_kernel,
        out_shape=shape((2 * domains, block, half), BF16),
        in_specs=[vmem] * (1 + len(given)),
        out_specs=vmem,
        compiler_params=params(16),
        name="couple",
    )(flux, *given)

    terms = lax.all_to_all(terms, ("dom", "dir"), split_axis=0, concat_axis=0, tiled=True)

    scale = (3.0 * atoms * domains) ** (-0.5)
    return pl.pallas_call(
        lambda *refs: sum_kernel(scale, *refs),
        out_shape=shape((1, block, cols), F32),
        in_specs=[vmem],
        out_specs=vmem,
        compiler_params=params(),
        name="total",
    )(terms)


def solution(mesh):
    in_specs = (
        P("dom", ("panel", "blk")),
        P(None, None, "dom"),
        P("dir", None, "dom"),
        P(None, "dom"),
        P("dom"),
        P("dom"),
    )
    out_specs = P("dir", ("panel", "dom"), "blk")
    return jax.shard_map(
        per_device, mesh=mesh, in_specs=in_specs, out_specs=out_specs, check_vma=False
    )
```

```python
import jax
import jax.numpy as jnp
from jax import lax
from jax.experimental import pallas as pl
from jax.experimental.pallas import tpu as pltpu
from jax.sharding import PartitionSpec as P

GROUP = 16
BF16 = jnp.bfloat16
F32 = jnp.float32


def params(mib=24):
    return pltpu.CompilerParams(vmem_limit_bytes=mib * 1024 * 1024)


def dot(a, b, contract=((1,), (0,))):
    return lax.dot_general(a, b, (contract, ((), ())), preferred_element_type=F32)


def one_hot(mask):
    return jnp.where(mask, 1.0, 0.0).astype(BF16)


def fetch(sources, targets, sems):
    copies = [
        pltpu.make_async_copy(source, target, sems.at[i])
        for i, (source, target) in enumerate(zip(sources, targets))
    ]
    for copy in copies:
        copy.start()
    for copy in copies:
        copy.wait()


def prep_kernel(
    v_hbm, low_hbm, high_hbm, force_hbm, bond_hbm, near_hbm,
    own_ref, send_low_ref, send_high_ref, turned_ref, source_ref,
    v_ref, low_ref, high_ref, near_ref, sems,
):
    rows, half = v_ref.shape
    atoms = rows // 3
    columns = pl.ds(pl.multiple_of(lax.axis_index("dir") * half, 128), half)
    fetch(
        (v_hbm.at[:, columns], low_hbm, high_hbm, force_hbm, bond_hbm, near_hbm),
        (v_ref, low_ref, high_ref, source_ref.at[0:9], source_ref.at[9:10], near_ref),
        sems,
    )
    source_ref[10] = near_ref[...].astype(F32)
    v = v_ref[...]
    lane = lax.broadcasted_iota(jnp.int32, (atoms, rows), 1)
    atom = lax.broadcasted_iota(jnp.int32, (atoms, rows), 0)
    for b in range(3):
        picked = dot(one_hot(lane == 3 * atom + b), v)
        own_ref[b * atoms : (b + 1) * atoms, :] = picked.astype(BF16)
        turned_ref[:, b * atoms : (b + 1) * atoms] = picked.T.astype(BF16)
    for list_ref, out_ref in ((low_ref, send_low_ref), (high_ref, send_high_ref)):
        count = list_ref.shape[1]
        named = jnp.broadcast_to(list_ref[...], (128, count)).T
        lane = lax.broadcasted_iota(jnp.int32, (count, 128), 1)
        for b in range(3):
            wanted = 3 * named + b
            hot = jnp.concatenate(
                [one_hot(lane + t * 128 == wanted) for t in range(rows // 128)], axis=1
            )
            out_ref[b * count : (b + 1) * count, :] = dot(hot, v).astype(BF16)


def weights_kernel(
    source_ref, other_ref,
    own_hi_ref, own_lo_ref, hi_ref, lo_ref, table_ref,
):
    _, steps, atoms = source_ref.shape
    groups = atoms // GROUP
    halo = hi_ref.shape[1] // 3
    extent = atoms + halo
    bonds = (source_ref[9], other_ref[0])
    lane = lax.broadcasted_iota(jnp.int32, (24, atoms), 1)
    rows = []
    for k in range(steps):
        force = source_ref[0:9, k, :]
        near = source_ref[10, k : k + 1, :]
        rows.append(
            jnp.concatenate(
                [force * bonds[0][k : k + 1, :], force * bonds[1][k : k + 1, :]]
                + [jnp.broadcast_to(near, (6, atoms))],
                axis=0,
            )
        )
    bit = 1
    while bit < steps:
        taken = ((lane // GROUP) & bit) != 0
        turned = list(rows)
        for p in range(steps):
            if p & bit:
                continue
            q = p | bit
            turned[p] = jnp.where(taken, pltpu.roll(rows[q], GROUP * bit, 1), rows[p])
            turned[q] = jnp.where(taken, rows[q], pltpu.roll(rows[p], atoms - GROUP * bit, 1))
        rows = turned
        bit *= 2
    for g in range(groups):
        table_ref[g] = rows[g]

    mask = (
        lax.broadcasted_iota(jnp.int32, (GROUP, atoms), 1) % GROUP
        == lax.broadcasted_iota(jnp.int32, (GROUP, atoms), 0)
    )
    target = lax.broadcasted_iota(jnp.int32, (extent, atoms), 0).astype(F32)

    def group(g, carry):
        table = table_ref[g]
        hot = one_hot(target == table[18:19, :])
        spread = jnp.concatenate(
            [jnp.where(mask, table[r : r + 1, :], 0.0) for r in range(18)], axis=0
        )
        top = spread.astype(BF16)
        rest = (spread - top.astype(F32)).astype(BF16)
        both = ((1,), (1,))
        dense = dot(top, hot, both) + dot(rest, hot, both)
        hi = dense.astype(BF16)
        lo = (dense - hi.astype(F32)).astype(BF16)
        for e in range(2):
            for a in range(3):
                at = pl.ds(pl.multiple_of((e * 3 + a) * atoms + g * GROUP, GROUP), GROUP)
                for b in range(3):
                    r = (e * 9 + 3 * a + b) * GROUP
                    near, far = slice(b * atoms, (b + 1) * atoms), slice(b * halo, (b + 1) * halo)
                    own_hi_ref[at, near] = hi[r : r + GROUP, :atoms]
                    own_lo_ref[at, near] = lo[r : r + GROUP, :atoms]
                    hi_ref[at, far] = hi[r : r + GROUP, atoms:]
                    lo_ref[at, far] = lo[r : r + GROUP, atoms:]
        return carry

    lax.fori_loop(0, groups, group, 0)


def own_kernel(hi_ref, lo_ref, own_ref, below_ref, above_ref, *refs):
    quarters = len(refs) // 2 - 1
    flux_ref, halo_ref = refs[quarters : quarters + 2]
    own = own_ref[...]
    part = own.shape[0] // 3
    for at in range(0, hi_ref.shape[0], part):
        rows = slice(at, at + part)
        flux_ref[rows, :] = dot(hi_ref[rows, :], own) + dot(lo_ref[rows, :], own)
    count = below_ref.shape[0] // 3
    for b in range(3):
        at = 2 * b * count
        halo_ref[at : at + count] = below_ref[b * count : (b + 1) * count]
        halo_ref[at + count : at + 2 * count] = above_ref[b * count : (b + 1) * count]
    for got_ref, given_ref in zip(refs[:quarters], refs[quarters + 2 :]):
        given_ref[...] = got_ref[...]


def flux_kernel(part_ref, hi_ref, lo_ref, halo_ref, flux_ref):
    half = part_ref.shape[1]
    atoms = flux_ref.shape[0] // 3
    halo = halo_ref[...]
    for e in range(2):
        for a in range(3):
            at = slice((e * 3 + a) * atoms, (e * 3 + a + 1) * atoms)
            flux = part_ref[at, :] + (dot(hi_ref[at, :], halo) + dot(lo_ref[at, :], halo))
            flux_ref[a * atoms : (a + 1) * atoms, e * half : (e + 1) * half] = flux.astype(BF16)


def terms_of(flux_ref, quarter_refs, store, wanted=lambda tile: True):
    tiles = len(quarter_refs) // 2
    me, core = lax.axis_index("blk"), lax.axis_index("dir")
    for j in range(tiles):
        tile = lax.rem(me - j + tiles, tiles)

        @pl.when(wanted(tile))
        def _():
            for s in range(2):
                quarter = 2 * tile + (core if s == 0 else 1 - core)
                store(quarter, dot(quarter_refs[2 * j + s][...], flux_ref[...]))


def couple_kernel(flux_ref, *refs):
    *quarter_refs, out_ref = refs
    half = quarter_refs[0].shape[0]
    block = out_ref.shape[1]
    core = lax.axis_index("dir")

    def store(quarter, term):
        for t in range(half // block):
            for e in range(2):
                at = 2 * (quarter * (half // block) + t) + (core if e == 0 else 1 - core)
                out_ref[at] = term[t * block : (t + 1) * block, e * half : (e + 1) * half].astype(BF16)

    terms_of(flux_ref, quarter_refs, store)


def sum_kernel(scale, terms_ref, out_ref):
    pairs, block, half = terms_ref.shape
    for c in range(2):
        total = terms_ref[c].astype(F32)
        for d in range(1, pairs // 2):
            total = total + terms_ref[2 * d + c].astype(F32)
        out_ref[0, :, c * half : (c + 1) * half] = total * scale


def far_kernel(flux_ref, *refs):
    *quarter_refs, far_ref, add_ref = refs
    half = quarter_refs[0].shape[0]
    home = lax.axis_index("dom")

    def store(quarter, term):
        away = quarter ^ home
        for e in range(2):
            part = term[:, e * half : (e + 1) * half]

            @pl.when(away == 3)
            def _():
                far_ref[e] = part.astype(BF16)

            @pl.when(away == 2)
            def _():
                add_ref[e] = part

    terms_of(flux_ref, quarter_refs, store, lambda tile: (tile ^ (home // 2)) == 1)


def near_kernel(flux_ref, *refs):
    *quarter_refs, near_ref, keep_ref, give_ref = refs
    half = quarter_refs[0].shape[0]
    home = lax.axis_index("dom")

    def store(quarter, term):
        away = quarter ^ home

        @pl.when(away == 1)
        def _():
            near_ref[0] = term[:, :half].astype(BF16)
            near_ref[1] = term[:, half:].astype(BF16)

        @pl.when(away == 0)
        def _():
            keep_ref[...] = term[:, :half]
            give_ref[...] = term[:, half:].astype(BF16)

    terms_of(flux_ref, quarter_refs, store, lambda tile: (tile ^ (home // 2)) == 0)


def add_kernel(far_ref, add_ref, near_ref, sum0_ref, sum1_ref, near0_ref, near1_ref):
    sum0_ref[...] = (add_ref[0] + far_ref[0].astype(F32)).astype(BF16)
    sum1_ref[...] = (add_ref[1] + far_ref[1].astype(F32)).astype(BF16)
    near0_ref[...] = near_ref[0]
    near1_ref[...] = near_ref[1]


def halving_sum_kernel(scale, keep_ref, give_ref, near0_ref, near1_ref, sum0_ref, sum1_ref, out_ref):
    half = keep_ref.shape[1]
    core = lax.axis_index("dir")
    mine = pl.ds(pl.multiple_of(core * half, 128), half)
    other = pl.ds(pl.multiple_of((1 - core) * half, 128), half)
    for at, first, near, far in (
        (mine, keep_ref, near0_ref, sum0_ref),
        (other, give_ref, near1_ref, sum1_ref),
    ):
        total = first[...].astype(F32) + near[...].astype(F32) + far[...].astype(F32)
        out_ref[0, :, at] = total * scale


def shift(value, axis, by):
    length = lax.axis_size(axis)
    return lax.ppermute(value, axis, [(i, (i + by) % length) for i in range(length)])


def swap(value, away, other_core):
    domains = lax.axis_size("dom")
    pairs = [
        (2 * d + c, 2 * (d ^ away) + (c ^ other_core)) for d in range(domains) for c in range(2)
    ]
    return lax.ppermute(value, ("dom", "dir"), pairs)


def shape(dims, dtype):
    return jax.ShapeDtypeStruct(dims, dtype)


def per_device(panel_vectors, force_blocks, bond_vectors, neighbours, boundary_low, boundary_high):
    rows, cols = panel_vectors.shape
    atoms = rows // 3
    half = cols // 2
    count = boundary_low.shape[0]
    domains, tiles = lax.axis_size("dom"), lax.axis_size("blk")
    block = cols * tiles // domains
    vmem = pl.BlockSpec(memory_space=pltpu.VMEM)
    hbm = pl.BlockSpec(memory_space=pltpu.HBM)

    other_bonds = shift(bond_vectors, "dir", 1)
    lists = [boundary_low.reshape(1, count), boundary_high.reshape(1, count)]
    forces = force_blocks.transpose(1, 0, 2)
    own, send_low, send_high, turned, sources = pl.pallas_call(
        prep_kernel,
        out_shape=(
            shape((rows, half), BF16),
            shape((3 * count, half), BF16),
            shape((3 * count, half), BF16),
            shape((half, rows), BF16),
            shape((11, *neighbours.shape), F32),
        ),
        in_specs=[hbm] * 6,
        out_specs=(vmem,) * 5,
        scratch_shapes=[
            pltpu.VMEM((rows, half), BF16),
            pltpu.VMEM((1, count), jnp.int32),
            pltpu.VMEM((1, count), jnp.int32),
            pltpu.VMEM(neighbours.shape, jnp.int32),
            pltpu.SemaphoreType.DMA((6,)),
        ],
        compiler_params=params(58),
        name="prep",
    )(panel_vectors, *lists, forces, bond_vectors, neighbours)
    below = shift(send_high, "dom", 1)
    above = shift(send_low, "dom", -1)
    quarters = [shift(turned, "blk", j) for j in range(1, tiles)]
    turned_other = shift(turned, "dir", 1)

    *own_weights, hi, lo = pl.pallas_call(
        weights_kernel,
        out_shape=(
            shape((2 * rows, rows), BF16),
            shape((2 * rows, rows), BF16),
            shape((2 * rows, 6 * count), BF16),
            shape((2 * rows, 6 * count), BF16),
        ),
        in_specs=[vmem] * 2,
        out_specs=(vmem,) * 4,
        scratch_shapes=[pltpu.VMEM((atoms // GROUP, 24, atoms), F32)],
        compiler_params=params(32),
        cost_estimate=pl.CostEstimate(
            flops=7 * 10**9, bytes_accessed=10**7, transcendentals=0
        ),
        name="weights",
    )(sources, other_bonds)

    partial_flux, halo, *quarters = pl.pallas_call(
        own_kernel,
        out_shape=[shape((2 * rows, half), F32), shape((6 * count, half), BF16)]
        + [shape(turned.shape, BF16)] * len(quarters),
        in_specs=[vmem] * (5 + len(quarters)),
        out_specs=[vmem] * (2 + len(quarters)),
        compiler_params=params(16),
        cost_estimate=pl.CostEstimate(
            flops=2 * 10**9, bytes_accessed=10**6, transcendentals=0
        ),
        name="own",
    )(*own_weights, own, below, above, *quarters)
    given = [turned, turned_other]
    for quarter in quarters:
        given += [quarter, shift(quarter, "dir", 1)]

    flux = pl.pallas_call(
        flux_kernel,
        out_shape=shape((rows, 2 * half), BF16),
        in_specs=[vmem] * 4,
        out_specs=vmem,
        compiler_params=params(16),
        cost_estimate=pl.CostEstimate(
            flops=2 * 10**9, bytes_accessed=10**6, transcendentals=0
        ),
        name="flux",
    )(partial_flux, hi, lo, halo)

    scale = (3.0 * atoms * domains) ** (-0.5)
    result = shape((1, block, cols), F32)
    if domains == 4 and block == half:
        sent, kept = shape((block, half), BF16), shape((block, half), F32)
        pair = shape((2, block, half), BF16)
        cost = pl.CostEstimate(flops=8 * 10**8, bytes_accessed=10**6, transcendentals=0)
        far, add = pl.pallas_call(
            far_kernel,
            out_shape=(pair, shape((2, block, half), F32)),
            in_specs=[vmem] * (1 + len(given)),
            out_specs=(vmem,) * 2,
            compiler_params=params(16),
            cost_estimate=cost,
            name="far",
        )(flux, *given)
        far = swap(far, 1, 0)
        near, keep, give = pl.pallas_call(
            near_kernel,
            out_shape=(pair, kept, sent),
            in_specs=[vmem] * (1 + len(given)),
            out_specs=(vmem,) * 3,
            compiler_params=params(16),
            cost_estimate=cost,
            name="near",
        )(flux, *given)
        give = swap(give, 0, 1)
        sum0, sum1, near0, near1 = pl.pallas_call(
            add_kernel,
            out_shape=(sent,) * 4,
            in_specs=[vmem] * 3,
            out_specs=(vmem,) * 4,
            compiler_params=params(16),
            name="add",
        )(far, add, near)
        sum0, sum1 = swap(sum0, 2, 0), swap(sum1, 2, 1)
        near0, near1 = swap(near0, 1, 0), swap(near1, 1, 1)
        return pl.pallas_call(
            lambda *refs: halving_sum_kernel(scale, *refs),
            out_shape=result,
            in_specs=[vmem] * 6,
            out_specs=vmem,
            compiler_params=params(16),
            name="total",
        )(keep, give, near0, near1, sum0, sum1)

    terms = pl.pallas_call(
        couple_kernel,
        out_shape=shape((2 * domains, block, half), BF16),
        in_specs=[vmem] * (1 + len(given)),
        out_specs=vmem,
        compiler_params=params(16),
        name="couple",
    )(flux, *given)
    terms = lax.all_to_all(terms, ("dom", "dir"), split_axis=0, concat_axis=0, tiled=True)
    return pl.pallas_call(
        lambda *refs: sum_kernel(scale, *refs),
        out_shape=result,
        in_specs=[vmem],
        out_specs=vmem,
        compiler_params=params(),
        name="total",
    )(terms)


def solution(mesh):
    in_specs = (
        P("dom", ("panel", "blk")),
        P(None, None, "dom"),
        P("dir", None, "dom"),
        P(None, "dom"),
        P("dom"),
        P("dom"),
    )
    out_specs = P("dir", ("panel", "dom"), "blk")
    return jax.shard_map(
        per_device, mesh=mesh, in_specs=in_specs, out_specs=out_specs, check_vma=False
    )
```

```python
import jax
import jax.numpy as jnp
from jax import lax
from jax.experimental import pallas as pl
from jax.experimental.pallas import tpu as pltpu
from jax.sharding import PartitionSpec as P

GROUP = 16
BF16 = jnp.bfloat16
F32 = jnp.float32


def params(mib=24):
    return pltpu.CompilerParams(vmem_limit_bytes=mib * 1024 * 1024)


def dot(a, b, contract=((1,), (0,))):
    return lax.dot_general(a, b, (contract, ((), ())), preferred_element_type=F32)


def one_hot(mask):
    return jnp.where(mask, 1.0, 0.0).astype(BF16)


def fetch(sources, targets, sems):
    copies = [
        pltpu.make_async_copy(source, target, sems.at[i])
        for i, (source, target) in enumerate(zip(sources, targets))
    ]
    for copy in copies:
        copy.start()
    for copy in copies:
        copy.wait()


def my_columns(half):
    return pl.ds(pl.multiple_of(lax.axis_index("dir") * half, 128), half)


def boundary_kernel(
    v_hbm, low_hbm, high_hbm, send_low_ref, send_high_ref, v_ref, low_ref, high_ref, sems
):
    rows, half = v_ref.shape
    fetch((v_hbm.at[:, my_columns(half)], low_hbm, high_hbm), (v_ref, low_ref, high_ref), sems)
    v = v_ref[...]
    for list_ref, out_ref in ((low_ref, send_low_ref), (high_ref, send_high_ref)):
        count = list_ref.shape[1]
        named = jnp.broadcast_to(list_ref[...], (128, count)).T
        lane = lax.broadcasted_iota(jnp.int32, (count, 128), 1)
        for b in range(3):
            wanted = 3 * named + b
            hot = jnp.concatenate(
                [one_hot(lane + t * 128 == wanted) for t in range(rows // 128)], axis=1
            )
            out_ref[b * count : (b + 1) * count, :] = dot(hot, v).astype(BF16)


def prep_kernel(
    v_hbm, force_hbm, bond_hbm, near_hbm, sent0_hbm, sent1_hbm,
    own_ref, turned_ref, source_ref, v_ref, near_ref, sems,
):
    rows, half = v_ref.shape
    atoms = rows // 3
    fetch(
        (v_hbm.at[:, my_columns(half)], force_hbm, bond_hbm, near_hbm),
        (v_ref, source_ref.at[0:9], source_ref.at[9:10], near_ref),
        sems,
    )
    source_ref[10] = near_ref[...].astype(F32)
    v = v_ref[...]
    lane = lax.broadcasted_iota(jnp.int32, (atoms, rows), 1)
    atom = lax.broadcasted_iota(jnp.int32, (atoms, rows), 0)
    for b in range(3):
        picked = dot(one_hot(lane == 3 * atom + b), v)
        own_ref[b * atoms : (b + 1) * atoms, :] = picked.astype(BF16)
        turned_ref[:, b * atoms : (b + 1) * atoms] = picked.T.astype(BF16)


def weights_kernel(
    source_ref, other_ref, own_ref,
    flux_ref, hi_ref, lo_ref, table_ref, own_hi_ref, own_lo_ref,
):
    _, steps, atoms = source_ref.shape
    groups = atoms // GROUP
    halo = hi_ref.shape[1] // 3
    extent = atoms + halo
    bonds = (source_ref[9], other_ref[0])
    lane = lax.broadcasted_iota(jnp.int32, (24, atoms), 1)
    rows = []
    for k in range(steps):
        force = source_ref[0:9, k, :]
        near = source_ref[10, k : k + 1, :]
        rows.append(
            jnp.concatenate(
                [force * bonds[0][k : k + 1, :], force * bonds[1][k : k + 1, :]]
                + [jnp.broadcast_to(near, (6, atoms))],
                axis=0,
            )
        )
    bit = 1
    while bit < steps:
        taken = ((lane // GROUP) & bit) != 0
        turned = list(rows)
        for p in range(steps):
            if p & bit:
                continue
            q = p | bit
            turned[p] = jnp.where(taken, pltpu.roll(rows[q], GROUP * bit, 1), rows[p])
            turned[q] = jnp.where(taken, rows[q], pltpu.roll(rows[p], atoms - GROUP * bit, 1))
        rows = turned
        bit *= 2
    for g in range(groups):
        table_ref[g] = rows[g]

    mask = (
        lax.broadcasted_iota(jnp.int32, (GROUP, atoms), 1) % GROUP
        == lax.broadcasted_iota(jnp.int32, (GROUP, atoms), 0)
    )
    target = lax.broadcasted_iota(jnp.int32, (256, atoms), 0).astype(F32).astype(BF16)

    def group(g):
        table = table_ref[g]
        named = [(table[18:19, :] - at).astype(BF16) for at in range(0, extent, 256)]
        hot = jnp.concatenate(
            [jnp.where(target == name, BF16(1), BF16(0)) for name in named], axis=0
        )
        spread = jnp.concatenate(
            [jnp.where(mask, table[r : r + 1, :], 0.0) for r in range(18)], axis=0
        )
        top = spread.astype(BF16)
        rest = (spread - top.astype(F32)).astype(BF16)
        both = ((1,), (1,))
        dense = dot(top, hot, both) + dot(rest, hot, both)
        hi = dense.astype(BF16)
        lo = (dense - hi.astype(F32)).astype(BF16)
        for e in range(2):
            for a in range(3):
                at = pl.ds(pl.multiple_of((e * 3 + a) * atoms + g * GROUP, GROUP), GROUP)
                for b in range(3):
                    r = (e * 9 + 3 * a + b) * GROUP
                    near, far = slice(b * atoms, (b + 1) * atoms), slice(b * halo, (b + 1) * halo)
                    own_hi_ref[at, near] = hi[r : r + GROUP, :atoms]
                    own_lo_ref[at, near] = lo[r : r + GROUP, :atoms]
                    hi_ref[at, far] = hi[r : r + GROUP, atoms:]
                    lo_ref[at, far] = lo[r : r + GROUP, atoms:]

    def several(step, carry):
        for g in range(4):
            group(4 * step + g)
        return carry

    lax.fori_loop(0, groups // 4, several, 0)
    own = own_ref[...]
    for part in range(6):
        at = slice(part * atoms, (part + 1) * atoms)
        flux_ref[at, :] = dot(own_hi_ref[at, :], own) + dot(own_lo_ref[at, :], own)


def relay_kernel(below_ref, above_ref, part_hbm, *refs):
    quarters = len(refs) // 2
    halo_ref = refs[quarters]
    count = below_ref.shape[0] // 3
    for b in range(3):
        at = 2 * b * count
        halo_ref[at : at + count] = below_ref[b * count : (b + 1) * count]
        halo_ref[at + count : at + 2 * count] = above_ref[b * count : (b + 1) * count]
    for got_ref, given_ref in zip(refs[:quarters], refs[quarters + 1 :]):
        given_ref[...] = got_ref[...]


def flux_kernel(part_ref, hi_ref, lo_ref, halo_ref, flux_ref):
    half = part_ref.shape[1]
    atoms = flux_ref.shape[0] // 3
    halo = halo_ref[...]
    for e in range(2):
        for a in range(3):
            at = slice((e * 3 + a) * atoms, (e * 3 + a + 1) * atoms)
            flux = part_ref[at, :] + (dot(hi_ref[at, :], halo) + dot(lo_ref[at, :], halo))
            flux_ref[a * atoms : (a + 1) * atoms, e * half : (e + 1) * half] = flux.astype(BF16)


def terms_of(flux_ref, quarter_refs, store, wanted=lambda tile: True):
    tiles = len(quarter_refs) // 2
    me, core = lax.axis_index("blk"), lax.axis_index("dir")
    for j in range(tiles):
        tile = lax.rem(me - j + tiles, tiles)

        @pl.when(wanted(tile))
        def _():
            for s in range(2):
                quarter = 2 * tile + (core if s == 0 else 1 - core)
                store(quarter, dot(quarter_refs[2 * j + s][...], flux_ref[...]))


def couple_kernel(flux_ref, *refs):
    *quarter_refs, out_ref = refs
    half = quarter_refs[0].shape[0]
    block = out_ref.shape[1]
    core = lax.axis_index("dir")

    def store(quarter, term):
        for t in range(half // block):
            for e in range(2):
                at = 2 * (quarter * (half // block) + t) + (core if e == 0 else 1 - core)
                out_ref[at] = term[t * block : (t + 1) * block, e * half : (e + 1) * half].astype(BF16)

    terms_of(flux_ref, quarter_refs, store)


def sum_kernel(scale, terms_ref, out_ref):
    pairs, block, half = terms_ref.shape
    for c in range(2):
        total = terms_ref[c].astype(F32)
        for d in range(1, pairs // 2):
            total = total + terms_ref[2 * d + c].astype(F32)
        out_ref[0, :, c * half : (c + 1) * half] = total * scale


def far_kernel(flux_ref, *refs):
    *quarter_refs, far_ref, add_ref = refs
    half = quarter_refs[0].shape[0]
    home = lax.axis_index("dom")

    def store(quarter, term):
        away = quarter ^ home
        for e in range(2):
            part = term[:, e * half : (e + 1) * half]

            @pl.when(away == 3)
            def _():
                far_ref[e] = part.astype(BF16)

            @pl.when(away == 2)
            def _():
                add_ref[e] = part

    terms_of(flux_ref, quarter_refs, store, lambda tile: (tile ^ (home // 2)) == 1)


def near_kernel(flux_ref, *refs):
    *quarter_refs, near_ref, keep_ref, give_ref = refs
    half = quarter_refs[0].shape[0]
    home = lax.axis_index("dom")

    def store(quarter, term):
        away = quarter ^ home

        @pl.when(away == 1)
        def _():
            near_ref[0] = term[:, :half].astype(BF16)
            near_ref[1] = term[:, half:].astype(BF16)

        @pl.when(away == 0)
        def _():
            keep_ref[...] = term[:, :half]
            give_ref[...] = term[:, half:].astype(BF16)

    terms_of(flux_ref, quarter_refs, store, lambda tile: (tile ^ (home // 2)) == 0)


def add_kernel(far_ref, add_ref, near_ref, sum0_ref, sum1_ref, near0_ref, near1_ref):
    sum0_ref[...] = (add_ref[0] + far_ref[0].astype(F32)).astype(BF16)
    sum1_ref[...] = (add_ref[1] + far_ref[1].astype(F32)).astype(BF16)
    near0_ref[...] = near_ref[0]
    near1_ref[...] = near_ref[1]


def halving_sum_kernel(scale, keep_ref, give_ref, near0_ref, near1_ref, sum0_ref, sum1_ref, out_ref):
    half = keep_ref.shape[1]
    core = lax.axis_index("dir")
    mine = pl.ds(pl.multiple_of(core * half, 128), half)
    other = pl.ds(pl.multiple_of((1 - core) * half, 128), half)
    for at, first, near, far in (
        (mine, keep_ref, near0_ref, sum0_ref),
        (other, give_ref, near1_ref, sum1_ref),
    ):
        total = first[...].astype(F32) + near[...].astype(F32) + far[...].astype(F32)
        out_ref[0, :, at] = total * scale


def shift(value, axis, by):
    length = lax.axis_size(axis)
    return lax.ppermute(value, axis, [(i, (i + by) % length) for i in range(length)])


def swap(value, away, other_core):
    domains = lax.axis_size("dom")
    pairs = [
        (2 * d + c, 2 * (d ^ away) + (c ^ other_core)) for d in range(domains) for c in range(2)
    ]
    return lax.ppermute(value, ("dom", "dir"), pairs)


def shape(dims, dtype):
    return jax.ShapeDtypeStruct(dims, dtype)


def per_device(panel_vectors, force_blocks, bond_vectors, neighbours, boundary_low, boundary_high):
    rows, cols = panel_vectors.shape
    atoms = rows // 3
    half = cols // 2
    count = boundary_low.shape[0]
    domains, tiles = lax.axis_size("dom"), lax.axis_size("blk")
    block = cols * tiles // domains
    vmem = pl.BlockSpec(memory_space=pltpu.VMEM)
    hbm = pl.BlockSpec(memory_space=pltpu.HBM)

    lists = [boundary_low.reshape(1, count), boundary_high.reshape(1, count)]
    send_low, send_high = pl.pallas_call(
        boundary_kernel,
        out_shape=(shape((3 * count, half), BF16),) * 2,
        in_specs=[hbm] * 3,
        out_specs=(vmem,) * 2,
        scratch_shapes=[
            pltpu.VMEM((rows, half), BF16),
            pltpu.VMEM((1, count), jnp.int32),
            pltpu.VMEM((1, count), jnp.int32),
            pltpu.SemaphoreType.DMA((3,)),
        ],
        compiler_params=params(58),
        name="boundary",
    )(panel_vectors, *lists)
    below = shift(send_high, "dom", 1)
    above = shift(send_low, "dom", -1)

    other_bonds = shift(bond_vectors, "dir", 1)
    forces = force_blocks.transpose(1, 0, 2)
    own, turned, sources = pl.pallas_call(
        prep_kernel,
        out_shape=(
            shape((rows, half), BF16),
            shape((half, rows), BF16),
            shape((11, *neighbours.shape), F32),
        ),
        in_specs=[hbm] * 6,
        out_specs=(vmem,) * 3,
        scratch_shapes=[
            pltpu.VMEM((rows, half), BF16),
            pltpu.VMEM(neighbours.shape, jnp.int32),
            pltpu.SemaphoreType.DMA((4,)),
        ],
        compiler_params=params(58),
        cost_estimate=pl.CostEstimate(
            flops=10**9, bytes_accessed=10**6, transcendentals=0
        ),
        name="prep",
    )(panel_vectors, forces, bond_vectors, neighbours, send_high, send_low)
    quarters = [shift(turned, "blk", j) for j in range(1, tiles)]
    turned_other = shift(turned, "dir", 1)

    partial_flux, hi, lo = pl.pallas_call(
        weights_kernel,
        out_shape=(
            shape((2 * rows, half), F32),
            shape((2 * rows, 6 * count), BF16),
            shape((2 * rows, 6 * count), BF16),
        ),
        in_specs=[vmem] * 3,
        out_specs=(vmem,) * 3,
        scratch_shapes=[
            pltpu.VMEM((atoms // GROUP, 24, atoms), F32),
            pltpu.VMEM((2 * rows, rows), BF16),
            pltpu.VMEM((2 * rows, rows), BF16),
        ],
        compiler_params=params(32),
        cost_estimate=pl.CostEstimate(
            flops=8*10**9, bytes_accessed=10**7, transcendentals=0
        ),
        name="weights",
    )(sources, other_bonds, own)

    halo, *quarters = pl.pallas_call(
        relay_kernel,
        out_shape=[shape((6 * count, half), BF16)] + [shape(turned.shape, BF16)] * (tiles - 1),
        in_specs=[vmem, vmem, pl.BlockSpec(memory_space=pl.ANY)] + [vmem] * len(quarters),
        out_specs=[vmem] * tiles,
        compiler_params=params(16),
        name="relay",
    )(below, above, partial_flux, *quarters)
    given = [turned, turned_other]
    for quarter in quarters:
        given += [quarter, shift(quarter, "dir", 1)]

    flux = pl.pallas_call(
        flux_kernel,
        out_shape=shape((rows, 2 * half), BF16),
        in_specs=[vmem] * 4,
        out_specs=vmem,
        compiler_params=params(16),
        cost_estimate=pl.CostEstimate(
            flops=2 * 10**9, bytes_accessed=10**6, transcendentals=0
        ),
        name="flux",
    )(partial_flux, hi, lo, halo)

    scale = (3.0 * atoms * domains) ** (-0.5)
    result = shape((1, block, cols), F32)
    if domains == 4 and block == half:
        sent, kept = shape((block, half), BF16), shape((block, half), F32)
        pair = shape((2, block, half), BF16)
        cost = pl.CostEstimate(flops=8 * 10**8, bytes_accessed=10**6, transcendentals=0)
        far, add = pl.pallas_call(
            far_kernel,
            out_shape=(pair, shape((2, block, half), F32)),
            in_specs=[vmem] * (1 + len(given)),
            out_specs=(vmem,) * 2,
            compiler_params=params(16),
            cost_estimate=cost,
            name="far",
        )(flux, *given)
        far = swap(far, 1, 0)
        near, keep, give = pl.pallas_call(
            near_kernel,
            out_shape=(pair, kept, sent),
            in_specs=[vmem] * (1 + len(given)),
            out_specs=(vmem,) * 3,
            compiler_params=params(16),
            cost_estimate=cost,
            name="near",
        )(flux, *given)
        give = swap(give, 0, 1)
        sum0, sum1, near0, near1 = pl.pallas_call(
            add_kernel,
            out_shape=(sent,) * 4,
            in_specs=[vmem] * 3,
            out_specs=(vmem,) * 4,
            compiler_params=params(16),
            name="add",
        )(far, add, near)
        sum0, sum1 = swap(sum0, 2, 0), swap(sum1, 2, 1)
        near0, near1 = swap(near0, 1, 0), swap(near1, 1, 1)
        return pl.pallas_call(
            lambda *refs: halving_sum_kernel(scale, *refs),
            out_shape=result,
            in_specs=[vmem] * 6,
            out_specs=vmem,
            compiler_params=params(16),
            name="total",
        )(keep, give, near0, near1, sum0, sum1)

    terms = pl.pallas_call(
        couple_kernel,
        out_shape=shape((2 * domains, block, half), BF16),
        in_specs=[vmem] * (1 + len(given)),
        out_specs=vmem,
        compiler_params=params(16),
        name="couple",
    )(flux, *given)
    terms = lax.all_to_all(terms, ("dom", "dir"), split_axis=0, concat_axis=0, tiled=True)
    return pl.pallas_call(
        lambda *refs: sum_kernel(scale, *refs),
        out_shape=result,
        in_specs=[vmem],
        out_specs=vmem,
        compiler_params=params(),
        name="total",
    )(terms)


def solution(mesh):
    in_specs = (
        P("dom", ("panel", "blk")),
        P(None, None, "dom"),
        P("dir", None, "dom"),
        P(None, "dom"),
        P("dom"),
        P("dom"),
    )
    out_specs = P("dir", ("panel", "dom"), "blk")
    return jax.shard_map(
        per_device, mesh=mesh, in_specs=in_specs, out_specs=out_specs, check_vma=False
    )
```

```python
import functools

import jax
import jax.numpy as jnp
from jax import lax
from jax.experimental import pallas as pl
from jax.experimental.pallas import tpu as pltpu
from jax.sharding import PartitionSpec as P

GROUP = 16
BF16 = jnp.bfloat16
F32 = jnp.float32


def params(mib=24):
    return pltpu.CompilerParams(vmem_limit_bytes=mib * 1024 * 1024)


def dot(a, b, contract=((1,), (0,))):
    return lax.dot_general(a, b, (contract, ((), ())), preferred_element_type=F32)


def one_hot(mask):
    return jnp.where(mask, 1.0, 0.0).astype(BF16)


def my_columns(half):
    return pl.ds(pl.multiple_of(lax.axis_index("dir") * half, 128), half)


def prep_kernel(
    v_hbm, low_hbm, high_hbm, force_hbm, bond_hbm, near_hbm,
    turned_hbm, send_low_hbm, send_high_hbm, own_hbm, source_hbm,
    v_ref, low_ref, high_ref, near_ref, turned_ref, send_low_ref, send_high_ref, own_ref,
    name_ref, in_sems, out_sems,
):
    rows, half = v_ref.shape
    atoms = rows // 3
    v_in = pltpu.make_async_copy(v_hbm.at[:, my_columns(half)], v_ref, in_sems.at[0])
    v_in.start()
    lists_in = [
        pltpu.make_async_copy(low_hbm, low_ref, in_sems.at[1]),
        pltpu.make_async_copy(high_hbm, high_ref, in_sems.at[2]),
        pltpu.make_async_copy(near_hbm, near_ref, in_sems.at[3]),
    ]
    for copy in lists_in:
        copy.start()
    out = [
        pltpu.make_async_copy(force_hbm, source_hbm.at[0:9], out_sems.at[0]),
        pltpu.make_async_copy(bond_hbm, source_hbm.at[9:10], out_sems.at[1]),
    ]
    for copy in out:
        copy.start()

    def leave(ref, hbm):
        copy = pltpu.make_async_copy(ref, hbm, out_sems.at[len(out)])
        copy.start()
        out.append(copy)

    lane = lax.broadcasted_iota(jnp.int32, (atoms, rows), 1)
    atom = lax.broadcasted_iota(jnp.int32, (atoms, rows), 0)
    hot = [one_hot(lane == 3 * atom + b) for b in range(3)]
    v_in.wait()
    v = v_ref[...]
    for b in range(3):
        picked = dot(hot[b], v)
        turned_ref[:, b * atoms : (b + 1) * atoms] = picked.T.astype(BF16)
        own_ref[b * atoms : (b + 1) * atoms, :] = picked.astype(BF16)
    leave(turned_ref, turned_hbm)
    for copy in lists_in:
        copy.wait()
    name_ref[0] = near_ref[...].astype(F32)
    for list_ref, send_ref, send_hbm in (
        (high_ref, send_high_ref, send_high_hbm),
        (low_ref, send_low_ref, send_low_hbm),
    ):
        count = list_ref.shape[1]
        named = jnp.broadcast_to(list_ref[...], (128, count)).T
        lane = lax.broadcasted_iota(jnp.int32, (count, 128), 1)
        for b in range(3):
            wanted = 3 * named + b
            picks = jnp.concatenate(
                [one_hot(lane + t * 128 == wanted) for t in range(rows // 128)], axis=1
            )
            send_ref[b * count : (b + 1) * count, :] = dot(picks, v).astype(BF16)
        leave(send_ref, send_hbm)
    leave(own_ref, own_hbm)
    leave(name_ref, source_hbm.at[10:11])
    for copy in out:
        copy.wait()


def weights_kernel(
    source_ref, other_ref, own_ref,
    flux_ref, hi_ref, lo_ref, table_ref, own_hi_ref, own_lo_ref,
):
    _, steps, atoms = source_ref.shape
    groups = atoms // GROUP
    halo = hi_ref.shape[1] // 3
    extent = atoms + halo
    bonds = (source_ref[9], other_ref[0])
    lane = lax.broadcasted_iota(jnp.int32, (24, atoms), 1)
    rows = []
    for k in range(steps):
        force = source_ref[0:9, k, :]
        near = source_ref[10, k : k + 1, :]
        rows.append(
            jnp.concatenate(
                [force * bonds[0][k : k + 1, :], force * bonds[1][k : k + 1, :]]
                + [jnp.broadcast_to(near, (6, atoms))],
                axis=0,
            )
        )
    bit = 1
    while bit < steps:
        taken = ((lane // GROUP) & bit) != 0
        turned = list(rows)
        for p in range(steps):
            if p & bit:
                continue
            q = p | bit
            turned[p] = jnp.where(taken, pltpu.roll(rows[q], GROUP * bit, 1), rows[p])
            turned[q] = jnp.where(taken, rows[q], pltpu.roll(rows[p], atoms - GROUP * bit, 1))
        rows = turned
        bit *= 2
    for g in range(groups):
        table_ref[g] = rows[g]

    mask = (
        lax.broadcasted_iota(jnp.int32, (GROUP, atoms), 1) % GROUP
        == lax.broadcasted_iota(jnp.int32, (GROUP, atoms), 0)
    )
    target = lax.broadcasted_iota(jnp.int32, (256, atoms), 0).astype(F32).astype(BF16)

    def group(g):
        table = table_ref[g]
        named = [(table[18:19, :] - at).astype(BF16) for at in range(0, extent, 256)]
        hot = jnp.concatenate(
            [jnp.where(target == name, BF16(1), BF16(0)) for name in named], axis=0
        )
        spread = jnp.concatenate(
            [jnp.where(mask, table[r : r + 1, :], 0.0) for r in range(18)], axis=0
        )
        top = spread.astype(BF16)
        rest = (spread - top.astype(F32)).astype(BF16)
        both = ((1,), (1,))
        dense = dot(top, hot, both) + dot(rest, hot, both)
        hi = dense.astype(BF16)
        lo = (dense - hi.astype(F32)).astype(BF16)
        for e in range(2):
            for a in range(3):
                at = pl.ds(pl.multiple_of((e * 3 + a) * atoms + g * GROUP, GROUP), GROUP)
                for b in range(3):
                    r = (e * 9 + 3 * a + b) * GROUP
                    near, far = slice(b * atoms, (b + 1) * atoms), slice(b * halo, (b + 1) * halo)
                    own_hi_ref[at, near] = hi[r : r + GROUP, :atoms]
                    own_lo_ref[at, near] = lo[r : r + GROUP, :atoms]
                    hi_ref[at, far] = hi[r : r + GROUP, atoms:]
                    lo_ref[at, far] = lo[r : r + GROUP, atoms:]

    def several(step, carry):
        for g in range(4):
            group(4 * step + g)
        return carry

    lax.fori_loop(0, groups // 4, several, 0)
    own = own_ref[...]
    for part in range(6):
        at = slice(part * atoms, (part + 1) * atoms)
        flux_ref[at, :] = dot(own_hi_ref[at, :], own) + dot(own_lo_ref[at, :], own)


def relay_kernel(part_hbm, below_hbm, above_hbm, *refs):
    for got_ref, given_ref in zip(refs[: len(refs) // 2], refs[len(refs) // 2 :]):
        given_ref[...] = got_ref[...]


def flux_kernel(e, part_ref, hi_ref, lo_ref, below_ref, above_ref, flux_ref, halo_ref):
    count = below_ref.shape[0] // 3
    for b in range(3):
        at = 2 * b * count
        halo_ref[at : at + count] = below_ref[b * count : (b + 1) * count]
        halo_ref[at + count : at + 2 * count] = above_ref[b * count : (b + 1) * count]
    atoms = flux_ref.shape[0] // 3
    halo = halo_ref[...]
    for a in range(3):
        at = slice((e * 3 + a) * atoms, (e * 3 + a + 1) * atoms)
        flux = part_ref[at, :] + (dot(hi_ref[at, :], halo) + dot(lo_ref[at, :], halo))
        flux_ref[a * atoms : (a + 1) * atoms, :] = flux.astype(BF16)


def terms_of(quarter_refs, store, wanted=lambda tile: True):
    tiles = len(quarter_refs) // 2
    me, core = lax.axis_index("blk"), lax.axis_index("dir")
    for j in range(tiles):
        tile = lax.rem(me - j + tiles, tiles)

        @pl.when(wanted(tile))
        def _():
            for s in range(2):
                store(2 * tile + (core if s == 0 else 1 - core), quarter_refs[2 * j + s])


def couple_kernel(flux0_ref, flux1_ref, *refs):
    *quarter_refs, out_ref = refs
    half = quarter_refs[0].shape[0]
    block = out_ref.shape[1]
    core = lax.axis_index("dir")

    def store(quarter, turned_ref):
        for e, flux_ref in enumerate((flux0_ref, flux1_ref)):
            term = dot(turned_ref[...], flux_ref[...]).astype(BF16)
            for t in range(half // block):
                at = 2 * (quarter * (half // block) + t) + (core if e == 0 else 1 - core)
                out_ref[at] = term[t * block : (t + 1) * block]

    terms_of(quarter_refs, store)


def sum_kernel(scale, terms_ref, out_ref):
    pairs, block, half = terms_ref.shape
    for c in range(2):
        total = terms_ref[c].astype(F32)
        for d in range(1, pairs // 2):
            total = total + terms_ref[2 * d + c].astype(F32)
        out_ref[0, :, c * half : (c + 1) * half] = total * scale


def far_kernel(flux_ref, *refs):
    *quarter_refs, far_ref, add_ref = refs
    home = lax.axis_index("dom")

    def store(quarter, turned_ref):
        term = dot(turned_ref[...], flux_ref[...])

        @pl.when((quarter ^ home) == 3)
        def _():
            far_ref[...] = term.astype(BF16)

        @pl.when((quarter ^ home) == 2)
        def _():
            add_ref[...] = term

    terms_of(quarter_refs, store, lambda tile: (tile ^ (home // 2)) == 1)


def near_kernel(flux0_ref, flux1_ref, *refs):
    *quarter_refs, near0_ref, near1_ref, keep_ref, give_ref = refs
    home = lax.axis_index("dom")

    def store(quarter, turned_ref):
        terms = [dot(turned_ref[...], ref[...]) for ref in (flux0_ref, flux1_ref)]

        @pl.when((quarter ^ home) == 1)
        def _():
            near0_ref[...] = terms[0].astype(BF16)
            near1_ref[...] = terms[1].astype(BF16)

        @pl.when((quarter ^ home) == 0)
        def _():
            keep_ref[...] = terms[0]
            give_ref[...] = terms[1].astype(BF16)

    terms_of(quarter_refs, store, lambda tile: (tile ^ (home // 2)) == 0)


def add_kernel(far_ref, add_ref, sum_ref):
    sum_ref[...] = (add_ref[...] + far_ref[...].astype(F32)).astype(BF16)


def halving_sum_kernel(scale, keep_ref, give_ref, near0_ref, near1_ref, sum0_ref, sum1_ref, out_ref):
    half = keep_ref.shape[1]
    core = lax.axis_index("dir")
    mine = pl.ds(pl.multiple_of(core * half, 128), half)
    other = pl.ds(pl.multiple_of((1 - core) * half, 128), half)
    for at, first, near, far in (
        (mine, keep_ref, near0_ref, sum0_ref),
        (other, give_ref, near1_ref, sum1_ref),
    ):
        total = first[...].astype(F32) + near[...].astype(F32) + far[...].astype(F32)
        out_ref[0, :, at] = total * scale


def shift(value, axis, by):
    length = lax.axis_size(axis)
    return lax.ppermute(value, axis, [(i, (i + by) % length) for i in range(length)])


def swap(value, away, other_core):
    domains = lax.axis_size("dom")
    pairs = [
        (2 * d + c, 2 * (d ^ away) + (c ^ other_core)) for d in range(domains) for c in range(2)
    ]
    return lax.ppermute(value, ("dom", "dir"), pairs)


def shape(dims, dtype):
    return jax.ShapeDtypeStruct(dims, dtype)


def per_device(panel_vectors, force_blocks, bond_vectors, neighbours, boundary_low, boundary_high):
    rows, cols = panel_vectors.shape
    atoms = rows // 3
    half = cols // 2
    count = boundary_low.shape[0]
    domains, tiles = lax.axis_size("dom"), lax.axis_size("blk")
    block = cols * tiles // domains
    vmem = pl.BlockSpec(memory_space=pltpu.VMEM)
    hbm = pl.BlockSpec(memory_space=pltpu.HBM)
    anywhere = pl.BlockSpec(memory_space=pl.ANY)

    other_bonds = shift(bond_vectors, "dir", 1)
    lists = [boundary_low.reshape(1, count), boundary_high.reshape(1, count)]
    forces = force_blocks.transpose(1, 0, 2)
    prepared = (
        shape((half, rows), BF16),
        shape((3 * count, half), BF16),
        shape((3 * count, half), BF16),
        shape((rows, half), BF16),
    )
    turned, send_low, send_high, own, sources = pl.pallas_call(
        prep_kernel,
        out_shape=(*prepared, shape((11, *neighbours.shape), F32)),
        in_specs=[hbm] * 6,
        out_specs=(hbm,) * 5,
        scratch_shapes=[
            pltpu.VMEM((rows, half), BF16),
            pltpu.VMEM((1, count), jnp.int32),
            pltpu.VMEM((1, count), jnp.int32),
            pltpu.VMEM(neighbours.shape, jnp.int32),
            *[pltpu.VMEM(like.shape, like.dtype) for like in prepared],
            pltpu.VMEM((1, *neighbours.shape), F32),
            pltpu.SemaphoreType.DMA((4,)),
            pltpu.SemaphoreType.DMA((7,)),
        ],
        compiler_params=params(58),
        name="prep",
    )(panel_vectors, *lists, forces, bond_vectors, neighbours)
    quarters = [shift(turned, "blk", j) for j in range(1, tiles)]
    turned_other = shift(turned, "dir", 1)
    below = shift(send_high, "dom", 1)
    above = shift(send_low, "dom", -1)

    partial_flux, hi, lo = pl.pallas_call(
        weights_kernel,
        out_shape=(
            shape((2 * rows, half), F32),
            shape((2 * rows, 6 * count), BF16),
            shape((2 * rows, 6 * count), BF16),
        ),
        in_specs=[vmem] * 3,
        out_specs=(vmem,) * 3,
        scratch_shapes=[
            pltpu.VMEM((atoms // GROUP, 24, atoms), F32),
            pltpu.VMEM((2 * rows, rows), BF16),
            pltpu.VMEM((2 * rows, rows), BF16),
        ],
        compiler_params=params(32),
        cost_estimate=pl.CostEstimate(
            flops=8*10**9, bytes_accessed=10**7, transcendentals=0
        ),
        name="weights",
    )(sources, other_bonds, own)

    quarters = pl.pallas_call(
        relay_kernel,
        out_shape=[shape(turned.shape, BF16)] * (tiles - 1),
        in_specs=[anywhere] * 3 + [vmem] * len(quarters),
        out_specs=[vmem] * (tiles - 1),
        compiler_params=params(16),
        name="relay",
    )(partial_flux, below, above, *quarters)
    given = [turned, turned_other]
    for quarter in quarters:
        given += [quarter, shift(quarter, "dir", 1)]

    def flux_of(e):
        return pl.pallas_call(
            functools.partial(flux_kernel, e),
            out_shape=shape((rows, half), BF16),
            in_specs=[vmem] * 5,
            out_specs=vmem,
            scratch_shapes=[pltpu.VMEM((6 * count, half), BF16)],
            compiler_params=params(16),
            cost_estimate=pl.CostEstimate(
                flops=10**9, bytes_accessed=10**6, transcendentals=0
            ),
            name="flux",
        )(partial_flux, hi, lo, below, above)

    scale = (3.0 * atoms * domains) ** (-0.5)
    result = shape((1, block, cols), F32)
    if domains == 4 and block == half:
        sent, kept = shape((block, half), BF16), shape((block, half), F32)
        cost = pl.CostEstimate(flops=4 * 10**8, bytes_accessed=10**6, transcendentals=0)

        def far_of(flux):
            far, add = pl.pallas_call(
                far_kernel,
                out_shape=(sent, kept),
                in_specs=[vmem] * (1 + len(given)),
                out_specs=(vmem,) * 2,
                compiler_params=params(16),
                cost_estimate=cost,
                name="far",
            )(flux, *given)
            return far, add

        flux0, flux1 = flux_of(0), flux_of(1)
        far0, add0 = far_of(flux0)
        far1, add1 = far_of(flux1)
        far0, far1 = swap(far0, 1, 0), swap(far1, 1, 0)
        near0, near1, keep, give = pl.pallas_call(
            near_kernel,
            out_shape=(sent, sent, kept, sent),
            in_specs=[vmem] * (2 + len(given)),
            out_specs=(vmem,) * 4,
            compiler_params=params(16),
            cost_estimate=cost,
            name="near",
        )(flux0, flux1, *given)
        give, near0, near1 = swap(give, 0, 1), swap(near0, 1, 0), swap(near1, 1, 1)

        def sum_of(far, add):
            return pl.pallas_call(
                add_kernel,
                out_shape=sent,
                in_specs=[vmem] * 2,
                out_specs=vmem,
                compiler_params=params(16),
                name="add",
            )(far, add)

        sum0, sum1 = swap(sum_of(far0, add0), 2, 0), swap(sum_of(far1, add1), 2, 1)
        return pl.pallas_call(
            lambda *refs: halving_sum_kernel(scale, *refs),
            out_shape=result,
            in_specs=[vmem] * 6,
            out_specs=vmem,
            compiler_params=params(16),
            name="total",
        )(keep, give, near0, near1, sum0, sum1)

    terms = pl.pallas_call(
        couple_kernel,
        out_shape=shape((2 * domains, block, half), BF16),
        in_specs=[vmem] * (2 + len(given)),
        out_specs=vmem,
        compiler_params=params(16),
        name="couple",
    )(flux_of(0), flux_of(1), *given)
    terms = lax.all_to_all(terms, ("dom", "dir"), split_axis=0, concat_axis=0, tiled=True)
    return pl.pallas_call(
        lambda *refs: sum_kernel(scale, *refs),
        out_shape=result,
        in_specs=[vmem],
        out_specs=vmem,
        compiler_params=params(),
        name="total",
    )(terms)


def solution(mesh):
    in_specs = (
        P("dom", ("panel", "blk")),
        P(None, None, "dom"),
        P("dir", None, "dom"),
        P(None, "dom"),
        P("dom"),
        P("dom"),
    )
    out_specs = P("dir", ("panel", "dom"), "blk")
    return jax.shard_map(
        per_device, mesh=mesh, in_specs=in_specs, out_specs=out_specs, check_vma=False
    )
```

```python
import functools

import jax
import jax.numpy as jnp
from jax import lax
from jax.experimental import pallas as pl
from jax.experimental.pallas import tpu as pltpu
from jax.sharding import PartitionSpec as P

GROUP = 16
BF16 = jnp.bfloat16
F32 = jnp.float32


def params(mib=24):
    return pltpu.CompilerParams(vmem_limit_bytes=mib * 1024 * 1024)


def dot(a, b, contract=((1,), (0,))):
    return lax.dot_general(a, b, (contract, ((), ())), preferred_element_type=F32)


def one_hot(mask):
    return jnp.where(mask, 1.0, 0.0).astype(BF16)


def my_columns(half):
    return pl.ds(pl.multiple_of(lax.axis_index("dir") * half, 128), half)


def prep_kernel(
    v_hbm, low_hbm, high_hbm, force_hbm, bond_hbm, near_hbm,
    turned_hbm, send_low_hbm, send_high_hbm, own_hbm, source_hbm, bond_out_hbm,
    v_ref, low_ref, high_ref, near_ref, turned_ref, send_low_ref, send_high_ref, own_ref,
    source_ref, in_sems, out_sems,
):
    rows, half = v_ref.shape
    atoms = rows // 3
    arriving = [
        pltpu.make_async_copy(source, target, in_sems.at[i])
        for i, (source, target) in enumerate(
            (
                (v_hbm.at[:, my_columns(half)], v_ref),
                (low_hbm, low_ref),
                (high_hbm, high_ref),
                (near_hbm, near_ref),
                (force_hbm, source_ref.at[0:9]),
                (bond_hbm, source_ref.at[9:10]),
            )
        )
    ]
    for copy in arriving:
        copy.start()
    leaving = []

    def leave(ref, hbm):
        copy = pltpu.make_async_copy(ref, hbm, out_sems.at[len(leaving)])
        copy.start()
        leaving.append(copy)

    lane = lax.broadcasted_iota(jnp.int32, (atoms, rows), 1)
    atom = lax.broadcasted_iota(jnp.int32, (atoms, rows), 0)
    hot = [one_hot(lane == 3 * atom + b) for b in range(3)]
    for copy in arriving:
        copy.wait()
    source_ref[10] = near_ref[...].astype(F32)
    leave(source_ref.at[9:10], bond_out_hbm)
    leave(source_ref, source_hbm)
    v = v_ref[...]
    for b in range(3):
        picked = dot(hot[b], v)
        turned_ref[:, b * atoms : (b + 1) * atoms] = picked.T.astype(BF16)
        own_ref[b * atoms : (b + 1) * atoms, :] = picked.astype(BF16)
    leave(turned_ref, turned_hbm)
    leave(own_ref, own_hbm)
    for list_ref, send_ref, send_hbm in (
        (high_ref, send_high_ref, send_high_hbm),
        (low_ref, send_low_ref, send_low_hbm),
    ):
        count = list_ref.shape[1]
        named = jnp.broadcast_to(list_ref[...], (128, count)).T
        lane = lax.broadcasted_iota(jnp.int32, (count, 128), 1)
        for b in range(3):
            wanted = 3 * named + b
            picks = jnp.concatenate(
                [one_hot(lane + t * 128 == wanted) for t in range(rows // 128)], axis=1
            )
            send_ref[b * count : (b + 1) * count, :] = dot(picks, v).astype(BF16)
        leave(send_ref, send_hbm)
    for copy in leaving:
        copy.wait()


def weights_kernel(
    source_ref, other_ref, own_ref,
    flux_ref, hi_ref, lo_ref, table_ref, own_hi_ref, own_lo_ref,
):
    _, steps, atoms = source_ref.shape
    groups = atoms // GROUP
    halo = hi_ref.shape[1] // 3
    extent = atoms + halo
    bonds = (source_ref[9], other_ref[0])
    lane = lax.broadcasted_iota(jnp.int32, (24, atoms), 1)
    rows = []
    for k in range(steps):
        force = source_ref[0:9, k, :]
        near = source_ref[10, k : k + 1, :]
        rows.append(
            jnp.concatenate(
                [force * bonds[0][k : k + 1, :], force * bonds[1][k : k + 1, :]]
                + [jnp.broadcast_to(near, (6, atoms))],
                axis=0,
            )
        )
    bit = 1
    while bit < steps:
        taken = ((lane // GROUP) & bit) != 0
        turned = list(rows)
        for p in range(steps):
            if p & bit:
                continue
            q = p | bit
            turned[p] = jnp.where(taken, pltpu.roll(rows[q], GROUP * bit, 1), rows[p])
            turned[q] = jnp.where(taken, rows[q], pltpu.roll(rows[p], atoms - GROUP * bit, 1))
        rows = turned
        bit *= 2
    for g in range(groups):
        table_ref[g] = rows[g]

    mask = (
        lax.broadcasted_iota(jnp.int32, (GROUP, atoms), 1) % GROUP
        == lax.broadcasted_iota(jnp.int32, (GROUP, atoms), 0)
    )
    target = lax.broadcasted_iota(jnp.int32, (256, atoms), 0).astype(F32).astype(BF16)

    def group(g):
        table = table_ref[g]
        named = [(table[18:19, :] - at).astype(BF16) for at in range(0, extent, 256)]
        hot = jnp.concatenate(
            [jnp.where(target == name, BF16(1), BF16(0)) for name in named], axis=0
        )
        spread = jnp.concatenate(
            [jnp.where(mask, table[r : r + 1, :], 0.0) for r in range(18)], axis=0
        )
        top = spread.astype(BF16)
        rest = (spread - top.astype(F32)).astype(BF16)
        both = ((1,), (1,))
        dense = dot(top, hot, both) + dot(rest, hot, both)
        hi = dense.astype(BF16)
        lo = (dense - hi.astype(F32)).astype(BF16)
        for e in range(2):
            for a in range(3):
                at = pl.ds(pl.multiple_of((e * 3 + a) * atoms + g * GROUP, GROUP), GROUP)
                for b in range(3):
                    r = (e * 9 + 3 * a + b) * GROUP
                    near, far = slice(b * atoms, (b + 1) * atoms), slice(b * halo, (b + 1) * halo)
                    own_hi_ref[at, near] = hi[r : r + GROUP, :atoms]
                    own_lo_ref[at, near] = lo[r : r + GROUP, :atoms]
                    hi_ref[at, far] = hi[r : r + GROUP, atoms:]
                    lo_ref[at, far] = lo[r : r + GROUP, atoms:]

    def several(step, carry):
        for g in range(4):
            group(4 * step + g)
        return carry

    lax.fori_loop(0, groups // 4, several, 0)
    own = own_ref[...]
    for part in range(6):
        at = slice(part * atoms, (part + 1) * atoms)
        flux_ref[at, :] = dot(own_hi_ref[at, :], own) + dot(own_lo_ref[at, :], own)


def relay_kernel(part_hbm, below_hbm, above_hbm, *refs):
    for got_ref, given_ref in zip(refs[: len(refs) // 2], refs[len(refs) // 2 :]):
        given_ref[...] = got_ref[...]


def flux_kernel(e, part_ref, hi_ref, lo_ref, below_ref, above_ref, flux_ref, halo_ref):
    count = below_ref.shape[0] // 3
    for b in range(3):
        at = 2 * b * count
        halo_ref[at : at + count] = below_ref[b * count : (b + 1) * count]
        halo_ref[at + count : at + 2 * count] = above_ref[b * count : (b + 1) * count]
    atoms = flux_ref.shape[0] // 3
    halo = halo_ref[...]
    for a in range(3):
        at = slice((e * 3 + a) * atoms, (e * 3 + a + 1) * atoms)
        flux = part_ref[at, :] + (dot(hi_ref[at, :], halo) + dot(lo_ref[at, :], halo))
        flux_ref[a * atoms : (a + 1) * atoms, :] = flux.astype(BF16)


def terms_of(quarter_refs, store, wanted=lambda tile: True):
    tiles = len(quarter_refs) // 2
    me, core = lax.axis_index("blk"), lax.axis_index("dir")
    for j in range(tiles):
        tile = lax.rem(me - j + tiles, tiles)

        @pl.when(wanted(tile))
        def _():
            for s in range(2):
                store(2 * tile + (core if s == 0 else 1 - core), quarter_refs[2 * j + s])


def couple_kernel(flux0_ref, flux1_ref, *refs):
    *quarter_refs, out_ref = refs
    half = quarter_refs[0].shape[0]
    block = out_ref.shape[1]
    core = lax.axis_index("dir")

    def store(quarter, turned_ref):
        for e, flux_ref in enumerate((flux0_ref, flux1_ref)):
            term = dot(turned_ref[...], flux_ref[...]).astype(BF16)
            for t in range(half // block):
                at = 2 * (quarter * (half // block) + t) + (core if e == 0 else 1 - core)
                out_ref[at] = term[t * block : (t + 1) * block]

    terms_of(quarter_refs, store)


def sum_kernel(scale, terms_ref, out_ref):
    pairs, block, half = terms_ref.shape
    for c in range(2):
        total = terms_ref[c].astype(F32)
        for d in range(1, pairs // 2):
            total = total + terms_ref[2 * d + c].astype(F32)
        out_ref[0, :, c * half : (c + 1) * half] = total * scale


def far_kernel(flux_ref, *refs):
    *quarter_refs, far_ref, add_ref = refs
    home = lax.axis_index("dom")

    def store(quarter, turned_ref):
        term = dot(turned_ref[...], flux_ref[...])

        @pl.when((quarter ^ home) == 3)
        def _():
            far_ref[...] = term.astype(BF16)

        @pl.when((quarter ^ home) == 2)
        def _():
            add_ref[...] = term

    terms_of(quarter_refs, store, lambda tile: (tile ^ (home // 2)) == 1)


def near_kernel(flux0_ref, flux1_ref, *refs):
    *quarter_refs, near0_ref, near1_ref, keep_ref, give_ref = refs
    home = lax.axis_index("dom")

    def store(quarter, turned_ref):
        terms = [dot(turned_ref[...], ref[...]) for ref in (flux0_ref, flux1_ref)]

        @pl.when((quarter ^ home) == 1)
        def _():
            near0_ref[...] = terms[0].astype(BF16)
            near1_ref[...] = terms[1].astype(BF16)

        @pl.when((quarter ^ home) == 0)
        def _():
            keep_ref[...] = terms[0]
            give_ref[...] = terms[1].astype(BF16)

    terms_of(quarter_refs, store, lambda tile: (tile ^ (home // 2)) == 0)


def add_kernel(far_ref, add_ref, sum_ref):
    sum_ref[...] = (add_ref[...] + far_ref[...].astype(F32)).astype(BF16)


def halving_sum_kernel(scale, keep_ref, give_ref, near0_ref, near1_ref, sum0_ref, sum1_ref, out_ref):
    half = keep_ref.shape[1]
    core = lax.axis_index("dir")
    mine = pl.ds(pl.multiple_of(core * half, 128), half)
    other = pl.ds(pl.multiple_of((1 - core) * half, 128), half)
    for at, first, near, far in (
        (mine, keep_ref, near0_ref, sum0_ref),
        (other, give_ref, near1_ref, sum1_ref),
    ):
        total = first[...].astype(F32) + near[...].astype(F32) + far[...].astype(F32)
        out_ref[0, :, at] = total * scale


def shift(value, axis, by):
    length = lax.axis_size(axis)
    return lax.ppermute(value, axis, [(i, (i + by) % length) for i in range(length)])


def swap(value, away, other_core):
    domains = lax.axis_size("dom")
    pairs = [
        (2 * d + c, 2 * (d ^ away) + (c ^ other_core)) for d in range(domains) for c in range(2)
    ]
    return lax.ppermute(value, ("dom", "dir"), pairs)


def shape(dims, dtype):
    return jax.ShapeDtypeStruct(dims, dtype)


def per_device(panel_vectors, force_blocks, bond_vectors, neighbours, boundary_low, boundary_high):
    rows, cols = panel_vectors.shape
    atoms = rows // 3
    half = cols // 2
    count = boundary_low.shape[0]
    domains, tiles = lax.axis_size("dom"), lax.axis_size("blk")
    block = cols * tiles // domains
    vmem = pl.BlockSpec(memory_space=pltpu.VMEM)
    hbm = pl.BlockSpec(memory_space=pltpu.HBM)
    anywhere = pl.BlockSpec(memory_space=pl.ANY)

    lists = [boundary_low.reshape(1, count), boundary_high.reshape(1, count)]
    forces = force_blocks.transpose(1, 0, 2)
    prepared = (
        shape((half, rows), BF16),
        shape((3 * count, half), BF16),
        shape((3 * count, half), BF16),
        shape((rows, half), BF16),
    )
    turned, send_low, send_high, own, sources, bonds = pl.pallas_call(
        prep_kernel,
        out_shape=(
            *prepared,
            shape((11, *neighbours.shape), F32),
            shape(bond_vectors.shape, F32),
        ),
        in_specs=[hbm] * 6,
        out_specs=(hbm,) * 6,
        scratch_shapes=[
            pltpu.VMEM((rows, half), BF16),
            pltpu.VMEM((1, count), jnp.int32),
            pltpu.VMEM((1, count), jnp.int32),
            pltpu.VMEM(neighbours.shape, jnp.int32),
            *[pltpu.VMEM(like.shape, like.dtype) for like in prepared],
            pltpu.VMEM((11, *neighbours.shape), F32),
            pltpu.SemaphoreType.DMA((6,)),
            pltpu.SemaphoreType.DMA((6,)),
        ],
        compiler_params=params(58),
        name="prep",
    )(panel_vectors, *lists, forces, bond_vectors, neighbours)
    quarters = [shift(turned, "blk", j) for j in range(1, tiles)]
    turned_other = shift(turned, "dir", 1)
    other_bonds = shift(bonds, "dir", 1)
    below = shift(send_high, "dom", 1)
    above = shift(send_low, "dom", -1)

    partial_flux, hi, lo = pl.pallas_call(
        weights_kernel,
        out_shape=(
            shape((2 * rows, half), F32),
            shape((2 * rows, 6 * count), BF16),
            shape((2 * rows, 6 * count), BF16),
        ),
        in_specs=[vmem] * 3,
        out_specs=(vmem,) * 3,
        scratch_shapes=[
            pltpu.VMEM((atoms // GROUP, 24, atoms), F32),
            pltpu.VMEM((2 * rows, rows), BF16),
            pltpu.VMEM((2 * rows, rows), BF16),
        ],
        compiler_params=params(32),
        cost_estimate=pl.CostEstimate(
            flops=8*10**9, bytes_accessed=10**7, transcendentals=0
        ),
        name="weights",
    )(sources, other_bonds, own)

    quarters = pl.pallas_call(
        relay_kernel,
        out_shape=[shape(turned.shape, BF16)] * (tiles - 1),
        in_specs=[anywhere] * 3 + [vmem] * len(quarters),
        out_specs=[vmem] * (tiles - 1),
        compiler_params=params(16),
        name="relay",
    )(partial_flux, below, above, *quarters)
    given = [turned, turned_other]
    for quarter in quarters:
        given += [quarter, shift(quarter, "dir", 1)]

    def flux_of(e):
        return pl.pallas_call(
            functools.partial(flux_kernel, e),
            out_shape=shape((rows, half), BF16),
            in_specs=[vmem] * 5,
            out_specs=vmem,
            scratch_shapes=[pltpu.VMEM((6 * count, half), BF16)],
            compiler_params=params(16),
            cost_estimate=pl.CostEstimate(
                flops=10**9, bytes_accessed=10**6, transcendentals=0
            ),
            name="flux",
        )(partial_flux, hi, lo, below, above)

    scale = (3.0 * atoms * domains) ** (-0.5)
    result = shape((1, block, cols), F32)
    if domains == 4 and block == half:
        sent, kept = shape((block, half), BF16), shape((block, half), F32)
        cost = pl.CostEstimate(flops=4 * 10**8, bytes_accessed=10**6, transcendentals=0)

        def far_of(flux):
            far, add = pl.pallas_call(
                far_kernel,
                out_shape=(sent, kept),
                in_specs=[vmem] * (1 + len(given)),
                out_specs=(vmem,) * 2,
                compiler_params=params(16),
                cost_estimate=cost,
                name="far",
            )(flux, *given)
            return far, add

        flux0, flux1 = flux_of(0), flux_of(1)
        far0, add0 = far_of(flux0)
        far1, add1 = far_of(flux1)
        far0, far1 = swap(far0, 1, 0), swap(far1, 1, 0)
        near0, near1, keep, give = pl.pallas_call(
            near_kernel,
            out_shape=(sent, sent, kept, sent),
            in_specs=[vmem] * (2 + len(given)),
            out_specs=(vmem,) * 4,
            compiler_params=params(16),
            cost_estimate=cost,
            name="near",
        )(flux0, flux1, *given)
        give, near0, near1 = swap(give, 0, 1), swap(near0, 1, 0), swap(near1, 1, 1)

        def sum_of(far, add):
            return pl.pallas_call(
                add_kernel,
                out_shape=sent,
                in_specs=[vmem] * 2,
                out_specs=vmem,
                compiler_params=params(16),
                name="add",
            )(far, add)

        sum0, sum1 = swap(sum_of(far0, add0), 2, 0), swap(sum_of(far1, add1), 2, 1)
        return pl.pallas_call(
            lambda *refs: halving_sum_kernel(scale, *refs),
            out_shape=result,
            in_specs=[vmem] * 6,
            out_specs=vmem,
            compiler_params=params(16),
            name="total",
        )(keep, give, near0, near1, sum0, sum1)

    terms = pl.pallas_call(
        couple_kernel,
        out_shape=shape((2 * domains, block, half), BF16),
        in_specs=[vmem] * (2 + len(given)),
        out_specs=vmem,
        compiler_params=params(16),
        name="couple",
    )(flux_of(0), flux_of(1), *given)
    terms = lax.all_to_all(terms, ("dom", "dir"), split_axis=0, concat_axis=0, tiled=True)
    return pl.pallas_call(
        lambda *refs: sum_kernel(scale, *refs),
        out_shape=result,
        in_specs=[vmem],
        out_specs=vmem,
        compiler_params=params(),
        name="total",
    )(terms)


def solution(mesh):
    in_specs = (
        P("dom", ("panel", "blk")),
        P(None, None, "dom"),
        P("dir", None, "dom"),
        P(None, "dom"),
        P("dom"),
        P("dom"),
    )
    out_specs = P("dir", ("panel", "dom"), "blk")
    return jax.shard_map(
        per_device, mesh=mesh, in_specs=in_specs, out_specs=out_specs, check_vma=False
    )
```

```python
import functools

import jax
import jax.numpy as jnp
from jax import lax
from jax.experimental import pallas as pl
from jax.experimental.pallas import tpu as pltpu
from jax.sharding import PartitionSpec as P

GROUP = 16
BF16 = jnp.bfloat16
F32 = jnp.float32


def params(mib=24):
    return pltpu.CompilerParams(vmem_limit_bytes=mib * 1024 * 1024)


def dot(a, b, contract=((1,), (0,))):
    return lax.dot_general(a, b, (contract, ((), ())), preferred_element_type=F32)


def one_hot(mask):
    return jnp.where(mask, 1.0, 0.0).astype(BF16)


def my_columns(half):
    return pl.ds(pl.multiple_of(lax.axis_index("dir") * half, 128), half)


def prep_kernel(
    v_hbm, low_hbm, high_hbm, force_hbm, bond_hbm, near_hbm,
    turned_hbm, send_low_hbm, send_high_hbm, source_hbm, bond_out_hbm,
    v_ref, low_ref, high_ref, near_ref, turned_ref, send_low_ref, send_high_ref,
    source_ref, in_sems, out_sems,
):
    rows, half = v_ref.shape
    atoms = rows // 3
    arriving = [
        pltpu.make_async_copy(source, target, in_sems.at[i])
        for i, (source, target) in enumerate(
            (
                (v_hbm.at[:, my_columns(half)], v_ref),
                (low_hbm, low_ref),
                (high_hbm, high_ref),
                (near_hbm, near_ref),
                (force_hbm, source_ref.at[0:9]),
                (bond_hbm, source_ref.at[9:10]),
            )
        )
    ]
    for copy in arriving:
        copy.start()
    leaving = []

    def leave(ref, hbm):
        copy = pltpu.make_async_copy(ref, hbm, out_sems.at[len(leaving)])
        copy.start()
        leaving.append(copy)

    lane = lax.broadcasted_iota(jnp.int32, (atoms, rows), 1)
    atom = lax.broadcasted_iota(jnp.int32, (atoms, rows), 0)
    hot = [one_hot(lane == 3 * atom + b) for b in range(3)]
    for copy in arriving[1:]:
        copy.wait()
    source_ref[10] = near_ref[...].astype(F32)
    leave(source_ref.at[9:10], bond_out_hbm)
    leave(source_ref, source_hbm)
    picks = []
    for list_ref in (high_ref, low_ref):
        count = list_ref.shape[1]
        named = jnp.broadcast_to(list_ref[...], (128, count)).T
        lane = lax.broadcasted_iota(jnp.int32, (count, 128), 1)
        for b in range(3):
            wanted = 3 * named + b
            picks.append(
                jnp.concatenate(
                    [one_hot(lane + t * 128 == wanted) for t in range(rows // 128)], axis=1
                )
            )
    arriving[0].wait()
    v = v_ref[...]
    for b in range(3):
        turned_ref[:, b * atoms : (b + 1) * atoms] = dot(hot[b], v).T.astype(BF16)
    leave(turned_ref, turned_hbm)
    for i, (send_ref, send_hbm) in enumerate(
        ((send_high_ref, send_high_hbm), (send_low_ref, send_low_hbm))
    ):
        for b in range(3):
            send_ref[b * count : (b + 1) * count, :] = dot(picks[3 * i + b], v).astype(BF16)
        leave(send_ref, send_hbm)
    for copy in leaving:
        copy.wait()


def weights_kernel(
    source_ref, other_ref, turned_ref,
    flux_ref, hi_ref, lo_ref, table_ref, own_hi_ref, own_lo_ref,
):
    _, steps, atoms = source_ref.shape
    groups = atoms // GROUP
    halo = hi_ref.shape[1] // 3
    extent = atoms + halo
    bonds = (source_ref[9], other_ref[0])
    lane = lax.broadcasted_iota(jnp.int32, (24, atoms), 1)
    rows = []
    for k in range(steps):
        force = source_ref[0:9, k, :]
        near = source_ref[10, k : k + 1, :]
        rows.append(
            jnp.concatenate(
                [force * bonds[0][k : k + 1, :], force * bonds[1][k : k + 1, :]]
                + [jnp.broadcast_to(near, (6, atoms))],
                axis=0,
            )
        )
    bit = 1
    while bit < steps:
        taken = ((lane // GROUP) & bit) != 0
        turned = list(rows)
        for p in range(steps):
            if p & bit:
                continue
            q = p | bit
            turned[p] = jnp.where(taken, pltpu.roll(rows[q], GROUP * bit, 1), rows[p])
            turned[q] = jnp.where(taken, rows[q], pltpu.roll(rows[p], atoms - GROUP * bit, 1))
        rows = turned
        bit *= 2
    for g in range(groups):
        table_ref[g] = rows[g]

    mask = (
        lax.broadcasted_iota(jnp.int32, (GROUP, atoms), 1) % GROUP
        == lax.broadcasted_iota(jnp.int32, (GROUP, atoms), 0)
    )
    target = lax.broadcasted_iota(jnp.int32, (256, atoms), 0).astype(F32).astype(BF16)

    def group(g):
        table = table_ref[g]
        named = [(table[18:19, :] - at).astype(BF16) for at in range(0, extent, 256)]
        hot = jnp.concatenate(
            [jnp.where(target == name, BF16(1), BF16(0)) for name in named], axis=0
        )
        spread = jnp.concatenate(
            [jnp.where(mask, table[r : r + 1, :], 0.0) for r in range(18)], axis=0
        )
        top = spread.astype(BF16)
        rest = (spread - top.astype(F32)).astype(BF16)
        both = ((1,), (1,))
        dense = dot(top, hot, both) + dot(rest, hot, both)
        hi = dense.astype(BF16)
        lo = (dense - hi.astype(F32)).astype(BF16)
        for e in range(2):
            for a in range(3):
                at = pl.ds(pl.multiple_of((e * 3 + a) * atoms + g * GROUP, GROUP), GROUP)
                for b in range(3):
                    r = (e * 9 + 3 * a + b) * GROUP
                    near, far = slice(b * atoms, (b + 1) * atoms), slice(b * halo, (b + 1) * halo)
                    own_hi_ref[at, near] = hi[r : r + GROUP, :atoms]
                    own_lo_ref[at, near] = lo[r : r + GROUP, :atoms]
                    hi_ref[at, far] = hi[r : r + GROUP, atoms:]
                    lo_ref[at, far] = lo[r : r + GROUP, atoms:]

    def several(step, carry):
        for g in range(4):
            group(4 * step + g)
        return carry

    lax.fori_loop(0, groups // 4, several, 0)
    turned = turned_ref[...]
    for part in range(6):
        at = slice(part * atoms, (part + 1) * atoms)
        hi, lo = own_hi_ref[at, :], own_lo_ref[at, :]
        flux_ref[at, :] = dot(hi, turned, ((1,), (1,))) + dot(lo, turned, ((1,), (1,)))


def relay_kernel(part_hbm, below_hbm, above_hbm, *refs):
    for got_ref, given_ref in zip(refs[: len(refs) // 2], refs[len(refs) // 2 :]):
        given_ref[...] = got_ref[...]


def flux_kernel(e, part_ref, hi_ref, lo_ref, below_ref, above_ref, flux_ref, halo_ref):
    count = below_ref.shape[0] // 3
    for b in range(3):
        at = 2 * b * count
        halo_ref[at : at + count] = below_ref[b * count : (b + 1) * count]
        halo_ref[at + count : at + 2 * count] = above_ref[b * count : (b + 1) * count]
    atoms = flux_ref.shape[0] // 3
    halo = halo_ref[...]
    for a in range(3):
        at = slice((e * 3 + a) * atoms, (e * 3 + a + 1) * atoms)
        flux = part_ref[at, :] + (dot(hi_ref[at, :], halo) + dot(lo_ref[at, :], halo))
        flux_ref[a * atoms : (a + 1) * atoms, :] = flux.astype(BF16)


def terms_of(quarter_refs, store, wanted=lambda tile: True):
    tiles = len(quarter_refs) // 2
    me, core = lax.axis_index("blk"), lax.axis_index("dir")
    for j in range(tiles):
        tile = lax.rem(me - j + tiles, tiles)

        @pl.when(wanted(tile))
        def _():
            for s in range(2):
                store(2 * tile + (core if s == 0 else 1 - core), quarter_refs[2 * j + s])


def couple_kernel(flux0_ref, flux1_ref, *refs):
    *quarter_refs, out_ref = refs
    half = quarter_refs[0].shape[0]
    block = out_ref.shape[1]
    core = lax.axis_index("dir")

    def store(quarter, turned_ref):
        for e, flux_ref in enumerate((flux0_ref, flux1_ref)):
            term = dot(turned_ref[...], flux_ref[...]).astype(BF16)
            for t in range(half // block):
                at = 2 * (quarter * (half // block) + t) + (core if e == 0 else 1 - core)
                out_ref[at] = term[t * block : (t + 1) * block]

    terms_of(quarter_refs, store)


def sum_kernel(scale, terms_ref, out_ref):
    pairs, block, half = terms_ref.shape
    for c in range(2):
        total = terms_ref[c].astype(F32)
        for d in range(1, pairs // 2):
            total = total + terms_ref[2 * d + c].astype(F32)
        out_ref[0, :, c * half : (c + 1) * half] = total * scale


def far_kernel(after, flux_ref, *refs):
    *quarter_refs, far_ref, add_ref = refs
    home = lax.axis_index("dom")

    def store(quarter, turned_ref):
        term = dot(turned_ref[...], flux_ref[...])

        @pl.when((quarter ^ home) == 3)
        def _():
            far_ref[...] = term.astype(BF16)

        @pl.when((quarter ^ home) == 2)
        def _():
            add_ref[...] = term

    terms_of(quarter_refs, store, lambda tile: (tile ^ (home // 2)) == 1)


def near_kernel(flux0_ref, flux1_ref, *refs):
    *quarter_refs, near0_ref, near1_ref, keep_ref, give_ref = refs
    home = lax.axis_index("dom")

    def store(quarter, turned_ref):
        terms = [dot(turned_ref[...], ref[...]) for ref in (flux0_ref, flux1_ref)]

        @pl.when((quarter ^ home) == 1)
        def _():
            near0_ref[...] = terms[0].astype(BF16)
            near1_ref[...] = terms[1].astype(BF16)

        @pl.when((quarter ^ home) == 0)
        def _():
            keep_ref[...] = terms[0]
            give_ref[...] = terms[1].astype(BF16)

    terms_of(quarter_refs, store, lambda tile: (tile ^ (home // 2)) == 0)


def add_kernel(far_ref, add_ref, *refs):
    held_refs, (sum_ref, *given_refs) = refs[: len(refs) // 2], refs[len(refs) // 2 :]
    sum_ref[...] = (add_ref[...] + far_ref[...].astype(F32)).astype(BF16)
    for held_ref, given_ref in zip(held_refs, given_refs):
        given_ref[...] = held_ref[...]


def halving_sum_kernel(scale, keep_ref, give_ref, near0_ref, near1_ref, sum0_ref, sum1_ref, out_ref):
    half = keep_ref.shape[1]
    core = lax.axis_index("dir")
    mine = pl.ds(pl.multiple_of(core * half, 128), half)
    other = pl.ds(pl.multiple_of((1 - core) * half, 128), half)
    for at, first, near, far in (
        (mine, keep_ref, near0_ref, sum0_ref),
        (other, give_ref, near1_ref, sum1_ref),
    ):
        total = first[...].astype(F32) + near[...].astype(F32) + far[...].astype(F32)
        out_ref[0, :, at] = total * scale


def shift(value, axis, by):
    length = lax.axis_size(axis)
    return lax.ppermute(value, axis, [(i, (i + by) % length) for i in range(length)])


def swap(value, away, other_core):
    domains = lax.axis_size("dom")
    pairs = [
        (2 * d + c, 2 * (d ^ away) + (c ^ other_core)) for d in range(domains) for c in range(2)
    ]
    return lax.ppermute(value, ("dom", "dir"), pairs)


def shape(dims, dtype):
    return jax.ShapeDtypeStruct(dims, dtype)


def per_device(panel_vectors, force_blocks, bond_vectors, neighbours, boundary_low, boundary_high):
    rows, cols = panel_vectors.shape
    atoms = rows // 3
    half = cols // 2
    count = boundary_low.shape[0]
    domains, tiles = lax.axis_size("dom"), lax.axis_size("blk")
    block = cols * tiles // domains
    vmem = pl.BlockSpec(memory_space=pltpu.VMEM)
    hbm = pl.BlockSpec(memory_space=pltpu.HBM)
    anywhere = pl.BlockSpec(memory_space=pl.ANY)

    lists = [boundary_low.reshape(1, count), boundary_high.reshape(1, count)]
    forces = force_blocks.transpose(1, 0, 2)
    prepared = (
        shape((half, rows), BF16),
        shape((3 * count, half), BF16),
        shape((3 * count, half), BF16),
    )
    turned, send_low, send_high, sources, bonds = pl.pallas_call(
        prep_kernel,
        out_shape=(
            *prepared,
            shape((11, *neighbours.shape), F32),
            shape(bond_vectors.shape, F32),
        ),
        in_specs=[hbm] * 6,
        out_specs=(hbm,) * 5,
        scratch_shapes=[
            pltpu.VMEM((rows, half), BF16),
            pltpu.VMEM((1, count), jnp.int32),
            pltpu.VMEM((1, count), jnp.int32),
            pltpu.VMEM(neighbours.shape, jnp.int32),
            *[pltpu.VMEM(like.shape, like.dtype) for like in prepared],
            pltpu.VMEM((11, *neighbours.shape), F32),
            pltpu.SemaphoreType.DMA((6,)),
            pltpu.SemaphoreType.DMA((5,)),
        ],
        compiler_params=params(58),
        name="prep",
    )(panel_vectors, *lists, forces, bond_vectors, neighbours)
    quarters = [shift(turned, "blk", j) for j in range(1, tiles)]
    turned_other = shift(turned, "dir", 1)
    other_bonds = shift(bonds, "dir", 1)
    below = shift(send_high, "dom", 1)
    above = shift(send_low, "dom", -1)

    partial_flux, hi, lo = pl.pallas_call(
        weights_kernel,
        out_shape=(
            shape((2 * rows, half), F32),
            shape((2 * rows, 6 * count), BF16),
            shape((2 * rows, 6 * count), BF16),
        ),
        in_specs=[vmem] * 3,
        out_specs=(vmem,) * 3,
        scratch_shapes=[
            pltpu.VMEM((atoms // GROUP, 24, atoms), F32),
            pltpu.VMEM((2 * rows, rows), BF16),
            pltpu.VMEM((2 * rows, rows), BF16),
        ],
        compiler_params=params(32),
        cost_estimate=pl.CostEstimate(
            flops=8*10**9, bytes_accessed=10**7, transcendentals=0
        ),
        name="weights",
    )(sources, other_bonds, turned)

    quarters = pl.pallas_call(
        relay_kernel,
        out_shape=[shape(turned.shape, BF16)] * (tiles - 1),
        in_specs=[anywhere] * 3 + [vmem] * len(quarters),
        out_specs=[vmem] * (tiles - 1),
        compiler_params=params(16),
        name="relay",
    )(partial_flux, below, above, *quarters)
    given = [turned, turned_other]
    for quarter in quarters:
        given += [quarter, shift(quarter, "dir", 1)]

    def flux_of(e):
        return pl.pallas_call(
            functools.partial(flux_kernel, e),
            out_shape=shape((rows, half), BF16),
            in_specs=[vmem] * 5,
            out_specs=vmem,
            scratch_shapes=[pltpu.VMEM((6 * count, half), BF16)],
            compiler_params=params(16),
            cost_estimate=pl.CostEstimate(
                flops=10**9, bytes_accessed=10**6, transcendentals=0
            ),
            name="flux",
        )(partial_flux, hi, lo, below, above)

    scale = (3.0 * atoms * domains) ** (-0.5)
    result = shape((1, block, cols), F32)
    if domains == 4 and block == half:
        sent, kept = shape((block, half), BF16), shape((block, half), F32)
        cost = pl.CostEstimate(flops=4 * 10**8, bytes_accessed=10**6, transcendentals=0)

        def far_of(flux, after):
            far, add = pl.pallas_call(
                far_kernel,
                out_shape=(sent, kept),
                in_specs=[anywhere] + [vmem] * (1 + len(given)),
                out_specs=(vmem,) * 2,
                compiler_params=params(16),
                cost_estimate=cost,
                name="far",
            )(after, flux, *given)
            return far, add

        flux0, flux1 = flux_of(0), flux_of(1)
        far0, add0 = far_of(flux0, flux1)
        far1, add1 = far_of(flux1, far0)
        far0, far1 = swap(far0, 1, 0), swap(far1, 1, 0)
        near0, near1, keep, give = pl.pallas_call(
            near_kernel,
            out_shape=(sent, sent, kept, sent),
            in_specs=[vmem] * (2 + len(given)),
            out_specs=(vmem,) * 4,
            compiler_params=params(16),
            cost_estimate=cost,
            name="near",
        )(flux0, flux1, *given)

        def sum_of(far, add, *handed_on):
            return pl.pallas_call(
                add_kernel,
                out_shape=[sent] * (1 + len(handed_on)),
                in_specs=[vmem] * (2 + len(handed_on)),
                out_specs=[vmem] * (1 + len(handed_on)),
                compiler_params=params(16),
                name="add",
            )(far, add, *handed_on)

        near0 = swap(near0, 1, 0)
        sum0 = swap(sum_of(far0, add0)[0], 2, 0)
        sum1, near1, give = sum_of(far1, add1, near1, give)
        sum1, near1, give = swap(sum1, 2, 1), swap(near1, 1, 1), swap(give, 0, 1)
        return pl.pallas_call(
            lambda *refs: halving_sum_kernel(scale, *refs),
            out_shape=result,
            in_specs=[vmem] * 6,
            out_specs=vmem,
            compiler_params=params(16),
            name="total",
        )(keep, give, near0, near1, sum0, sum1)

    terms = pl.pallas_call(
        couple_kernel,
        out_shape=shape((2 * domains, block, half), BF16),
        in_specs=[vmem] * (2 + len(given)),
        out_specs=vmem,
        compiler_params=params(16),
        name="couple",
    )(flux_of(0), flux_of(1), *given)
    terms = lax.all_to_all(terms, ("dom", "dir"), split_axis=0, concat_axis=0, tiled=True)
    return pl.pallas_call(
        lambda *refs: sum_kernel(scale, *refs),
        out_shape=result,
        in_specs=[vmem],
        out_specs=vmem,
        compiler_params=params(),
        name="total",
    )(terms)


def solution(mesh):
    in_specs = (
        P("dom", ("panel", "blk")),
        P(None, None, "dom"),
        P("dir", None, "dom"),
        P(None, "dom"),
        P("dom"),
        P("dom"),
    )
    out_specs = P("dir", ("panel", "dom"), "blk")
    return jax.shard_map(
        per_device, mesh=mesh, in_specs=in_specs, out_specs=out_specs, check_vma=False
    )
```

```python
import functools

import jax
import jax.numpy as jnp
from jax import lax
from jax.experimental import pallas as pl
from jax.experimental.pallas import tpu as pltpu
from jax.sharding import PartitionSpec as P

GROUP = 16
BF16 = jnp.bfloat16
F32 = jnp.float32


def params(mib=24):
    return pltpu.CompilerParams(vmem_limit_bytes=mib * 1024 * 1024)


def dot(a, b, contract=((1,), (0,))):
    return lax.dot_general(a, b, (contract, ((), ())), preferred_element_type=F32)


def one_hot(mask):
    return jnp.where(mask, 1.0, 0.0).astype(BF16)


def my_columns(half):
    return pl.ds(pl.multiple_of(lax.axis_index("dir") * half, 128), half)


def prep_kernel(
    v_hbm, low_hbm, high_hbm, force_hbm, bond_hbm, near_hbm,
    turned_hbm, send_low_hbm, send_high_hbm, source_hbm, bond_out_hbm,
    v_ref, low_ref, high_ref, near_ref, turned_ref, send_low_ref, send_high_ref,
    source_ref, pick_ref, wide_ref, in_sems, out_sems,
):
    rows, half = v_ref.shape
    atoms = rows // 3
    arriving = [
        pltpu.make_async_copy(source, target, in_sems.at[i])
        for i, (source, target) in enumerate(
            (
                (v_hbm.at[:, my_columns(half)], v_ref),
                (low_hbm, low_ref),
                (high_hbm, high_ref),
                (near_hbm, near_ref),
                (force_hbm, source_ref.at[0:9]),
                (bond_hbm, source_ref.at[9:10]),
            )
        )
    ]
    for copy in arriving:
        copy.start()
    leaving = []

    def leave(ref, hbm):
        copy = pltpu.make_async_copy(ref, hbm, out_sems.at[len(leaving)])
        copy.start()
        leaving.append(copy)

    for copy in arriving[1:]:
        copy.wait()
    source_ref[10] = near_ref[...].astype(F32)
    leave(source_ref.at[9:10], bond_out_hbm)
    leave(source_ref, source_hbm)
    for i, list_ref in enumerate((high_ref, low_ref)):
        count = list_ref.shape[1]
        named = jnp.broadcast_to(list_ref[...], (128, count)).T
        lane = lax.broadcasted_iota(jnp.int32, (count, 128), 1)
        for b in range(3):
            wanted = 3 * named + b
            at = (3 * i + b) * count
            for t in range(rows // 128):
                pick_ref[at : at + count, t * 128 : (t + 1) * 128] = one_hot(
                    lane + t * 128 == wanted
                )
    arriving[0].wait()
    for t in range(half // 128):
        columns = slice(t * 128, (t + 1) * 128)
        wide_ref[t] = v_ref[:, columns].astype(F32)
        for b in range(3):
            part = wide_ref[t, pl.ds(b, atoms, stride=3), :]
            turned_ref[columns, b * atoms : (b + 1) * atoms] = part.T.astype(BF16)
    leave(turned_ref, turned_hbm)
    picked = dot(pick_ref[...], v_ref[...]).astype(BF16)
    send_high_ref[...] = picked[: 3 * count]
    leave(send_high_ref, send_high_hbm)
    send_low_ref[...] = picked[3 * count :]
    leave(send_low_ref, send_low_hbm)
    for copy in leaving:
        copy.wait()


def weights_kernel(
    source_ref, other_ref, turned_ref,
    flux_ref, hi_ref, lo_ref, table_ref, own_hi_ref, own_lo_ref,
):
    _, steps, atoms = source_ref.shape
    groups = atoms // GROUP
    halo = hi_ref.shape[1] // 3
    extent = atoms + halo
    bonds = (source_ref[9], other_ref[0])
    lane = lax.broadcasted_iota(jnp.int32, (24, atoms), 1)
    rows = []
    for k in range(steps):
        force = source_ref[0:9, k, :]
        near = source_ref[10, k : k + 1, :]
        rows.append(
            jnp.concatenate(
                [force * bonds[0][k : k + 1, :], force * bonds[1][k : k + 1, :]]
                + [jnp.broadcast_to(near, (6, atoms))],
                axis=0,
            )
        )
    bit = 1
    while bit < steps:
        taken = ((lane // GROUP) & bit) != 0
        turned = list(rows)
        for p in range(steps):
            if p & bit:
                continue
            q = p | bit
            turned[p] = jnp.where(taken, pltpu.roll(rows[q], GROUP * bit, 1), rows[p])
            turned[q] = jnp.where(taken, rows[q], pltpu.roll(rows[p], atoms - GROUP * bit, 1))
        rows = turned
        bit *= 2
    for g in range(groups):
        table_ref[g] = rows[g]

    mask = (
        lax.broadcasted_iota(jnp.int32, (GROUP, atoms), 1) % GROUP
        == lax.broadcasted_iota(jnp.int32, (GROUP, atoms), 0)
    )
    target = lax.broadcasted_iota(jnp.int32, (256, atoms), 0).astype(F32).astype(BF16)

    def group(g):
        table = table_ref[g]
        named = [(table[18:19, :] - at).astype(BF16) for at in range(0, extent, 256)]
        hot = jnp.concatenate(
            [jnp.where(target == name, BF16(1), BF16(0)) for name in named], axis=0
        )
        spread = jnp.concatenate(
            [jnp.where(mask, table[r : r + 1, :], 0.0) for r in range(18)], axis=0
        )
        top = spread.astype(BF16)
        rest = (spread - top.astype(F32)).astype(BF16)
        both = ((1,), (1,))
        dense = dot(top, hot, both) + dot(rest, hot, both)
        hi = dense.astype(BF16)
        lo = (dense - hi.astype(F32)).astype(BF16)
        for e in range(2):
            for a in range(3):
                at = pl.ds(pl.multiple_of((e * 3 + a) * atoms + g * GROUP, GROUP), GROUP)
                for b in range(3):
                    r = (e * 9 + 3 * a + b) * GROUP
                    near, far = slice(b * atoms, (b + 1) * atoms), slice(b * halo, (b + 1) * halo)
                    own_hi_ref[at, near] = hi[r : r + GROUP, :atoms]
                    own_lo_ref[at, near] = lo[r : r + GROUP, :atoms]
                    hi_ref[at, far] = hi[r : r + GROUP, atoms:]
                    lo_ref[at, far] = lo[r : r + GROUP, atoms:]

    def several(step, carry):
        for g in range(4):
            group(4 * step + g)
        return carry

    lax.fori_loop(0, groups // 4, several, 0)
    turned = turned_ref[...]
    for e in range(2):
        at = slice(3 * e * atoms, 3 * (e + 1) * atoms)
        hi, lo = own_hi_ref[at, :], own_lo_ref[at, :]
        flux_ref[at, :] = dot(hi, turned, ((1,), (1,))) + dot(lo, turned, ((1,), (1,)))


def relay_kernel(part_hbm, below_hbm, above_hbm, *refs):
    for got_ref, given_ref in zip(refs[: len(refs) // 2], refs[len(refs) // 2 :]):
        given_ref[...] = got_ref[...]


def flux_kernel(e, part_ref, hi_ref, lo_ref, below_ref, above_ref, flux_ref, halo_ref):
    count = below_ref.shape[0] // 3
    for b in range(3):
        at = 2 * b * count
        halo_ref[at : at + count] = below_ref[b * count : (b + 1) * count]
        halo_ref[at + count : at + 2 * count] = above_ref[b * count : (b + 1) * count]
    atoms = flux_ref.shape[0] // 3
    halo = halo_ref[...]
    at = slice(3 * e * atoms, 3 * (e + 1) * atoms)
    flux = part_ref[at, :] + (dot(hi_ref[at, :], halo) + dot(lo_ref[at, :], halo))
    flux_ref[...] = flux.astype(BF16)


def terms_of(quarter_refs, store, wanted=lambda tile: True):
    tiles = len(quarter_refs) // 2
    me, core = lax.axis_index("blk"), lax.axis_index("dir")
    for j in range(tiles):
        tile = lax.rem(me - j + tiles, tiles)

        @pl.when(wanted(tile))
        def _():
            for s in range(2):
                store(2 * tile + (core if s == 0 else 1 - core), quarter_refs[2 * j + s])


def couple_kernel(flux0_ref, flux1_ref, *refs):
    *quarter_refs, out_ref = refs
    half = quarter_refs[0].shape[0]
    block = out_ref.shape[1]
    core = lax.axis_index("dir")

    def store(quarter, turned_ref):
        for e, flux_ref in enumerate((flux0_ref, flux1_ref)):
            term = dot(turned_ref[...], flux_ref[...]).astype(BF16)
            for t in range(half // block):
                at = 2 * (quarter * (half // block) + t) + (core if e == 0 else 1 - core)
                out_ref[at] = term[t * block : (t + 1) * block]

    terms_of(quarter_refs, store)


def sum_kernel(scale, terms_ref, out_ref):
    pairs, block, half = terms_ref.shape
    for c in range(2):
        total = terms_ref[c].astype(F32)
        for d in range(1, pairs // 2):
            total = total + terms_ref[2 * d + c].astype(F32)
        out_ref[0, :, c * half : (c + 1) * half] = total * scale


def far_kernel(after, flux_ref, *refs):
    *quarter_refs, far_ref, add_ref = refs
    home = lax.axis_index("dom")

    def store(quarter, turned_ref):
        term = dot(turned_ref[...], flux_ref[...])

        @pl.when((quarter ^ home) == 3)
        def _():
            far_ref[...] = term.astype(BF16)

        @pl.when((quarter ^ home) == 2)
        def _():
            add_ref[...] = term

    terms_of(quarter_refs, store, lambda tile: (tile ^ (home // 2)) == 1)


def near_kernel(flux0_ref, flux1_ref, *refs):
    *quarter_refs, near0_ref, near1_ref, keep_ref, give_ref = refs
    home = lax.axis_index("dom")

    def store(quarter, turned_ref):
        terms = [dot(turned_ref[...], ref[...]) for ref in (flux0_ref, flux1_ref)]

        @pl.when((quarter ^ home) == 1)
        def _():
            near0_ref[...] = terms[0].astype(BF16)
            near1_ref[...] = terms[1].astype(BF16)

        @pl.when((quarter ^ home) == 0)
        def _():
            keep_ref[...] = terms[0]
            give_ref[...] = terms[1].astype(BF16)

    terms_of(quarter_refs, store, lambda tile: (tile ^ (home // 2)) == 0)


def add_kernel(far_ref, add_ref, *refs):
    held_refs, (sum_ref, *given_refs) = refs[: len(refs) // 2], refs[len(refs) // 2 :]
    sum_ref[...] = (add_ref[...] + far_ref[...].astype(F32)).astype(BF16)
    for held_ref, given_ref in zip(held_refs, given_refs):
        given_ref[...] = held_ref[...]


def halving_sum_kernel(scale, keep_ref, give_ref, near0_ref, near1_ref, sum0_ref, sum1_ref, out_ref):
    half = keep_ref.shape[1]
    core = lax.axis_index("dir")
    mine = pl.ds(pl.multiple_of(core * half, 128), half)
    other = pl.ds(pl.multiple_of((1 - core) * half, 128), half)
    for at, first, near, far in (
        (mine, keep_ref, near0_ref, sum0_ref),
        (other, give_ref, near1_ref, sum1_ref),
    ):
        total = first[...].astype(F32) + near[...].astype(F32) + far[...].astype(F32)
        out_ref[0, :, at] = total * scale


def shift(value, axis, by):
    length = lax.axis_size(axis)
    return lax.ppermute(value, axis, [(i, (i + by) % length) for i in range(length)])


def swap(value, away, other_core):
    domains = lax.axis_size("dom")
    pairs = [
        (2 * d + c, 2 * (d ^ away) + (c ^ other_core)) for d in range(domains) for c in range(2)
    ]
    return lax.ppermute(value, ("dom", "dir"), pairs)


def shape(dims, dtype):
    return jax.ShapeDtypeStruct(dims, dtype)


def per_device(panel_vectors, force_blocks, bond_vectors, neighbours, boundary_low, boundary_high):
    rows, cols = panel_vectors.shape
    atoms = rows // 3
    half = cols // 2
    count = boundary_low.shape[0]
    domains, tiles = lax.axis_size("dom"), lax.axis_size("blk")
    block = cols * tiles // domains
    vmem = pl.BlockSpec(memory_space=pltpu.VMEM)
    hbm = pl.BlockSpec(memory_space=pltpu.HBM)
    anywhere = pl.BlockSpec(memory_space=pl.ANY)

    lists = [boundary_low.reshape(1, count), boundary_high.reshape(1, count)]
    forces = force_blocks.transpose(1, 0, 2)
    prepared = (
        shape((half, rows), BF16),
        shape((3 * count, half), BF16),
        shape((3 * count, half), BF16),
    )
    turned, send_low, send_high, sources, bonds = pl.pallas_call(
        prep_kernel,
        out_shape=(
            *prepared,
            shape((11, *neighbours.shape), F32),
            shape(bond_vectors.shape, F32),
        ),
        in_specs=[hbm] * 6,
        out_specs=(hbm,) * 5,
        scratch_shapes=[
            pltpu.VMEM((rows, half), BF16),
            pltpu.VMEM((1, count), jnp.int32),
            pltpu.VMEM((1, count), jnp.int32),
            pltpu.VMEM(neighbours.shape, jnp.int32),
            *[pltpu.VMEM(like.shape, like.dtype) for like in prepared],
            pltpu.VMEM((11, *neighbours.shape), F32),
            pltpu.VMEM((6 * count, rows), BF16),
            pltpu.VMEM((half // 128, rows, 128), F32),
            pltpu.SemaphoreType.DMA((6,)),
            pltpu.SemaphoreType.DMA((5,)),
        ],
        compiler_params=params(58),
        name="prep",
    )(panel_vectors, *lists, forces, bond_vectors, neighbours)
    quarters = [shift(turned, "blk", j) for j in range(1, tiles)]
    turned_other = shift(turned, "dir", 1)
    other_bonds = shift(bonds, "dir", 1)
    below = shift(send_high, "dom", 1)
    above = shift(send_low, "dom", -1)

    partial_flux, hi, lo = pl.pallas_call(
        weights_kernel,
        out_shape=(
            shape((2 * rows, half), F32),
            shape((2 * rows, 6 * count), BF16),
            shape((2 * rows, 6 * count), BF16),
        ),
        in_specs=[vmem] * 3,
        out_specs=(vmem,) * 3,
        scratch_shapes=[
            pltpu.VMEM((atoms // GROUP, 24, atoms), F32),
            pltpu.VMEM((2 * rows, rows), BF16),
            pltpu.VMEM((2 * rows, rows), BF16),
        ],
        compiler_params=params(32),
        cost_estimate=pl.CostEstimate(
            flops=8*10**9, bytes_accessed=10**7, transcendentals=0
        ),
        name="weights",
    )(sources, other_bonds, turned)

    quarters = pl.pallas_call(
        relay_kernel,
        out_shape=[shape(turned.shape, BF16)] * (tiles - 1),
        in_specs=[anywhere] * 3 + [vmem] * len(quarters),
        out_specs=[vmem] * (tiles - 1),
        compiler_params=params(16),
        name="relay",
    )(partial_flux, below, above, *quarters)
    given = [turned, turned_other]
    for quarter in quarters:
        given += [quarter, shift(quarter, "dir", 1)]

    def flux_of(e):
        return pl.pallas_call(
            functools.partial(flux_kernel, e),
            out_shape=shape((rows, half), BF16),
            in_specs=[vmem] * 5,
            out_specs=vmem,
            scratch_shapes=[pltpu.VMEM((6 * count, half), BF16)],
            compiler_params=params(16),
            cost_estimate=pl.CostEstimate(
                flops=10**9, bytes_accessed=10**6, transcendentals=0
            ),
            name="flux",
        )(partial_flux, hi, lo, below, above)

    scale = (3.0 * atoms * domains) ** (-0.5)
    result = shape((1, block, cols), F32)
    if domains == 4 and block == half:
        sent, kept = shape((block, half), BF16), shape((block, half), F32)
        cost = pl.CostEstimate(flops=4 * 10**8, bytes_accessed=10**6, transcendentals=0)

        def far_of(flux, after):
            far, add = pl.pallas_call(
                far_kernel,
                out_shape=(sent, kept),
                in_specs=[anywhere] + [vmem] * (1 + len(given)),
                out_specs=(vmem,) * 2,
                compiler_params=params(16),
                cost_estimate=cost,
                name="far",
            )(after, flux, *given)
            return far, add

        flux0, flux1 = flux_of(0), flux_of(1)
        far0, add0 = far_of(flux0, flux1)
        far1, add1 = far_of(flux1, far0)
        far0, far1 = swap(far0, 1, 0), swap(far1, 1, 0)
        near0, near1, keep, give = pl.pallas_call(
            near_kernel,
            out_shape=(sent, sent, kept, sent),
            in_specs=[vmem] * (2 + len(given)),
            out_specs=(vmem,) * 4,
            compiler_params=params(16),
            cost_estimate=cost,
            name="near",
        )(flux0, flux1, *given)

        def sum_of(far, add, *handed_on):
            return pl.pallas_call(
                add_kernel,
                out_shape=[sent] * (1 + len(handed_on)),
                in_specs=[vmem] * (2 + len(handed_on)),
                out_specs=[vmem] * (1 + len(handed_on)),
                compiler_params=params(16),
                name="add",
            )(far, add, *handed_on)

        near0 = swap(near0, 1, 0)
        sum0 = swap(sum_of(far0, add0)[0], 2, 0)
        sum1, near1, give = sum_of(far1, add1, near1, give)
        sum1, near1, give = swap(sum1, 2, 1), swap(near1, 1, 1), swap(give, 0, 1)
        return pl.pallas_call(
            lambda *refs: halving_sum_kernel(scale, *refs),
            out_shape=result,
            in_specs=[vmem] * 6,
            out_specs=vmem,
            compiler_params=params(16),
            name="total",
        )(keep, give, near0, near1, sum0, sum1)

    terms = pl.pallas_call(
        couple_kernel,
        out_shape=shape((2 * domains, block, half), BF16),
        in_specs=[vmem] * (2 + len(given)),
        out_specs=vmem,
        compiler_params=params(16),
        name="couple",
    )(flux_of(0), flux_of(1), *given)
    terms = lax.all_to_all(terms, ("dom", "dir"), split_axis=0, concat_axis=0, tiled=True)
    return pl.pallas_call(
        lambda *refs: sum_kernel(scale, *refs),
        out_shape=result,
        in_specs=[vmem],
        out_specs=vmem,
        compiler_params=params(),
        name="total",
    )(terms)


def solution(mesh):
    in_specs = (
        P("dom", ("panel", "blk")),
        P(None, None, "dom"),
        P("dir", None, "dom"),
        P(None, "dom"),
        P("dom"),
        P("dom"),
    )
    out_specs = P("dir", ("panel", "dom"), "blk")
    return jax.shard_map(
        per_device, mesh=mesh, in_specs=in_specs, out_specs=out_specs, check_vma=False
    )
```

```python
import functools

import jax
import jax.numpy as jnp
from jax import lax
from jax.experimental import pallas as pl
from jax.experimental.pallas import tpu as pltpu
from jax.sharding import PartitionSpec as P

GROUP = 16
BF16 = jnp.bfloat16
F32 = jnp.float32


def params(mib=24):
    return pltpu.CompilerParams(vmem_limit_bytes=mib * 1024 * 1024)


def dot(a, b, contract=((1,), (0,))):
    return lax.dot_general(a, b, (contract, ((), ())), preferred_element_type=F32)


def one_hot(mask):
    return jnp.where(mask, 1.0, 0.0).astype(BF16)


def my_columns(half):
    return pl.ds(pl.multiple_of(lax.axis_index("dir") * half, 128), half)


def prep_kernel(
    v_hbm, low_hbm, high_hbm, force_hbm, bond_hbm, near_hbm,
    turned_hbm, send_low_hbm, send_high_hbm, source_hbm, bond_out_hbm,
    v_ref, low_ref, high_ref, near_ref, turned_ref, send_low_ref, send_high_ref,
    source_ref, pick_ref, wide_ref, v_sems, in_sems, out_sems,
):
    rows, half = v_ref.shape
    atoms = rows // 3
    arriving = [
        pltpu.make_async_copy(source, target, in_sems.at[i])
        for i, (source, target) in enumerate(
            (
                (low_hbm, low_ref),
                (high_hbm, high_ref),
                (near_hbm, near_ref),
                (force_hbm, source_ref.at[0:9]),
                (bond_hbm, source_ref.at[9:10]),
            )
        )
    ]
    quarter = rows // 4
    v_in = [
        pltpu.make_async_copy(
            v_hbm.at[pl.ds(at, quarter), my_columns(half)], v_ref.at[pl.ds(at, quarter)], v_sems.at[i]
        )
        for i, at in enumerate(range(0, rows, quarter))
    ]
    for copy in arriving + v_in:
        copy.start()
    leaving = []

    def leave(ref, hbm):
        copy = pltpu.make_async_copy(ref, hbm, out_sems.at[len(leaving)])
        copy.start()
        leaving.append(copy)

    for copy in arriving:
        copy.wait()
    source_ref[10] = near_ref[...].astype(F32)
    leave(source_ref.at[9:10], bond_out_hbm)
    leave(source_ref, source_hbm)
    for i, list_ref in enumerate((high_ref, low_ref)):
        count = list_ref.shape[1]
        named = jnp.broadcast_to(list_ref[...], (128, count)).T
        lane = lax.broadcasted_iota(jnp.int32, (count, 128), 1)
        for b in range(3):
            wanted = 3 * named + b
            at = (3 * i + b) * count
            for t in range(rows // 128):
                pick_ref[at : at + count, t * 128 : (t + 1) * 128] = one_hot(
                    lane + t * 128 == wanted
                )
    for copy in v_in:
        copy.wait()
    for t in range(half // 128):
        columns = slice(t * 128, (t + 1) * 128)
        wide_ref[t] = v_ref[:, columns].astype(F32)
        for b in range(3):
            part = wide_ref[t, pl.ds(b, atoms, stride=3), :]
            turned_ref[columns, b * atoms : (b + 1) * atoms] = part.T.astype(BF16)
    leave(turned_ref, turned_hbm)
    picked = dot(pick_ref[...], v_ref[...]).astype(BF16)
    send_high_ref[...] = picked[: 3 * count]
    leave(send_high_ref, send_high_hbm)
    send_low_ref[...] = picked[3 * count :]
    leave(send_low_ref, send_low_hbm)
    for copy in leaving:
        copy.wait()


def weights_kernel(
    source_ref, other_ref, turned_ref,
    flux_ref, hi_ref, lo_ref, table_ref, own_hi_ref, own_lo_ref,
):
    _, steps, atoms = source_ref.shape
    groups = atoms // GROUP
    halo = hi_ref.shape[1] // 3
    extent = atoms + halo
    bonds = (source_ref[9], other_ref[0])
    lane = lax.broadcasted_iota(jnp.int32, (24, atoms), 1)
    rows = []
    for k in range(steps):
        force = source_ref[0:9, k, :]
        near = source_ref[10, k : k + 1, :]
        rows.append(
            jnp.concatenate(
                [force * bonds[0][k : k + 1, :], force * bonds[1][k : k + 1, :]]
                + [jnp.broadcast_to(near, (6, atoms))],
                axis=0,
            )
        )
    bit = 1
    while bit < steps:
        taken = ((lane // GROUP) & bit) != 0
        turned = list(rows)
        for p in range(steps):
            if p & bit:
                continue
            q = p | bit
            turned[p] = jnp.where(taken, pltpu.roll(rows[q], GROUP * bit, 1), rows[p])
            turned[q] = jnp.where(taken, rows[q], pltpu.roll(rows[p], atoms - GROUP * bit, 1))
        rows = turned
        bit *= 2
    for g in range(groups):
        table_ref[g] = rows[g]

    mask = (
        lax.broadcasted_iota(jnp.int32, (GROUP, atoms), 1) % GROUP
        == lax.broadcasted_iota(jnp.int32, (GROUP, atoms), 0)
    )
    target = lax.broadcasted_iota(jnp.int32, (256, atoms), 0).astype(F32).astype(BF16)

    def group(g):
        table = table_ref[g]
        named = [(table[18:19, :] - at).astype(BF16) for at in range(0, extent, 256)]
        hot = jnp.concatenate(
            [jnp.where(target == name, BF16(1), BF16(0)) for name in named], axis=0
        )
        spread = jnp.concatenate(
            [jnp.where(mask, table[r : r + 1, :], 0.0) for r in range(18)], axis=0
        )
        top = spread.astype(BF16)
        rest = (spread - top.astype(F32)).astype(BF16)
        both = ((1,), (1,))
        dense = dot(top, hot, both) + dot(rest, hot, both)
        hi = dense.astype(BF16)
        lo = (dense - hi.astype(F32)).astype(BF16)
        for e in range(2):
            for a in range(3):
                at = pl.ds(pl.multiple_of((e * 3 + a) * atoms + g * GROUP, GROUP), GROUP)
                for b in range(3):
                    r = (e * 9 + 3 * a + b) * GROUP
                    near, far = slice(b * atoms, (b + 1) * atoms), slice(b * halo, (b + 1) * halo)
                    own_hi_ref[at, near] = hi[r : r + GROUP, :atoms]
                    own_lo_ref[at, near] = lo[r : r + GROUP, :atoms]
                    hi_ref[at, far] = hi[r : r + GROUP, atoms:]
                    lo_ref[at, far] = lo[r : r + GROUP, atoms:]

    def several(step, carry):
        for g in range(4):
            group(4 * step + g)
        return carry

    lax.fori_loop(0, groups // 4, several, 0)
    turned = turned_ref[...]
    for e in range(2):
        at = slice(3 * e * atoms, 3 * (e + 1) * atoms)
        hi, lo = own_hi_ref[at, :], own_lo_ref[at, :]
        flux_ref[at, :] = dot(hi, turned, ((1,), (1,))) + dot(lo, turned, ((1,), (1,)))


def relay_kernel(part_hbm, below_hbm, above_hbm, *refs):
    for got_ref, given_ref in zip(refs[: len(refs) // 2], refs[len(refs) // 2 :]):
        given_ref[...] = got_ref[...]


def flux_kernel(e, part_ref, hi_ref, lo_ref, below_ref, above_ref, flux_ref, halo_ref):
    count = below_ref.shape[0] // 3
    for b in range(3):
        at = 2 * b * count
        halo_ref[at : at + count] = below_ref[b * count : (b + 1) * count]
        halo_ref[at + count : at + 2 * count] = above_ref[b * count : (b + 1) * count]
    atoms = flux_ref.shape[0] // 3
    halo = halo_ref[...]
    at = slice(3 * e * atoms, 3 * (e + 1) * atoms)
    flux = part_ref[at, :] + (dot(hi_ref[at, :], halo) + dot(lo_ref[at, :], halo))
    flux_ref[...] = flux.astype(BF16)


def terms_of(quarter_refs, store):
    tiles = len(quarter_refs) // 2
    me, core = lax.axis_index("blk"), lax.axis_index("dir")
    for j in range(tiles):
        tile = lax.rem(me - j + tiles, tiles)
        for s in range(2):
            store(2 * tile + (core if s == 0 else 1 - core), quarter_refs[2 * j + s])


def couple_kernel(flux0_ref, flux1_ref, *refs):
    *quarter_refs, out_ref = refs
    half = quarter_refs[0].shape[0]
    block = out_ref.shape[1]
    core = lax.axis_index("dir")

    def store(quarter, turned_ref):
        for e, flux_ref in enumerate((flux0_ref, flux1_ref)):
            term = dot(turned_ref[...], flux_ref[...]).astype(BF16)
            for t in range(half // block):
                at = 2 * (quarter * (half // block) + t) + (core if e == 0 else 1 - core)
                out_ref[at] = term[t * block : (t + 1) * block]

    terms_of(quarter_refs, store)


def sum_kernel(scale, terms_ref, out_ref):
    pairs, block, half = terms_ref.shape
    for c in range(2):
        total = terms_ref[c].astype(F32)
        for d in range(1, pairs // 2):
            total = total + terms_ref[2 * d + c].astype(F32)
        out_ref[0, :, c * half : (c + 1) * half] = total * scale


def far_kernel(after, flux_ref, *refs):
    *quarter_refs, far_ref = refs
    home = lax.axis_index("dom")

    def store(quarter, turned_ref):
        @pl.when((quarter ^ home) == 3)
        def _():
            far_ref[...] = dot(turned_ref[...], flux_ref[...]).astype(BF16)

    terms_of(quarter_refs, store)


def near_kernel(flux0_ref, flux1_ref, *refs):
    *quarter_refs, near0_ref, near1_ref, add0_ref, add1_ref, keep_ref, give_ref = refs
    home = lax.axis_index("dom")
    outs = {0: (keep_ref, give_ref), 1: (near0_ref, near1_ref), 2: (add0_ref, add1_ref)}

    def store(quarter, turned_ref):
        for away, out_refs in outs.items():

            @pl.when((quarter ^ home) == away)
            def _():
                for flux_ref, out_ref in zip((flux0_ref, flux1_ref), out_refs):
                    out_ref[...] = dot(turned_ref[...], flux_ref[...]).astype(out_ref.dtype)

    terms_of(quarter_refs, store)


def add_kernel(far_ref, add_ref, *refs):
    held_refs, (sum_ref, *given_refs) = refs[: len(refs) // 2], refs[len(refs) // 2 :]
    sum_ref[...] = (add_ref[...] + far_ref[...].astype(F32)).astype(BF16)
    for held_ref, given_ref in zip(held_refs, given_refs):
        given_ref[...] = held_ref[...]


def halving_sum_kernel(
    scale, keep_ref, give_ref, near0_ref, near1_ref, sum0_ref, sum1_ref, out_hbm, total_ref, sems
):
    half = keep_ref.shape[1]
    core = lax.axis_index("dir")
    copies = []
    for i, (owner, first, near, far) in enumerate(
        ((core, keep_ref, near0_ref, sum0_ref), (1 - core, give_ref, near1_ref, sum1_ref))
    ):
        total = first[...].astype(F32) + near[...].astype(F32) + far[...].astype(F32)
        total_ref[i] = total * scale
        columns = pl.ds(pl.multiple_of(owner * half, 128), half)
        copies.append(
            pltpu.make_async_copy(total_ref.at[i], out_hbm.at[0, :, columns], sems.at[i])
        )
        copies[i].start()
    for copy in copies:
        copy.wait()


def shift(value, axis, by):
    length = lax.axis_size(axis)
    return lax.ppermute(value, axis, [(i, (i + by) % length) for i in range(length)])


def swap(value, away, other_core):
    domains = lax.axis_size("dom")
    pairs = [
        (2 * d + c, 2 * (d ^ away) + (c ^ other_core)) for d in range(domains) for c in range(2)
    ]
    return lax.ppermute(value, ("dom", "dir"), pairs)


def shape(dims, dtype):
    return jax.ShapeDtypeStruct(dims, dtype)


def per_device(panel_vectors, force_blocks, bond_vectors, neighbours, boundary_low, boundary_high):
    rows, cols = panel_vectors.shape
    atoms = rows // 3
    half = cols // 2
    count = boundary_low.shape[0]
    domains, tiles = lax.axis_size("dom"), lax.axis_size("blk")
    block = cols * tiles // domains
    vmem = pl.BlockSpec(memory_space=pltpu.VMEM)
    hbm = pl.BlockSpec(memory_space=pltpu.HBM)
    anywhere = pl.BlockSpec(memory_space=pl.ANY)

    lists = [boundary_low.reshape(1, count), boundary_high.reshape(1, count)]
    forces = force_blocks.transpose(1, 0, 2)
    prepared = (
        shape((half, rows), BF16),
        shape((3 * count, half), BF16),
        shape((3 * count, half), BF16),
    )
    turned, send_low, send_high, sources, bonds = pl.pallas_call(
        prep_kernel,
        out_shape=(
            *prepared,
            shape((11, *neighbours.shape), F32),
            shape(bond_vectors.shape, F32),
        ),
        in_specs=[hbm] * 6,
        out_specs=(hbm,) * 5,
        scratch_shapes=[
            pltpu.VMEM((rows, half), BF16),
            pltpu.VMEM((1, count), jnp.int32),
            pltpu.VMEM((1, count), jnp.int32),
            pltpu.VMEM(neighbours.shape, jnp.int32),
            *[pltpu.VMEM(like.shape, like.dtype) for like in prepared],
            pltpu.VMEM((11, *neighbours.shape), F32),
            pltpu.VMEM((6 * count, rows), BF16),
            pltpu.VMEM((half // 128, rows, 128), F32),
            pltpu.SemaphoreType.DMA((4,)),
            pltpu.SemaphoreType.DMA((5,)),
            pltpu.SemaphoreType.DMA((5,)),
        ],
        compiler_params=params(58),
        name="prep",
    )(panel_vectors, *lists, forces, bond_vectors, neighbours)
    quarters = [shift(turned, "blk", j) for j in range(1, tiles)]
    turned_other = shift(turned, "dir", 1)
    other_bonds = shift(bonds, "dir", 1)
    below = shift(send_high, "dom", 1)
    above = shift(send_low, "dom", -1)

    partial_flux, hi, lo = pl.pallas_call(
        weights_kernel,
        out_shape=(
            shape((2 * rows, half), F32),
            shape((2 * rows, 6 * count), BF16),
            shape((2 * rows, 6 * count), BF16),
        ),
        in_specs=[vmem] * 3,
        out_specs=(vmem,) * 3,
        scratch_shapes=[
            pltpu.VMEM((atoms // GROUP, 24, atoms), F32),
            pltpu.VMEM((2 * rows, rows), BF16),
            pltpu.VMEM((2 * rows, rows), BF16),
        ],
        compiler_params=params(32),
        cost_estimate=pl.CostEstimate(
            flops=8*10**9, bytes_accessed=10**7, transcendentals=0
        ),
        name="weights",
    )(sources, other_bonds, turned)

    quarters = pl.pallas_call(
        relay_kernel,
        out_shape=[shape(turned.shape, BF16)] * (tiles - 1),
        in_specs=[anywhere] * 3 + [vmem] * len(quarters),
        out_specs=[vmem] * (tiles - 1),
        compiler_params=params(16),
        name="relay",
    )(partial_flux, below, above, *quarters)
    given = [turned, turned_other]
    for quarter in quarters:
        given += [quarter, shift(quarter, "dir", 1)]

    def flux_of(e):
        return pl.pallas_call(
            functools.partial(flux_kernel, e),
            out_shape=shape((rows, half), BF16),
            in_specs=[vmem] * 5,
            out_specs=vmem,
            scratch_shapes=[pltpu.VMEM((6 * count, half), BF16)],
            compiler_params=params(16),
            cost_estimate=pl.CostEstimate(
                flops=10**9, bytes_accessed=10**6, transcendentals=0
            ),
            name="flux",
        )(partial_flux, hi, lo, below, above)

    scale = (3.0 * atoms * domains) ** (-0.5)
    result = shape((1, block, cols), F32)
    if domains == 4 and block == half:
        sent, kept = shape((block, half), BF16), shape((block, half), F32)
        cost = pl.CostEstimate(flops=4 * 10**8, bytes_accessed=10**6, transcendentals=0)

        def far_of(flux, after):
            return pl.pallas_call(
                far_kernel,
                out_shape=sent,
                in_specs=[anywhere] + [vmem] * (1 + len(given)),
                out_specs=vmem,
                compiler_params=params(16),
                cost_estimate=cost,
                name="far",
            )(after, flux, *given)

        flux0, flux1 = flux_of(0), flux_of(1)
        far0 = far_of(flux0, flux1)
        far1 = far_of(flux1, far0)
        far0, far1 = swap(far0, 1, 0), swap(far1, 1, 0)
        near0, near1, add0, add1, keep, give = pl.pallas_call(
            near_kernel,
            out_shape=(sent, sent, kept, kept, kept, sent),
            in_specs=[vmem] * (2 + len(given)),
            out_specs=(vmem,) * 6,
            compiler_params=params(16),
            cost_estimate=cost,
            name="near",
        )(flux0, flux1, *given)

        def sum_of(far, add, *handed_on):
            return pl.pallas_call(
                add_kernel,
                out_shape=[sent] * (1 + len(handed_on)),
                in_specs=[vmem] * (2 + len(handed_on)),
                out_specs=[vmem] * (1 + len(handed_on)),
                compiler_params=params(16),
                name="add",
            )(far, add, *handed_on)

        near0 = swap(near0, 1, 0)
        sum0 = swap(sum_of(far0, add0)[0], 2, 0)
        sum1, near1, give = sum_of(far1, add1, near1, give)
        sum1, near1, give = swap(sum1, 2, 1), swap(near1, 1, 1), swap(give, 0, 1)
        return pl.pallas_call(
            lambda *refs: halving_sum_kernel(scale, *refs),
            out_shape=result,
            in_specs=[vmem] * 6,
            out_specs=hbm,
            scratch_shapes=[
                pltpu.VMEM((2, block, half), F32),
                pltpu.SemaphoreType.DMA((2,)),
            ],
            compiler_params=params(16),
            name="total",
        )(keep, give, near0, near1, sum0, sum1)

    terms = pl.pallas_call(
        couple_kernel,
        out_shape=shape((2 * domains, block, half), BF16),
        in_specs=[vmem] * (2 + len(given)),
        out_specs=vmem,
        compiler_params=params(16),
        name="couple",
    )(flux_of(0), flux_of(1), *given)
    terms = lax.all_to_all(terms, ("dom", "dir"), split_axis=0, concat_axis=0, tiled=True)
    return pl.pallas_call(
        lambda *refs: sum_kernel(scale, *refs),
        out_shape=result,
        in_specs=[vmem],
        out_specs=vmem,
        compiler_params=params(),
        name="total",
    )(terms)


def solution(mesh):
    in_specs = (
        P("dom", ("panel", "blk")),
        P(None, None, "dom"),
        P("dir", None, "dom"),
        P(None, "dom"),
        P("dom"),
        P("dom"),
    )
    out_specs = P("dir", ("panel", "dom"), "blk")
    return jax.shard_map(
        per_device, mesh=mesh, in_specs=in_specs, out_specs=out_specs, check_vma=False
    )
```

```python
import functools

import jax
import jax.numpy as jnp
from jax import lax
from jax.experimental import pallas as pl
from jax.experimental.pallas import tpu as pltpu
from jax.sharding import PartitionSpec as P

PIECES = 2
GROUP = 16
BF16 = jnp.bfloat16
F32 = jnp.float32


def params(mib=24):
    return pltpu.CompilerParams(vmem_limit_bytes=mib * 1024 * 1024)


def dot(a, b, contract=((1,), (0,))):
    return lax.dot_general(a, b, (contract, ((), ())), preferred_element_type=F32)


def one_hot(mask):
    return jnp.where(mask, 1.0, 0.0).astype(BF16)


def my_columns(half):
    return pl.ds(pl.multiple_of(lax.axis_index("dir") * half, 128), half)


def prep_kernel(
    v_hbm, low_hbm, high_hbm, force_hbm, bond_hbm, near_hbm,
    turned_hbm, send_low_hbm, send_high_hbm, source_hbm, bond_out_hbm, *refs
):
    piece_hbms, scratch_refs = refs[:PIECES], refs[PIECES:]
    v_ref, low_ref, high_ref, near_ref, turned_ref, send_low_ref, send_high_ref = scratch_refs[:7]
    source_ref, pick_ref, wide_ref, v_sems, in_sems, out_sems = scratch_refs[7:]
    rows, half = v_ref.shape
    atoms = rows // 3
    arriving = [
        pltpu.make_async_copy(source, target, in_sems.at[i])
        for i, (source, target) in enumerate(
            (
                (low_hbm, low_ref),
                (high_hbm, high_ref),
                (near_hbm, near_ref),
                (force_hbm, source_ref.at[0:9]),
                (bond_hbm, source_ref.at[9:10]),
            )
        )
    ]
    quarter = rows // 4
    v_in = [
        pltpu.make_async_copy(
            v_hbm.at[pl.ds(at, quarter), my_columns(half)], v_ref.at[pl.ds(at, quarter)], v_sems.at[i]
        )
        for i, at in enumerate(range(0, rows, quarter))
    ]
    for copy in arriving + v_in:
        copy.start()
    leaving = []

    def leave(ref, hbm):
        copy = pltpu.make_async_copy(ref, hbm, out_sems.at[len(leaving)])
        copy.start()
        leaving.append(copy)

    for copy in arriving:
        copy.wait()
    source_ref[10] = near_ref[...].astype(F32)
    leave(source_ref.at[9:10], bond_out_hbm)
    leave(source_ref, source_hbm)
    for i, list_ref in enumerate((high_ref, low_ref)):
        count = list_ref.shape[1]
        named = jnp.broadcast_to(list_ref[...], (128, count)).T
        lane = lax.broadcasted_iota(jnp.int32, (count, 128), 1)
        for b in range(3):
            wanted = 3 * named + b
            at = (3 * i + b) * count
            for t in range(rows // 128):
                pick_ref[at : at + count, t * 128 : (t + 1) * 128] = one_hot(
                    lane + t * 128 == wanted
                )
    for copy in v_in:
        copy.wait()
    for t in range(half // 128):
        columns = slice(t * 128, (t + 1) * 128)
        wide_ref[t] = v_ref[:, columns].astype(F32)
        for b in range(3):
            part = wide_ref[t, pl.ds(b, atoms, stride=3), :]
            turned_ref[columns, b * atoms : (b + 1) * atoms] = part.T.astype(BF16)
    leave(turned_ref, turned_hbm)
    for i, piece_hbm in enumerate(piece_hbms):
        length = piece_hbm.shape[0]
        leave(turned_ref.at[pl.ds(i * length, length)], piece_hbm)
    picked = dot(pick_ref[...], v_ref[...]).astype(BF16)
    send_high_ref[...] = picked[: 3 * count]
    leave(send_high_ref, send_high_hbm)
    send_low_ref[...] = picked[3 * count :]
    leave(send_low_ref, send_low_hbm)
    for copy in leaving:
        copy.wait()


def weights_kernel(
    source_ref, other_ref, turned_ref,
    flux_ref, hi_ref, lo_ref, table_ref, own_hi_ref, own_lo_ref,
):
    _, steps, atoms = source_ref.shape
    groups = atoms // GROUP
    halo = hi_ref.shape[1] // 3
    extent = atoms + halo
    bonds = (source_ref[9], other_ref[0])
    lane = lax.broadcasted_iota(jnp.int32, (24, atoms), 1)
    rows = []
    for k in range(steps):
        force = source_ref[0:9, k, :]
        near = source_ref[10, k : k + 1, :]
        rows.append(
            jnp.concatenate(
                [force * bonds[0][k : k + 1, :], force * bonds[1][k : k + 1, :]]
                + [jnp.broadcast_to(near, (6, atoms))],
                axis=0,
            )
        )
    bit = 1
    while bit < steps:
        taken = ((lane // GROUP) & bit) != 0
        turned = list(rows)
        for p in range(steps):
            if p & bit:
                continue
            q = p | bit
            turned[p] = jnp.where(taken, pltpu.roll(rows[q], GROUP * bit, 1), rows[p])
            turned[q] = jnp.where(taken, rows[q], pltpu.roll(rows[p], atoms - GROUP * bit, 1))
        rows = turned
        bit *= 2
    for g in range(groups):
        table_ref[g] = rows[g]

    mask = (
        lax.broadcasted_iota(jnp.int32, (GROUP, atoms), 1) % GROUP
        == lax.broadcasted_iota(jnp.int32, (GROUP, atoms), 0)
    )
    target = lax.broadcasted_iota(jnp.int32, (256, atoms), 0).astype(F32).astype(BF16)

    def group(g):
        table = table_ref[g]
        named = [(table[18:19, :] - at).astype(BF16) for at in range(0, extent, 256)]
        hot = jnp.concatenate(
            [jnp.where(target == name, BF16(1), BF16(0)) for name in named], axis=0
        )
        spread = jnp.concatenate(
            [jnp.where(mask, table[r : r + 1, :], 0.0) for r in range(18)], axis=0
        )
        top = spread.astype(BF16)
        rest = (spread - top.astype(F32)).astype(BF16)
        both = ((1,), (1,))
        dense = dot(top, hot, both) + dot(rest, hot, both)
        hi = dense.astype(BF16)
        lo = (dense - hi.astype(F32)).astype(BF16)
        for e in range(2):
            for a in range(3):
                at = pl.ds(pl.multiple_of((e * 3 + a) * atoms + g * GROUP, GROUP), GROUP)
                for b in range(3):
                    r = (e * 9 + 3 * a + b) * GROUP
                    near, far = slice(b * atoms, (b + 1) * atoms), slice(b * halo, (b + 1) * halo)
                    own_hi_ref[at, near] = hi[r : r + GROUP, :atoms]
                    own_lo_ref[at, near] = lo[r : r + GROUP, :atoms]
                    hi_ref[at, far] = hi[r : r + GROUP, atoms:]
                    lo_ref[at, far] = lo[r : r + GROUP, atoms:]

    def several(step, carry):
        for g in range(4):
            group(4 * step + g)
        return carry

    lax.fori_loop(0, groups // 4, several, 0)
    turned = turned_ref[...]
    for e in range(2):
        at = slice(3 * e * atoms, 3 * (e + 1) * atoms)
        hi, lo = own_hi_ref[at, :], own_lo_ref[at, :]
        flux_ref[at, :] = dot(hi, turned, ((1,), (1,))) + dot(lo, turned, ((1,), (1,)))


def relay_kernel(part_hbm, below_hbm, above_hbm, *refs):
    quarters = len(refs) // (PIECES + 1)
    for t, given_ref in enumerate(refs[quarters * PIECES :]):
        length = given_ref.shape[0] // PIECES
        for i in range(PIECES):
            given_ref[i * length : (i + 1) * length] = refs[t * PIECES + i][...]


def flux_kernel(e, part_ref, hi_ref, lo_ref, below_ref, above_ref, flux_ref, halo_ref):
    count = below_ref.shape[0] // 3
    for b in range(3):
        at = 2 * b * count
        halo_ref[at : at + count] = below_ref[b * count : (b + 1) * count]
        halo_ref[at + count : at + 2 * count] = above_ref[b * count : (b + 1) * count]
    atoms = flux_ref.shape[0] // 3
    halo = halo_ref[...]
    at = slice(3 * e * atoms, 3 * (e + 1) * atoms)
    flux = part_ref[at, :] + (dot(hi_ref[at, :], halo) + dot(lo_ref[at, :], halo))
    flux_ref[...] = flux.astype(BF16)


def terms_of(quarter_refs, store):
    tiles = len(quarter_refs) // 2
    me, core = lax.axis_index("blk"), lax.axis_index("dir")
    for j in range(tiles):
        tile = lax.rem(me - j + tiles, tiles)
        for s in range(2):
            store(2 * tile + (core if s == 0 else 1 - core), quarter_refs[2 * j + s])


def couple_kernel(flux0_ref, flux1_ref, *refs):
    *quarter_refs, out_ref = refs
    half = quarter_refs[0].shape[0]
    block = out_ref.shape[1]
    core = lax.axis_index("dir")

    def store(quarter, turned_ref):
        for e, flux_ref in enumerate((flux0_ref, flux1_ref)):
            term = dot(turned_ref[...], flux_ref[...]).astype(BF16)
            for t in range(half // block):
                at = 2 * (quarter * (half // block) + t) + (core if e == 0 else 1 - core)
                out_ref[at] = term[t * block : (t + 1) * block]

    terms_of(quarter_refs, store)


def sum_kernel(scale, terms_ref, out_ref):
    pairs, block, half = terms_ref.shape
    for c in range(2):
        total = terms_ref[c].astype(F32)
        for d in range(1, pairs // 2):
            total = total + terms_ref[2 * d + c].astype(F32)
        out_ref[0, :, c * half : (c + 1) * half] = total * scale


def far_kernel(after, flux_ref, *refs):
    *quarter_refs, far_ref = refs
    home = lax.axis_index("dom")

    def store(quarter, turned_ref):
        @pl.when((quarter ^ home) == 3)
        def _():
            far_ref[...] = dot(turned_ref[...], flux_ref[...]).astype(BF16)

    terms_of(quarter_refs, store)


def near_kernel(flux0_ref, flux1_ref, *refs):
    *quarter_refs, near0_ref, near1_ref, add0_ref, add1_ref, keep_ref, give_ref = refs
    home = lax.axis_index("dom")
    outs = {0: (keep_ref, give_ref), 1: (near0_ref, near1_ref), 2: (add0_ref, add1_ref)}

    def store(quarter, turned_ref):
        for away, out_refs in outs.items():

            @pl.when((quarter ^ home) == away)
            def _():
                for flux_ref, out_ref in zip((flux0_ref, flux1_ref), out_refs):
                    out_ref[...] = dot(turned_ref[...], flux_ref[...]).astype(out_ref.dtype)

    terms_of(quarter_refs, store)


def add_kernel(far_ref, add_ref, *refs):
    held_refs, (sum_ref, *given_refs) = refs[: len(refs) // 2], refs[len(refs) // 2 :]
    sum_ref[...] = (add_ref[...] + far_ref[...].astype(F32)).astype(BF16)
    for held_ref, given_ref in zip(held_refs, given_refs):
        given_ref[...] = held_ref[...]


def halving_sum_kernel(
    scale, keep_ref, give_ref, near0_ref, near1_ref, sum0_ref, sum1_ref, out_hbm, total_ref, sems
):
    half = keep_ref.shape[1]
    core = lax.axis_index("dir")
    copies = []
    for i, (owner, first, near, far) in enumerate(
        ((core, keep_ref, near0_ref, sum0_ref), (1 - core, give_ref, near1_ref, sum1_ref))
    ):
        total = first[...].astype(F32) + near[...].astype(F32) + far[...].astype(F32)
        total_ref[i] = total * scale
        columns = pl.ds(pl.multiple_of(owner * half, 128), half)
        copies.append(
            pltpu.make_async_copy(total_ref.at[i], out_hbm.at[0, :, columns], sems.at[i])
        )
        copies[i].start()
    for copy in copies:
        copy.wait()


def shift(value, axis, by):
    length = lax.axis_size(axis)
    return lax.ppermute(value, axis, [(i, (i + by) % length) for i in range(length)])


def swap(value, away, other_core):
    domains = lax.axis_size("dom")
    pairs = [
        (2 * d + c, 2 * (d ^ away) + (c ^ other_core)) for d in range(domains) for c in range(2)
    ]
    return lax.ppermute(value, ("dom", "dir"), pairs)


def shape(dims, dtype):
    return jax.ShapeDtypeStruct(dims, dtype)


def per_device(panel_vectors, force_blocks, bond_vectors, neighbours, boundary_low, boundary_high):
    rows, cols = panel_vectors.shape
    atoms = rows // 3
    half = cols // 2
    count = boundary_low.shape[0]
    domains, tiles = lax.axis_size("dom"), lax.axis_size("blk")
    block = cols * tiles // domains
    vmem = pl.BlockSpec(memory_space=pltpu.VMEM)
    hbm = pl.BlockSpec(memory_space=pltpu.HBM)
    anywhere = pl.BlockSpec(memory_space=pl.ANY)

    lists = [boundary_low.reshape(1, count), boundary_high.reshape(1, count)]
    forces = force_blocks.transpose(1, 0, 2)
    prepared = (
        shape((half, rows), BF16),
        shape((3 * count, half), BF16),
        shape((3 * count, half), BF16),
    )
    turned, send_low, send_high, sources, bonds, *pieces = pl.pallas_call(
        prep_kernel,
        out_shape=(
            *prepared,
            shape((11, *neighbours.shape), F32),
            shape(bond_vectors.shape, F32),
        )
        + (shape((half // PIECES, rows), BF16),) * PIECES,
        in_specs=[hbm] * 6,
        out_specs=(hbm,) * (5 + PIECES),
        scratch_shapes=[
            pltpu.VMEM((rows, half), BF16),
            pltpu.VMEM((1, count), jnp.int32),
            pltpu.VMEM((1, count), jnp.int32),
            pltpu.VMEM(neighbours.shape, jnp.int32),
            *[pltpu.VMEM(like.shape, like.dtype) for like in prepared],
            pltpu.VMEM((11, *neighbours.shape), F32),
            pltpu.VMEM((6 * count, rows), BF16),
            pltpu.VMEM((half // 128, rows, 128), F32),
            pltpu.SemaphoreType.DMA((4,)),
            pltpu.SemaphoreType.DMA((5,)),
            pltpu.SemaphoreType.DMA((5 + PIECES,)),
        ],
        compiler_params=params(58),
        name="prep",
    )(panel_vectors, *lists, forces, bond_vectors, neighbours)
    quarters = [shift(piece, "blk", j) for j in range(1, tiles) for piece in pieces]
    turned_other = shift(turned, "dir", 1)
    other_bonds = shift(bonds, "dir", 1)
    below = shift(send_high, "dom", 1)
    above = shift(send_low, "dom", -1)

    partial_flux, hi, lo = pl.pallas_call(
        weights_kernel,
        out_shape=(
            shape((2 * rows, half), F32),
            shape((2 * rows, 6 * count), BF16),
            shape((2 * rows, 6 * count), BF16),
        ),
        in_specs=[vmem] * 3,
        out_specs=(vmem,) * 3,
        scratch_shapes=[
            pltpu.VMEM((atoms // GROUP, 24, atoms), F32),
            pltpu.VMEM((2 * rows, rows), BF16),
            pltpu.VMEM((2 * rows, rows), BF16),
        ],
        compiler_params=params(32),
        cost_estimate=pl.CostEstimate(
            flops=8*10**9, bytes_accessed=10**7, transcendentals=0
        ),
        name="weights",
    )(sources, other_bonds, turned)

    quarters = pl.pallas_call(
        relay_kernel,
        out_shape=[shape(turned.shape, BF16)] * (tiles - 1),
        in_specs=[anywhere] * 3 + [vmem] * len(quarters),
        out_specs=[vmem] * (tiles - 1),
        compiler_params=params(16),
        name="relay",
    )(partial_flux, below, above, *quarters)
    given = [turned, turned_other]
    for quarter in quarters:
        given += [quarter, shift(quarter, "dir", 1)]

    def flux_of(e):
        return pl.pallas_call(
            functools.partial(flux_kernel, e),
            out_shape=shape((rows, half), BF16),
            in_specs=[vmem] * 5,
            out_specs=vmem,
            scratch_shapes=[pltpu.VMEM((6 * count, half), BF16)],
            compiler_params=params(16),
            cost_estimate=pl.CostEstimate(
                flops=10**9, bytes_accessed=10**6, transcendentals=0
            ),
            name="flux",
        )(partial_flux, hi, lo, below, above)

    scale = (3.0 * atoms * domains) ** (-0.5)
    result = shape((1, block, cols), F32)
    if domains == 4 and block == half:
        sent, kept = shape((block, half), BF16), shape((block, half), F32)
        cost = pl.CostEstimate(flops=4 * 10**8, bytes_accessed=10**6, transcendentals=0)

        def far_of(flux, after):
            return pl.pallas_call(
                far_kernel,
                out_shape=sent,
                in_specs=[anywhere] + [vmem] * (1 + len(given)),
                out_specs=vmem,
                compiler_params=params(16),
                cost_estimate=cost,
                name="far",
            )(after, flux, *given)

        flux0, flux1 = flux_of(0), flux_of(1)
        far0 = far_of(flux0, flux1)
        far1 = far_of(flux1, far0)
        far0, far1 = swap(far0, 1, 0), swap(far1, 1, 0)
        near0, near1, add0, add1, keep, give = pl.pallas_call(
            near_kernel,
            out_shape=(sent, sent, kept, kept, kept, sent),
            in_specs=[vmem] * (2 + len(given)),
            out_specs=(vmem,) * 6,
            compiler_params=params(16),
            cost_estimate=cost,
            name="near",
        )(flux0, flux1, *given)

        def sum_of(far, add, *handed_on):
            return pl.pallas_call(
                add_kernel,
                out_shape=[sent] * (1 + len(handed_on)),
                in_specs=[vmem] * (2 + len(handed_on)),
                out_specs=[vmem] * (1 + len(handed_on)),
                compiler_params=params(16),
                name="add",
            )(far, add, *handed_on)

        near0 = swap(near0, 1, 0)
        sum0 = swap(sum_of(far0, add0)[0], 2, 0)
        sum1, near1, give = sum_of(far1, add1, near1, give)
        sum1, near1, give = swap(sum1, 2, 1), swap(near1, 1, 1), swap(give, 0, 1)
        return pl.pallas_call(
            lambda *refs: halving_sum_kernel(scale, *refs),
            out_shape=result,
            in_specs=[vmem] * 6,
            out_specs=hbm,
            scratch_shapes=[
                pltpu.VMEM((2, block, half), F32),
                pltpu.SemaphoreType.DMA((2,)),
            ],
            compiler_params=params(16),
            name="total",
        )(keep, give, near0, near1, sum0, sum1)

    terms = pl.pallas_call(
        couple_kernel,
        out_shape=shape((2 * domains, block, half), BF16),
        in_specs=[vmem] * (2 + len(given)),
        out_specs=vmem,
        compiler_params=params(16),
        name="couple",
    )(flux_of(0), flux_of(1), *given)
    terms = lax.all_to_all(terms, ("dom", "dir"), split_axis=0, concat_axis=0, tiled=True)
    return pl.pallas_call(
        lambda *refs: sum_kernel(scale, *refs),
        out_shape=result,
        in_specs=[vmem],
        out_specs=vmem,
        compiler_params=params(),
        name="total",
    )(terms)


def solution(mesh):
    in_specs = (
        P("dom", ("panel", "blk")),
        P(None, None, "dom"),
        P("dir", None, "dom"),
        P(None, "dom"),
        P("dom"),
        P("dom"),
    )
    out_specs = P("dir", ("panel", "dom"), "blk")
    return jax.shard_map(
        per_device, mesh=mesh, in_specs=in_specs, out_specs=out_specs, check_vma=False
    )
```

```python
import functools

import jax
import jax.numpy as jnp
from jax import lax
from jax.experimental import pallas as pl
from jax.experimental.pallas import tpu as pltpu
from jax.sharding import PartitionSpec as P

GROUP = 16
BF16 = jnp.bfloat16
F32 = jnp.float32


def params(mib=24):
    return pltpu.CompilerParams(vmem_limit_bytes=mib * 1024 * 1024)


def dot(a, b, contract=((1,), (0,))):
    return lax.dot_general(a, b, (contract, ((), ())), preferred_element_type=F32)


def one_hot(mask):
    return jnp.where(mask, 1.0, 0.0).astype(BF16)


def my_columns(half):
    return pl.ds(pl.multiple_of(lax.axis_index("dir") * half, 128), half)


def prep_kernel(
    v_hbm, low_hbm, high_hbm, force_hbm, bond_hbm, near_hbm,
    turned_hbm, send_low_hbm, send_high_hbm, source_hbm, bond_out_hbm,
    v_ref, low_ref, high_ref, near_ref, turned_ref, send_low_ref, send_high_ref,
    source_ref, pick_ref, wide_ref, v_sems, in_sems, out_sems,
):
    rows, half = v_ref.shape
    atoms = rows // 3
    arriving = [
        pltpu.make_async_copy(source, target, in_sems.at[i])
        for i, (source, target) in enumerate(
            (
                (low_hbm, low_ref),
                (high_hbm, high_ref),
                (near_hbm, near_ref),
                (force_hbm, source_ref.at[0:9]),
                (bond_hbm, source_ref.at[9:10]),
            )
        )
    ]
    quarter = rows // 4
    v_in = [
        pltpu.make_async_copy(
            v_hbm.at[pl.ds(at, quarter), my_columns(half)], v_ref.at[pl.ds(at, quarter)], v_sems.at[i]
        )
        for i, at in enumerate(range(0, rows, quarter))
    ]
    for copy in arriving + v_in:
        copy.start()
    leaving = []

    def leave(ref, hbm):
        copy = pltpu.make_async_copy(ref, hbm, out_sems.at[len(leaving)])
        copy.start()
        leaving.append(copy)

    for copy in arriving:
        copy.wait()
    source_ref[10] = near_ref[...].astype(F32)
    leave(source_ref.at[9:10], bond_out_hbm)
    leave(source_ref, source_hbm)
    for i, list_ref in enumerate((high_ref, low_ref)):
        count = list_ref.shape[1]
        named = jnp.broadcast_to(list_ref[...], (128, count)).T
        lane = lax.broadcasted_iota(jnp.int32, (count, 128), 1)
        for b in range(3):
            wanted = 3 * named + b
            at = (3 * i + b) * count
            for t in range(rows // 128):
                pick_ref[at : at + count, t * 128 : (t + 1) * 128] = one_hot(
                    lane + t * 128 == wanted
                )
    for copy in v_in:
        copy.wait()
    for t in range(half // 128):
        columns = slice(t * 128, (t + 1) * 128)
        wide_ref[t] = v_ref[:, columns].astype(F32)
        for b in range(3):
            part = wide_ref[t, pl.ds(b, atoms, stride=3), :]
            turned_ref[columns, b * atoms : (b + 1) * atoms] = part.T.astype(BF16)
    leave(turned_ref, turned_hbm)
    picked = dot(pick_ref[...], v_ref[...]).astype(BF16)
    send_high_ref[...] = picked[: 3 * count]
    leave(send_high_ref, send_high_hbm)
    send_low_ref[...] = picked[3 * count :]
    leave(send_low_ref, send_low_hbm)
    for copy in leaving:
        copy.wait()


def weights_kernel(
    source_ref, other_ref, turned_ref,
    flux_ref, hi_ref, lo_ref, table_ref, own_hi_ref, own_lo_ref,
):
    _, steps, atoms = source_ref.shape
    groups = atoms // GROUP
    halo = hi_ref.shape[1] // 3
    extent = atoms + halo
    bonds = (source_ref[9], other_ref[0])
    lane = lax.broadcasted_iota(jnp.int32, (24, atoms), 1)
    rows = []
    for k in range(steps):
        force = source_ref[0:9, k, :]
        near = source_ref[10, k : k + 1, :]
        rows.append(
            jnp.concatenate(
                [force * bonds[0][k : k + 1, :], force * bonds[1][k : k + 1, :]]
                + [jnp.broadcast_to(near, (6, atoms))],
                axis=0,
            )
        )
    bit = 1
    while bit < steps:
        taken = ((lane // GROUP) & bit) != 0
        turned = list(rows)
        for p in range(steps):
            if p & bit:
                continue
            q = p | bit
            turned[p] = jnp.where(taken, pltpu.roll(rows[q], GROUP * bit, 1), rows[p])
            turned[q] = jnp.where(taken, rows[q], pltpu.roll(rows[p], atoms - GROUP * bit, 1))
        rows = turned
        bit *= 2
    for g in range(groups):
        table_ref[g] = rows[g]

    mask = (
        lax.broadcasted_iota(jnp.int32, (GROUP, atoms), 1) % GROUP
        == lax.broadcasted_iota(jnp.int32, (GROUP, atoms), 0)
    )
    target = lax.broadcasted_iota(jnp.int32, (256, atoms), 0).astype(F32).astype(BF16)

    def group(g):
        table = table_ref[g]
        named = [(table[18:19, :] - at).astype(BF16) for at in range(0, extent, 256)]
        hot = jnp.concatenate(
            [jnp.where(target == name, BF16(1), BF16(0)) for name in named], axis=0
        )
        spread = jnp.concatenate(
            [jnp.where(mask, table[r : r + 1, :], 0.0) for r in range(18)], axis=0
        )
        top = spread.astype(BF16)
        rest = (spread - top.astype(F32)).astype(BF16)
        both = ((1,), (1,))
        dense = dot(top, hot, both) + dot(rest, hot, both)
        hi = dense.astype(BF16)
        lo = (dense - hi.astype(F32)).astype(BF16)
        for e in range(2):
            for a in range(3):
                at = pl.ds(pl.multiple_of((e * 3 + a) * atoms + g * GROUP, GROUP), GROUP)
                for b in range(3):
                    r = (e * 9 + 3 * a + b) * GROUP
                    near, far = slice(b * atoms, (b + 1) * atoms), slice(b * halo, (b + 1) * halo)
                    own_hi_ref[at, near] = hi[r : r + GROUP, :atoms]
                    own_lo_ref[at, near] = lo[r : r + GROUP, :atoms]
                    hi_ref[at, far] = hi[r : r + GROUP, atoms:]
                    lo_ref[at, far] = lo[r : r + GROUP, atoms:]

    def several(step, carry):
        for g in range(4):
            group(4 * step + g)
        return carry

    lax.fori_loop(0, groups // 4, several, 0)
    turned = turned_ref[...]
    for e in range(2):
        at = slice(3 * e * atoms, 3 * (e + 1) * atoms)
        hi, lo = own_hi_ref[at, :], own_lo_ref[at, :]
        flux_ref[at, :] = dot(hi, turned, ((1,), (1,))) + dot(lo, turned, ((1,), (1,)))


def relay_kernel(part_hbm, below_hbm, above_hbm, *refs):
    for got_ref, given_ref in zip(refs[: len(refs) // 2], refs[len(refs) // 2 :]):
        given_ref[...] = got_ref[...]


def flux_kernel(e, part_ref, hi_ref, lo_ref, below_ref, above_ref, after, flux_ref, halo_ref):
    count = below_ref.shape[0] // 3
    for b in range(3):
        at = 2 * b * count
        halo_ref[at : at + count] = below_ref[b * count : (b + 1) * count]
        halo_ref[at + count : at + 2 * count] = above_ref[b * count : (b + 1) * count]
    atoms = flux_ref.shape[0] // 3
    halo = halo_ref[...]
    at = slice(3 * e * atoms, 3 * (e + 1) * atoms)
    flux = part_ref[at, :] + (dot(hi_ref[at, :], halo) + dot(lo_ref[at, :], halo))
    flux_ref[...] = flux.astype(BF16)


def terms_of(quarter_refs, store):
    tiles = len(quarter_refs) // 2
    me, core = lax.axis_index("blk"), lax.axis_index("dir")
    for j in range(tiles):
        tile = lax.rem(me - j + tiles, tiles)
        for s in range(2):
            store(2 * tile + (core if s == 0 else 1 - core), quarter_refs[2 * j + s])


def couple_kernel(flux0_ref, flux1_ref, *refs):
    *quarter_refs, out_ref = refs
    half = quarter_refs[0].shape[0]
    block = out_ref.shape[1]
    core = lax.axis_index("dir")

    def store(quarter, turned_ref):
        for e, flux_ref in enumerate((flux0_ref, flux1_ref)):
            term = dot(turned_ref[...], flux_ref[...]).astype(BF16)
            for t in range(half // block):
                at = 2 * (quarter * (half // block) + t) + (core if e == 0 else 1 - core)
                out_ref[at] = term[t * block : (t + 1) * block]

    terms_of(quarter_refs, store)


def sum_kernel(scale, terms_ref, out_ref):
    pairs, block, half = terms_ref.shape
    for c in range(2):
        total = terms_ref[c].astype(F32)
        for d in range(1, pairs // 2):
            total = total + terms_ref[2 * d + c].astype(F32)
        out_ref[0, :, c * half : (c + 1) * half] = total * scale


def far_kernel(after, flux_ref, *refs):
    *quarter_refs, far_ref = refs
    home = lax.axis_index("dom")

    def store(quarter, turned_ref):
        @pl.when((quarter ^ home) == 3)
        def _():
            far_ref[...] = dot(turned_ref[...], flux_ref[...]).astype(BF16)

    terms_of(quarter_refs, store)


def early_kernel(flux_ref, *refs):
    *quarter_refs, far_ref = refs
    home, me, core = lax.axis_index("dom"), lax.axis_index("blk"), lax.axis_index("dir")
    owned = (me == home // 2, me != home // 2)
    odd = ((core ^ home) & 1) == 1
    for use, quarter_ref in zip(owned, (quarter_refs[1], quarter_refs[0])):

        @pl.when(jnp.logical_and(use, odd))
        def _():
            far_ref[...] = dot(quarter_ref[...], flux_ref[...]).astype(BF16)


def near_kernel(flux0_ref, flux1_ref, *refs):
    *quarter_refs, near0_ref, near1_ref, add0_ref, add1_ref, keep_ref, give_ref = refs
    home = lax.axis_index("dom")
    outs = {0: (keep_ref, give_ref), 1: (near0_ref, near1_ref), 2: (add0_ref, add1_ref)}

    def store(quarter, turned_ref):
        for away, out_refs in outs.items():

            @pl.when((quarter ^ home) == away)
            def _():
                for flux_ref, out_ref in zip((flux0_ref, flux1_ref), out_refs):
                    out_ref[...] = dot(turned_ref[...], flux_ref[...]).astype(out_ref.dtype)

    terms_of(quarter_refs, store)


def first_add_kernel(early_ref, late_ref, add_ref, sum_ref):
    home, core = lax.axis_index("dom"), lax.axis_index("dir")
    early = ((core ^ home) & 1) == 0
    for came, far_ref in ((early, early_ref), (jnp.logical_not(early), late_ref)):

        @pl.when(came)
        def _():
            sum_ref[...] = (add_ref[...] + far_ref[...].astype(F32)).astype(BF16)


def add_kernel(far_ref, add_ref, *refs):
    held_refs, (sum_ref, *given_refs) = refs[: len(refs) // 2], refs[len(refs) // 2 :]
    sum_ref[...] = (add_ref[...] + far_ref[...].astype(F32)).astype(BF16)
    for held_ref, given_ref in zip(held_refs, given_refs):
        given_ref[...] = held_ref[...]


def halving_sum_kernel(
    scale, keep_ref, give_ref, near0_ref, near1_ref, sum0_ref, sum1_ref, out_hbm, total_ref, sems
):
    half = keep_ref.shape[1]
    core = lax.axis_index("dir")
    copies = []
    for i, (owner, first, near, far) in enumerate(
        ((core, keep_ref, near0_ref, sum0_ref), (1 - core, give_ref, near1_ref, sum1_ref))
    ):
        total = first[...].astype(F32) + near[...].astype(F32) + far[...].astype(F32)
        total_ref[i] = total * scale
        columns = pl.ds(pl.multiple_of(owner * half, 128), half)
        copies.append(
            pltpu.make_async_copy(total_ref.at[i], out_hbm.at[0, :, columns], sems.at[i])
        )
        copies[i].start()
    for copy in copies:
        copy.wait()


def shift(value, axis, by):
    length = lax.axis_size(axis)
    return lax.ppermute(value, axis, [(i, (i + by) % length) for i in range(length)])


def swap(value, away, other_core):
    domains = lax.axis_size("dom")
    pairs = [
        (2 * d + c, 2 * (d ^ away) + (c ^ other_core)) for d in range(domains) for c in range(2)
    ]
    return lax.ppermute(value, ("dom", "dir"), pairs)


def swap_some(value, odd):
    domains = lax.axis_size("dom")
    pairs = [
        (2 * d + c, 2 * (d ^ 1) + c) for d in range(domains) for c in range(2) if (c ^ d) & 1 == odd
    ]
    return lax.ppermute(value, ("dom", "dir"), pairs)


def shape(dims, dtype):
    return jax.ShapeDtypeStruct(dims, dtype)


def per_device(panel_vectors, force_blocks, bond_vectors, neighbours, boundary_low, boundary_high):
    rows, cols = panel_vectors.shape
    atoms = rows // 3
    half = cols // 2
    count = boundary_low.shape[0]
    domains, tiles = lax.axis_size("dom"), lax.axis_size("blk")
    block = cols * tiles // domains
    vmem = pl.BlockSpec(memory_space=pltpu.VMEM)
    hbm = pl.BlockSpec(memory_space=pltpu.HBM)
    anywhere = pl.BlockSpec(memory_space=pl.ANY)

    lists = [boundary_low.reshape(1, count), boundary_high.reshape(1, count)]
    forces = force_blocks.transpose(1, 0, 2)
    prepared = (
        shape((half, rows), BF16),
        shape((3 * count, half), BF16),
        shape((3 * count, half), BF16),
    )
    turned, send_low, send_high, sources, bonds = pl.pallas_call(
        prep_kernel,
        out_shape=(
            *prepared,
            shape((11, *neighbours.shape), F32),
            shape(bond_vectors.shape, F32),
        ),
        in_specs=[hbm] * 6,
        out_specs=(hbm,) * 5,
        scratch_shapes=[
            pltpu.VMEM((rows, half), BF16),
            pltpu.VMEM((1, count), jnp.int32),
            pltpu.VMEM((1, count), jnp.int32),
            pltpu.VMEM(neighbours.shape, jnp.int32),
            *[pltpu.VMEM(like.shape, like.dtype) for like in prepared],
            pltpu.VMEM((11, *neighbours.shape), F32),
            pltpu.VMEM((6 * count, rows), BF16),
            pltpu.VMEM((half // 128, rows, 128), F32),
            pltpu.SemaphoreType.DMA((4,)),
            pltpu.SemaphoreType.DMA((5,)),
            pltpu.SemaphoreType.DMA((5,)),
        ],
        compiler_params=params(58),
        name="prep",
    )(panel_vectors, *lists, forces, bond_vectors, neighbours)
    quarters = [shift(turned, "blk", j) for j in range(1, tiles)]
    turned_other = shift(turned, "dir", 1)
    other_bonds = shift(bonds, "dir", 1)
    below = shift(send_high, "dom", 1)
    above = shift(send_low, "dom", -1)

    partial_flux, hi, lo = pl.pallas_call(
        weights_kernel,
        out_shape=(
            shape((2 * rows, half), F32),
            shape((2 * rows, 6 * count), BF16),
            shape((2 * rows, 6 * count), BF16),
        ),
        in_specs=[vmem] * 3,
        out_specs=(vmem,) * 3,
        scratch_shapes=[
            pltpu.VMEM((atoms // GROUP, 24, atoms), F32),
            pltpu.VMEM((2 * rows, rows), BF16),
            pltpu.VMEM((2 * rows, rows), BF16),
        ],
        compiler_params=params(32),
        cost_estimate=pl.CostEstimate(
            flops=8*10**9, bytes_accessed=10**7, transcendentals=0
        ),
        name="weights",
    )(sources, other_bonds, turned)

    quarters = pl.pallas_call(
        relay_kernel,
        out_shape=[shape(turned.shape, BF16)] * (tiles - 1),
        in_specs=[anywhere] * 3 + [vmem] * len(quarters),
        out_specs=[vmem] * (tiles - 1),
        compiler_params=params(16),
        name="relay",
    )(partial_flux, below, above, *quarters)
    given = [turned, turned_other]
    for quarter in quarters:
        given += [quarter, shift(quarter, "dir", 1)]

    def flux_of(e, after):
        return pl.pallas_call(
            functools.partial(flux_kernel, e),
            out_shape=shape((rows, half), BF16),
            in_specs=[vmem] * 5 + [anywhere],
            out_specs=vmem,
            scratch_shapes=[pltpu.VMEM((6 * count, half), BF16)],
            compiler_params=params(16),
            cost_estimate=pl.CostEstimate(
                flops=10**9, bytes_accessed=10**6, transcendentals=0
            ),
            name="flux",
        )(partial_flux, hi, lo, below, above, after)

    scale = (3.0 * atoms * domains) ** (-0.5)
    result = shape((1, block, cols), F32)
    if domains == 4 and block == half:
        sent, kept = shape((block, half), BF16), shape((block, half), F32)
        cost = pl.CostEstimate(flops=4 * 10**8, bytes_accessed=10**6, transcendentals=0)

        def far_of(flux, after):
            return pl.pallas_call(
                far_kernel,
                out_shape=sent,
                in_specs=[anywhere] + [vmem] * (1 + len(given)),
                out_specs=vmem,
                compiler_params=params(16),
                cost_estimate=cost,
                name="far",
            )(after, flux, *given)

        flux0 = flux_of(0, turned)
        early = pl.pallas_call(
            early_kernel,
            out_shape=sent,
            in_specs=[vmem] * 3,
            out_specs=vmem,
            compiler_params=params(16),
            cost_estimate=cost,
            name="early",
        )(flux0, given[0], given[2])
        flux1 = flux_of(1, early)
        far0 = far_of(flux0, flux1)
        far1 = far_of(flux1, far0)
        early, late, far1 = swap_some(early, 1), swap_some(far0, 0), swap(far1, 1, 0)
        near0, near1, add0, add1, keep, give = pl.pallas_call(
            near_kernel,
            out_shape=(sent, sent, kept, kept, kept, sent),
            in_specs=[vmem] * (2 + len(given)),
            out_specs=(vmem,) * 6,
            compiler_params=params(16),
            cost_estimate=cost,
            name="near",
        )(flux0, flux1, *given)

        def sum_of(far, add, *handed_on):
            return pl.pallas_call(
                add_kernel,
                out_shape=[sent] * (1 + len(handed_on)),
                in_specs=[vmem] * (2 + len(handed_on)),
                out_specs=[vmem] * (1 + len(handed_on)),
                compiler_params=params(16),
                name="add",
            )(far, add, *handed_on)

        near0 = swap(near0, 1, 0)
        sum0 = pl.pallas_call(
            first_add_kernel,
            out_shape=sent,
            in_specs=[vmem] * 3,
            out_specs=vmem,
            compiler_params=params(16),
            name="add",
        )(early, late, add0)
        sum0 = swap(sum0, 2, 0)
        sum1, near1, give = sum_of(far1, add1, near1, give)
        sum1, near1, give = swap(sum1, 2, 1), swap(near1, 1, 1), swap(give, 0, 1)
        return pl.pallas_call(
            lambda *refs: halving_sum_kernel(scale, *refs),
            out_shape=result,
            in_specs=[vmem] * 6,
            out_specs=hbm,
            scratch_shapes=[
                pltpu.VMEM((2, block, half), F32),
                pltpu.SemaphoreType.DMA((2,)),
            ],
            compiler_params=params(16),
            name="total",
        )(keep, give, near0, near1, sum0, sum1)

    terms = pl.pallas_call(
        couple_kernel,
        out_shape=shape((2 * domains, block, half), BF16),
        in_specs=[vmem] * (2 + len(given)),
        out_specs=vmem,
        compiler_params=params(16),
        name="couple",
    )(flux_of(0, below), flux_of(1, below), *given)
    terms = lax.all_to_all(terms, ("dom", "dir"), split_axis=0, concat_axis=0, tiled=True)
    return pl.pallas_call(
        lambda *refs: sum_kernel(scale, *refs),
        out_shape=result,
        in_specs=[vmem],
        out_specs=vmem,
        compiler_params=params(),
        name="total",
    )(terms)


def solution(mesh):
    in_specs = (
        P("dom", ("panel", "blk")),
        P(None, None, "dom"),
        P("dir", None, "dom"),
        P(None, "dom"),
        P("dom"),
        P("dom"),
    )
    out_specs = P("dir", ("panel", "dom"), "blk")
    return jax.shard_map(
        per_device, mesh=mesh, in_specs=in_specs, out_specs=out_specs, check_vma=False
    )
```

```python
import functools

import jax
import jax.numpy as jnp
from jax import lax
from jax.experimental import pallas as pl
from jax.experimental.pallas import tpu as pltpu
from jax.sharding import PartitionSpec as P

GROUP = 16
BF16 = jnp.bfloat16
F32 = jnp.float32


def params(mib=24):
    return pltpu.CompilerParams(vmem_limit_bytes=mib * 1024 * 1024)


def dot(a, b, contract=((1,), (0,))):
    return lax.dot_general(a, b, (contract, ((), ())), preferred_element_type=F32)


def one_hot(mask):
    return jnp.where(mask, 1.0, 0.0).astype(BF16)


def core_columns(core, half, piece, i):
    return pl.ds(pl.multiple_of(core * piece, 128) + i * 2 * piece, piece)


def prep_kernel(
    v_hbm, low_hbm, high_hbm, force_hbm, bond_hbm, near_hbm,
    turned_hbm, send_low_hbm, send_high_hbm, source_hbm, bond_out_hbm, *refs
):
    pieces = len(refs) - 13
    piece_hbms, scratch_refs = refs[:pieces], refs[pieces:]
    v_ref, low_ref, high_ref, near_ref, turned_ref, send_low_ref, send_high_ref = scratch_refs[:7]
    source_ref, pick_ref, wide_ref, v_sems, in_sems, out_sems = scratch_refs[7:]
    rows, half = v_ref.shape
    atoms = rows // 3
    arriving = [
        pltpu.make_async_copy(source, target, in_sems.at[i])
        for i, (source, target) in enumerate(
            (
                (low_hbm, low_ref),
                (high_hbm, high_ref),
                (near_hbm, near_ref),
                (force_hbm, source_ref.at[0:9]),
                (bond_hbm, source_ref.at[9:10]),
            )
        )
    ]
    piece = half // pieces
    v_in = [
        pltpu.make_async_copy(
            v_hbm.at[:, core_columns(lax.axis_index("dir"), half, piece, i)],
            v_ref.at[:, pl.ds(i * piece, piece)],
            v_sems.at[i],
        )
        for i in range(pieces)
    ]
    for copy in arriving + v_in:
        copy.start()
    leaving = []

    def leave(ref, hbm):
        copy = pltpu.make_async_copy(ref, hbm, out_sems.at[len(leaving)])
        copy.start()
        leaving.append(copy)

    for copy in arriving:
        copy.wait()
    source_ref[10] = near_ref[...].astype(F32)
    leave(source_ref.at[9:10], bond_out_hbm)
    leave(source_ref, source_hbm)
    for i, list_ref in enumerate((high_ref, low_ref)):
        count = list_ref.shape[1]
        named = jnp.broadcast_to(list_ref[...], (128, count)).T
        lane = lax.broadcasted_iota(jnp.int32, (count, 128), 1)
        for b in range(3):
            wanted = 3 * named + b
            at = (3 * i + b) * count
            for t in range(rows // 128):
                pick_ref[at : at + count, t * 128 : (t + 1) * 128] = one_hot(
                    lane + t * 128 == wanted
                )
    for copy in v_in:
        copy.wait()
    for t in range(half // 128):
        columns = slice(t * 128, (t + 1) * 128)
        wide_ref[t] = v_ref[:, columns].astype(F32)
        for b in range(3):
            part = wide_ref[t, pl.ds(b, atoms, stride=3), :]
            turned_ref[columns, b * atoms : (b + 1) * atoms] = part.T.astype(BF16)
    leave(turned_ref, turned_hbm)
    for i, piece_hbm in enumerate(piece_hbms):
        at = lax.rem(lax.axis_index("dom") + i + 1, 2) * piece if pieces == 2 else 0
        leave(turned_ref.at[pl.ds(pl.multiple_of(at, 64), piece)], piece_hbm)
    picked = dot(pick_ref[...], v_ref[...]).astype(BF16)
    send_high_ref[...] = picked[: 3 * count]
    leave(send_high_ref, send_high_hbm)
    send_low_ref[...] = picked[3 * count :]
    leave(send_low_ref, send_low_hbm)
    for copy in leaving:
        copy.wait()


def weights_kernel(
    source_ref, other_ref, turned_ref,
    flux_ref, hi_ref, lo_ref, table_ref, own_hi_ref, own_lo_ref,
):
    _, steps, atoms = source_ref.shape
    groups = atoms // GROUP
    halo = hi_ref.shape[1] // 3
    extent = atoms + halo
    bonds = (source_ref[9], other_ref[0])
    lane = lax.broadcasted_iota(jnp.int32, (24, atoms), 1)
    rows = []
    for k in range(steps):
        force = source_ref[0:9, k, :]
        near = source_ref[10, k : k + 1, :]
        rows.append(
            jnp.concatenate(
                [force * bonds[0][k : k + 1, :], force * bonds[1][k : k + 1, :]]
                + [jnp.broadcast_to(near, (6, atoms))],
                axis=0,
            )
        )
    bit = 1
    while bit < steps:
        taken = ((lane // GROUP) & bit) != 0
        turned = list(rows)
        for p in range(steps):
            if p & bit:
                continue
            q = p | bit
            turned[p] = jnp.where(taken, pltpu.roll(rows[q], GROUP * bit, 1), rows[p])
            turned[q] = jnp.where(taken, rows[q], pltpu.roll(rows[p], atoms - GROUP * bit, 1))
        rows = turned
        bit *= 2
    for g in range(groups):
        table_ref[g] = rows[g]

    mask = (
        lax.broadcasted_iota(jnp.int32, (GROUP, atoms), 1) % GROUP
        == lax.broadcasted_iota(jnp.int32, (GROUP, atoms), 0)
    )
    target = lax.broadcasted_iota(jnp.int32, (256, atoms), 0).astype(F32).astype(BF16)

    def group(g):
        table = table_ref[g]
        named = [(table[18:19, :] - at).astype(BF16) for at in range(0, extent, 256)]
        hot = jnp.concatenate(
            [jnp.where(target == name, BF16(1), BF16(0)) for name in named], axis=0
        )
        spread = jnp.concatenate(
            [jnp.where(mask, table[r : r + 1, :], 0.0) for r in range(18)], axis=0
        )
        top = spread.astype(BF16)
        rest = (spread - top.astype(F32)).astype(BF16)
        both = ((1,), (1,))
        dense = dot(top, hot, both) + dot(rest, hot, both)
        hi = dense.astype(BF16)
        lo = (dense - hi.astype(F32)).astype(BF16)
        for e in range(2):
            for a in range(3):
                at = pl.ds(pl.multiple_of((e * 3 + a) * atoms + g * GROUP, GROUP), GROUP)
                for b in range(3):
                    r = (e * 9 + 3 * a + b) * GROUP
                    near, far = slice(b * atoms, (b + 1) * atoms), slice(b * halo, (b + 1) * halo)
                    own_hi_ref[at, near] = hi[r : r + GROUP, :atoms]
                    own_lo_ref[at, near] = lo[r : r + GROUP, :atoms]
                    hi_ref[at, far] = hi[r : r + GROUP, atoms:]
                    lo_ref[at, far] = lo[r : r + GROUP, atoms:]

    def several(step, carry):
        for g in range(4):
            group(4 * step + g)
        return carry

    lax.fori_loop(0, groups // 4, several, 0)
    turned = turned_ref[...]
    for e in range(2):
        at = slice(3 * e * atoms, 3 * (e + 1) * atoms)
        hi, lo = own_hi_ref[at, :], own_lo_ref[at, :]
        flux_ref[at, :] = dot(hi, turned, ((1,), (1,))) + dot(lo, turned, ((1,), (1,)))


def relay_kernel(waited, *refs):
    refs = refs[waited:]
    for got_ref, given_ref in zip(refs[: len(refs) // 2], refs[len(refs) // 2 :]):
        given_ref[...] = got_ref[...]


def flux_kernel(e, part_ref, hi_ref, lo_ref, below_ref, above_ref, flux_ref, halo_ref):
    count = below_ref.shape[0] // 3
    for b in range(3):
        at = 2 * b * count
        halo_ref[at : at + count] = below_ref[b * count : (b + 1) * count]
        halo_ref[at + count : at + 2 * count] = above_ref[b * count : (b + 1) * count]
    atoms = flux_ref.shape[0] // 3
    halo = halo_ref[...]
    at = slice(3 * e * atoms, 3 * (e + 1) * atoms)
    flux = part_ref[at, :] + (dot(hi_ref[at, :], halo) + dot(lo_ref[at, :], halo))
    flux_ref[...] = flux.astype(BF16)


def terms_of(quarter_refs, store):
    tiles = len(quarter_refs) // 2
    me, core = lax.axis_index("blk"), lax.axis_index("dir")
    for j in range(tiles):
        tile = lax.rem(me - j + tiles, tiles)
        for s in range(2):
            store(2 * tile + (core if s == 0 else 1 - core), quarter_refs[2 * j + s])


def couple_kernel(flux0_ref, flux1_ref, *refs):
    *quarter_refs, out_ref = refs
    half = quarter_refs[0].shape[0]
    block = out_ref.shape[1]
    core = lax.axis_index("dir")

    def store(quarter, turned_ref):
        for e, flux_ref in enumerate((flux0_ref, flux1_ref)):
            term = dot(turned_ref[...], flux_ref[...]).astype(BF16)
            for t in range(half // block):
                at = 2 * (quarter * (half // block) + t) + (core if e == 0 else 1 - core)
                out_ref[at] = term[t * block : (t + 1) * block]

    terms_of(quarter_refs, store)


def sum_kernel(scale, terms_ref, out_ref):
    pairs, block, half = terms_ref.shape
    for c in range(2):
        total = terms_ref[c].astype(F32)
        for d in range(1, pairs // 2):
            total = total + terms_ref[2 * d + c].astype(F32)
        out_ref[0, :, c * half : (c + 1) * half] = total * scale


def quarter_terms(this_half, parity, quarter_refs, flux_refs, out_refs):
    mine_ref, other_ref, *got_refs = quarter_refs
    home, core = lax.axis_index("dom"), lax.axis_index("dir")
    piece = got_refs[0].shape[0]
    here = (lax.axis_index("blk") == home // 2) == this_half
    rows = pl.ds(pl.multiple_of(((home ^ parity) & 1) * piece, 128), piece)

    def store(sources):
        for owner, turned in zip((core, 1 - core), sources):
            at = pl.ds(pl.multiple_of(owner * piece, 128), piece)
            for flux_ref, out_ref in zip(flux_refs, out_refs):
                out_ref[at, :] = dot(turned(), flux_ref[...]).astype(out_ref.dtype)

    @pl.when(here)
    def _():
        store((lambda: mine_ref[rows, :], lambda: other_ref[rows, :]))

    @pl.when(jnp.logical_not(here))
    def _():
        store((lambda: got_refs[0][...], lambda: got_refs[1][...]))


def far_kernel(*refs):
    quarter_terms(False, 1, refs[-5:-1], (refs[-6],), refs[-1:])


def near_kernel(flux0_ref, flux1_ref, *refs):
    quarter_terms(True, 1, refs[:4], (flux0_ref, flux1_ref), refs[4:])


def even_kernel(flux0_ref, flux1_ref, *refs):
    quarter_terms(False, 0, refs[:4], (flux0_ref, flux1_ref), refs[4:6])
    quarter_terms(True, 0, refs[:4], (flux0_ref, flux1_ref), refs[6:])


def add_kernel(far_ref, add_ref, *refs):
    held_refs, (sum_ref, *given_refs) = refs[: len(refs) // 2], refs[len(refs) // 2 :]
    sum_ref[...] = (add_ref[...] + far_ref[...].astype(F32)).astype(BF16)
    for held_ref, given_ref in zip(held_refs, given_refs):
        given_ref[...] = held_ref[...]


def halving_sum_kernel(
    scale, keep_ref, give_ref, near0_ref, near1_ref, sum0_ref, sum1_ref, out_hbm, total_ref, sems
):
    half = keep_ref.shape[1]
    core = lax.axis_index("dir")
    copies = []
    for i, (owner, first, near, far) in enumerate(
        ((core, keep_ref, near0_ref, sum0_ref), (1 - core, give_ref, near1_ref, sum1_ref))
    ):
        total = first[...].astype(F32) + near[...].astype(F32) + far[...].astype(F32)
        total_ref[i] = total * scale
        for j in range(2):
            piece = half // 2
            copy = pltpu.make_async_copy(
                total_ref.at[i, :, pl.ds(j * piece, piece)],
                out_hbm.at[0, :, core_columns(owner, half, piece, j)],
                sems.at[2 * i + j],
            )
            copy.start()
            copies.append(copy)
    for copy in copies:
        copy.wait()


def shift(value, axis, by):
    length = lax.axis_size(axis)
    return lax.ppermute(value, axis, [(i, (i + by) % length) for i in range(length)])


def swap(value, away, other_core):
    domains = lax.axis_size("dom")
    pairs = [
        (2 * d + c, 2 * (d ^ away) + (c ^ other_core)) for d in range(domains) for c in range(2)
    ]
    return lax.ppermute(value, ("dom", "dir"), pairs)


def shape(dims, dtype):
    return jax.ShapeDtypeStruct(dims, dtype)


def per_device(panel_vectors, force_blocks, bond_vectors, neighbours, boundary_low, boundary_high):
    rows, cols = panel_vectors.shape
    atoms = rows // 3
    half = cols // 2
    count = boundary_low.shape[0]
    domains, tiles = lax.axis_size("dom"), lax.axis_size("blk")
    block = cols * tiles // domains
    vmem = pl.BlockSpec(memory_space=pltpu.VMEM)
    hbm = pl.BlockSpec(memory_space=pltpu.HBM)
    anywhere = pl.BlockSpec(memory_space=pl.ANY)

    halving = domains == 4 and block == half
    pieces = 2 if halving else 1
    lists = [boundary_low.reshape(1, count), boundary_high.reshape(1, count)]
    forces = force_blocks.transpose(1, 0, 2)
    prepared = (
        shape((half, rows), BF16),
        shape((3 * count, half), BF16),
        shape((3 * count, half), BF16),
    )
    turned, send_low, send_high, sources, bonds, *sent_pieces = pl.pallas_call(
        prep_kernel,
        out_shape=(
            *prepared,
            shape((11, *neighbours.shape), F32),
            shape(bond_vectors.shape, F32),
        )
        + (shape((half // pieces, rows), BF16),) * pieces,
        in_specs=[hbm] * 6,
        out_specs=(hbm,) * (5 + pieces),
        scratch_shapes=[
            pltpu.VMEM((rows, half), BF16),
            pltpu.VMEM((1, count), jnp.int32),
            pltpu.VMEM((1, count), jnp.int32),
            pltpu.VMEM(neighbours.shape, jnp.int32),
            *[pltpu.VMEM(like.shape, like.dtype) for like in prepared],
            pltpu.VMEM((11, *neighbours.shape), F32),
            pltpu.VMEM((6 * count, rows), BF16),
            pltpu.VMEM((half // 128, rows, 128), F32),
            pltpu.SemaphoreType.DMA((4,)),
            pltpu.SemaphoreType.DMA((5,)),
            pltpu.SemaphoreType.DMA((5 + pieces,)),
        ],
        compiler_params=params(58),
        name="prep",
    )(panel_vectors, *lists, forces, bond_vectors, neighbours)
    quarters = [shift(piece, "blk", j) for j in range(1, tiles) for piece in sent_pieces[::-1]][::-1]
    turned_other = shift(turned, "dir", 1)
    other_bonds = shift(bonds, "dir", 1)
    below = shift(send_high, "dom", 1)
    above = shift(send_low, "dom", -1)

    partial_flux, hi, lo = pl.pallas_call(
        weights_kernel,
        out_shape=(
            shape((2 * rows, half), F32),
            shape((2 * rows, 6 * count), BF16),
            shape((2 * rows, 6 * count), BF16),
        ),
        in_specs=[vmem] * 3,
        out_specs=(vmem,) * 3,
        scratch_shapes=[
            pltpu.VMEM((atoms // GROUP, 24, atoms), F32),
            pltpu.VMEM((2 * rows, rows), BF16),
            pltpu.VMEM((2 * rows, rows), BF16),
        ],
        compiler_params=params(32),
        cost_estimate=pl.CostEstimate(
            flops=8*10**9, bytes_accessed=10**7, transcendentals=0
        ),
        name="weights",
    )(sources, other_bonds, turned)

    def relay(after, *values):
        return pl.pallas_call(
            functools.partial(relay_kernel, len(after)),
            out_shape=[shape(value.shape, value.dtype) for value in values],
            in_specs=[anywhere] * len(after) + [vmem] * len(values),
            out_specs=[vmem] * len(values),
            compiler_params=params(16),
            name="relay",
        )(*after, *values)

    def flux_of(e):
        return pl.pallas_call(
            functools.partial(flux_kernel, e),
            out_shape=shape((rows, half), BF16),
            in_specs=[vmem] * 5,
            out_specs=vmem,
            scratch_shapes=[pltpu.VMEM((6 * count, half), BF16)],
            compiler_params=params(16),
            cost_estimate=pl.CostEstimate(
                flops=10**9, bytes_accessed=10**6, transcendentals=0
            ),
            name="flux",
        )(partial_flux, hi, lo, below, above)

    scale = (3.0 * atoms * domains) ** (-0.5)
    result = shape((1, block, cols), F32)
    if halving:
        sent, kept = shape((block, half), BF16), shape((block, half), F32)
        cost = pl.CostEstimate(flops=4 * 10**8, bytes_accessed=10**6, transcendentals=0)

        (first,) = relay((partial_flux, below, above), quarters[0])
        odd = [turned, turned_other, first, shift(first, "dir", 1)]

        def terms_of_quarters(kernel, name, after, fluxes, quarter_values, like):
            return pl.pallas_call(
                kernel,
                out_shape=like,
                in_specs=[anywhere] * len(after) + [vmem] * (len(fluxes) + 4),
                out_specs=[vmem] * len(like),
                compiler_params=params(16),
                cost_estimate=cost,
                name=name,
            )(*after, *fluxes, *quarter_values)

        flux0, flux1 = flux_of(0), flux_of(1)
        (second,) = relay((flux0, flux1), quarters[1])
        (far0,) = terms_of_quarters(far_kernel, "far", (flux1, second), (flux0,), odd, [sent])
        (far1,) = terms_of_quarters(far_kernel, "far", (far0,), (flux1,), odd, [sent])
        even = [turned, turned_other, second, shift(second, "dir", 1)]
        far0, far1 = swap(far0, 1, 0), swap(far1, 1, 0)
        near0, near1 = terms_of_quarters(
            near_kernel, "near", (), (flux0, flux1), odd, [sent, sent]
        )
        add0, add1, keep, give = terms_of_quarters(
            even_kernel, "even", (), (flux0, flux1), even, [kept, kept, kept, sent]
        )

        def sum_of(far, add, *handed_on):
            return pl.pallas_call(
                add_kernel,
                out_shape=[sent] * (1 + len(handed_on)),
                in_specs=[vmem] * (2 + len(handed_on)),
                out_specs=[vmem] * (1 + len(handed_on)),
                compiler_params=params(16),
                name="add",
            )(far, add, *handed_on)

        near0 = swap(near0, 1, 0)
        sum0 = swap(sum_of(far0, add0)[0], 2, 0)
        sum1, near1, give = sum_of(far1, add1, near1, give)
        sum1, near1, give = swap(sum1, 2, 1), swap(near1, 1, 1), swap(give, 0, 1)
        return pl.pallas_call(
            lambda *refs: halving_sum_kernel(scale, *refs),
            out_shape=result,
            in_specs=[vmem] * 6,
            out_specs=hbm,
            scratch_shapes=[
                pltpu.VMEM((2, block, half), F32),
                pltpu.SemaphoreType.DMA((4,)),
            ],
            compiler_params=params(16),
            name="total",
        )(keep, give, near0, near1, sum0, sum1)

    given = [turned, turned_other]
    for quarter in relay((partial_flux, below, above), *quarters):
        given += [quarter, shift(quarter, "dir", 1)]
    terms = pl.pallas_call(
        couple_kernel,
        out_shape=shape((2 * domains, block, half), BF16),
        in_specs=[vmem] * (2 + len(given)),
        out_specs=vmem,
        compiler_params=params(16),
        name="couple",
    )(flux_of(0), flux_of(1), *given)
    terms = lax.all_to_all(terms, ("dom", "dir"), split_axis=0, concat_axis=0, tiled=True)
    return pl.pallas_call(
        lambda *refs: sum_kernel(scale, *refs),
        out_shape=result,
        in_specs=[vmem],
        out_specs=vmem,
        compiler_params=params(),
        name="total",
    )(terms)


def solution(mesh):
    in_specs = (
        P("dom", ("panel", "blk")),
        P(None, None, "dom"),
        P("dir", None, "dom"),
        P(None, "dom"),
        P("dom"),
        P("dom"),
    )
    out_specs = P("dir", ("panel", "dom"), "blk")
    return jax.shard_map(
        per_device, mesh=mesh, in_specs=in_specs, out_specs=out_specs, check_vma=False
    )
```

```python
import functools

import jax
import jax.numpy as jnp
from jax import lax
from jax.experimental import pallas as pl
from jax.experimental.pallas import tpu as pltpu
from jax.sharding import PartitionSpec as P

GROUP = 16
BF16 = jnp.bfloat16
F32 = jnp.float32


def params(mib=24):
    return pltpu.CompilerParams(vmem_limit_bytes=mib * 1024 * 1024)


def dot(a, b, contract=((1,), (0,))):
    return lax.dot_general(a, b, (contract, ((), ())), preferred_element_type=F32)


def one_hot(mask):
    return jnp.where(mask, 1.0, 0.0).astype(BF16)


def my_columns(half):
    return pl.ds(pl.multiple_of(lax.axis_index("dir") * half, 128), half)


def prep_kernel(
    v_hbm, low_hbm, high_hbm, force_hbm, bond_hbm, near_hbm,
    turned_hbm, send_low_hbm, send_high_hbm, source_hbm, bond_out_hbm,
    v_ref, low_ref, high_ref, near_ref, turned_ref, send_low_ref, send_high_ref,
    source_ref, pick_ref, wide_ref, v_sems, in_sems, out_sems,
):
    rows, half = v_ref.shape
    atoms = rows // 3
    arriving = [
        pltpu.make_async_copy(source, target, in_sems.at[i])
        for i, (source, target) in enumerate(
            (
                (low_hbm, low_ref),
                (high_hbm, high_ref),
                (near_hbm, near_ref),
                (force_hbm, source_ref.at[0:9]),
                (bond_hbm, source_ref.at[9:10]),
            )
        )
    ]
    quarter = rows // 4
    v_in = [
        pltpu.make_async_copy(
            v_hbm.at[pl.ds(at, quarter), my_columns(half)], v_ref.at[pl.ds(at, quarter)], v_sems.at[i]
        )
        for i, at in enumerate(range(0, rows, quarter))
    ]
    for copy in arriving + v_in:
        copy.start()
    leaving = []

    def leave(ref, hbm):
        copy = pltpu.make_async_copy(ref, hbm, out_sems.at[len(leaving)])
        copy.start()
        leaving.append(copy)

    for copy in arriving:
        copy.wait()
    source_ref[10] = near_ref[...].astype(F32)
    leave(source_ref.at[9:10], bond_out_hbm)
    leave(source_ref, source_hbm)
    for i, list_ref in enumerate((high_ref, low_ref)):
        count = list_ref.shape[1]
        named = jnp.broadcast_to(list_ref[...], (128, count)).T
        lane = lax.broadcasted_iota(jnp.int32, (count, 128), 1)
        for b in range(3):
            wanted = 3 * named + b
            at = (3 * i + b) * count
            for t in range(rows // 128):
                pick_ref[at : at + count, t * 128 : (t + 1) * 128] = one_hot(
                    lane + t * 128 == wanted
                )
    for copy in v_in:
        copy.wait()
    picked = dot(pick_ref[...], v_ref[...]).astype(BF16)
    send_high_ref[...] = picked[: 3 * count]
    leave(send_high_ref, send_high_hbm)
    send_low_ref[...] = picked[3 * count :]
    leave(send_low_ref, send_low_hbm)
    for t in range(half // 128):
        columns = slice(t * 128, (t + 1) * 128)
        wide_ref[t] = v_ref[:, columns].astype(F32)
        for b in range(3):
            part = wide_ref[t, pl.ds(b, atoms, stride=3), :]
            turned_ref[columns, b * atoms : (b + 1) * atoms] = part.astype(BF16).T
    leave(turned_ref, turned_hbm)
    for copy in leaving:
        copy.wait()


def weights_kernel(
    source_ref, other_ref, turned_ref,
    flux_ref, hi_ref, lo_ref, table_ref, own_hi_ref, own_lo_ref,
):
    _, steps, atoms = source_ref.shape
    groups = atoms // GROUP
    halo = hi_ref.shape[1] // 3
    extent = atoms + halo
    bonds = (source_ref[9], other_ref[0])
    lane = lax.broadcasted_iota(jnp.int32, (24, atoms), 1)
    rows = []
    for k in range(steps):
        force = source_ref[0:9, k, :]
        near = source_ref[10, k : k + 1, :]
        rows.append(
            jnp.concatenate(
                [force * bonds[0][k : k + 1, :], force * bonds[1][k : k + 1, :]]
                + [jnp.broadcast_to(near, (6, atoms))],
                axis=0,
            )
        )
    bit = 1
    while bit < steps:
        taken = ((lane // GROUP) & bit) != 0
        turned = list(rows)
        for p in range(steps):
            if p & bit:
                continue
            q = p | bit
            turned[p] = jnp.where(taken, pltpu.roll(rows[q], GROUP * bit, 1), rows[p])
            turned[q] = jnp.where(taken, rows[q], pltpu.roll(rows[p], atoms - GROUP * bit, 1))
        rows = turned
        bit *= 2
    for g in range(groups):
        table_ref[g] = rows[g]

    mask = (
        lax.broadcasted_iota(jnp.int32, (GROUP, atoms), 1) % GROUP
        == lax.broadcasted_iota(jnp.int32, (GROUP, atoms), 0)
    )
    target = lax.broadcasted_iota(jnp.int32, (256, atoms), 0).astype(F32).astype(BF16)

    def group(g):
        table = table_ref[g]
        named = [(table[18:19, :] - at).astype(BF16) for at in range(0, extent, 256)]
        hot = jnp.concatenate(
            [jnp.where(target == name, BF16(1), BF16(0)) for name in named], axis=0
        )
        spread = jnp.concatenate(
            [jnp.where(mask, table[r : r + 1, :], 0.0) for r in range(18)], axis=0
        )
        top = spread.astype(BF16)
        rest = (spread - top.astype(F32)).astype(BF16)
        both = ((1,), (1,))
        dense = dot(top, hot, both) + dot(rest, hot, both)
        hi = dense.astype(BF16)
        lo = (dense - hi.astype(F32)).astype(BF16)
        for e in range(2):
            for a in range(3):
                at = pl.ds(pl.multiple_of((e * 3 + a) * atoms + g * GROUP, GROUP), GROUP)
                for b in range(3):
                    r = (e * 9 + 3 * a + b) * GROUP
                    near, far = slice(b * atoms, (b + 1) * atoms), slice(b * halo, (b + 1) * halo)
                    own_hi_ref[at, near] = hi[r : r + GROUP, :atoms]
                    own_lo_ref[at, near] = lo[r : r + GROUP, :atoms]
                    hi_ref[at, far] = hi[r : r + GROUP, atoms:]
                    lo_ref[at, far] = lo[r : r + GROUP, atoms:]

    def several(step, carry):
        for g in range(4):
            group(4 * step + g)
        return carry

    lax.fori_loop(0, groups // 4, several, 0)
    turned = turned_ref[...]
    for e in range(2):
        at = slice(3 * e * atoms, 3 * (e + 1) * atoms)
        hi, lo = own_hi_ref[at, :], own_lo_ref[at, :]
        flux_ref[at, :] = dot(hi, turned, ((1,), (1,))) + dot(lo, turned, ((1,), (1,)))


def relay_kernel(part_hbm, below_hbm, above_hbm, *refs):
    for got_ref, given_ref in zip(refs[: len(refs) // 2], refs[len(refs) // 2 :]):
        given_ref[...] = got_ref[...]


def flux_kernel(e, part_ref, hi_ref, lo_ref, below_ref, above_ref, flux_ref, halo_ref):
    count = below_ref.shape[0] // 3
    for b in range(3):
        at = 2 * b * count
        halo_ref[at : at + count] = below_ref[b * count : (b + 1) * count]
        halo_ref[at + count : at + 2 * count] = above_ref[b * count : (b + 1) * count]
    atoms = flux_ref.shape[0] // 3
    halo = halo_ref[...]
    at = slice(3 * e * atoms, 3 * (e + 1) * atoms)
    flux = part_ref[at, :] + (dot(hi_ref[at, :], halo) + dot(lo_ref[at, :], halo))
    flux_ref[...] = flux.astype(BF16)


def terms_of(quarter_refs, store):
    tiles = len(quarter_refs) // 2
    me, core = lax.axis_index("blk"), lax.axis_index("dir")
    for j in range(tiles):
        tile = lax.rem(me - j + tiles, tiles)
        for s in range(2):
            store(2 * tile + (core if s == 0 else 1 - core), quarter_refs[2 * j + s])


def couple_kernel(flux0_ref, flux1_ref, *refs):
    *quarter_refs, out_ref = refs
    half = quarter_refs[0].shape[0]
    block = out_ref.shape[1]
    core = lax.axis_index("dir")

    def store(quarter, turned_ref):
        for e, flux_ref in enumerate((flux0_ref, flux1_ref)):
            term = dot(turned_ref[...], flux_ref[...]).astype(BF16)
            for t in range(half // block):
                at = 2 * (quarter * (half // block) + t) + (core if e == 0 else 1 - core)
                out_ref[at] = term[t * block : (t + 1) * block]

    terms_of(quarter_refs, store)


def sum_kernel(scale, terms_ref, out_ref):
    pairs, block, half = terms_ref.shape
    for c in range(2):
        total = terms_ref[c].astype(F32)
        for d in range(1, pairs // 2):
            total = total + terms_ref[2 * d + c].astype(F32)
        out_ref[0, :, c * half : (c + 1) * half] = total * scale


def far_kernel(after, flux_ref, *refs):
    *quarter_refs, far_ref = refs
    home = lax.axis_index("dom")

    def store(quarter, turned_ref):
        @pl.when((quarter ^ home) == 3)
        def _():
            far_ref[...] = dot(turned_ref[...], flux_ref[...]).astype(BF16)

    terms_of(quarter_refs, store)


def near_kernel(flux0_ref, flux1_ref, *refs):
    *quarter_refs, near0_ref, near1_ref, add0_ref, add1_ref, keep_ref, give_ref = refs
    home = lax.axis_index("dom")
    outs = {0: (keep_ref, give_ref), 1: (near0_ref, near1_ref), 2: (add0_ref, add1_ref)}

    def store(quarter, turned_ref):
        for away, out_refs in outs.items():

            @pl.when((quarter ^ home) == away)
            def _():
                for flux_ref, out_ref in zip((flux0_ref, flux1_ref), out_refs):
                    out_ref[...] = dot(turned_ref[...], flux_ref[...]).astype(out_ref.dtype)

    terms_of(quarter_refs, store)


def add_kernel(far_ref, add_ref, *refs):
    held_refs, (sum_ref, *given_refs) = refs[: len(refs) // 2], refs[len(refs) // 2 :]
    sum_ref[...] = (add_ref[...] + far_ref[...].astype(F32)).astype(BF16)
    for held_ref, given_ref in zip(held_refs, given_refs):
        given_ref[...] = held_ref[...]


def halving_sum_kernel(
    scale, keep_ref, give_ref, near0_ref, near1_ref, sum0_ref, sum1_ref, out_hbm, total_ref, sems
):
    half = keep_ref.shape[1]
    core = lax.axis_index("dir")
    copies = []
    for i, (owner, first, near, far) in enumerate(
        ((core, keep_ref, near0_ref, sum0_ref), (1 - core, give_ref, near1_ref, sum1_ref))
    ):
        total = first[...].astype(F32) + near[...].astype(F32) + far[...].astype(F32)
        total_ref[i] = total * scale
        columns = pl.ds(pl.multiple_of(owner * half, 128), half)
        copies.append(
            pltpu.make_async_copy(total_ref.at[i], out_hbm.at[0, :, columns], sems.at[i])
        )
        copies[i].start()
    for copy in copies:
        copy.wait()


def shift(value, axis, by):
    length = lax.axis_size(axis)
    return lax.ppermute(value, axis, [(i, (i + by) % length) for i in range(length)])


def swap(value, away, other_core):
    domains = lax.axis_size("dom")
    pairs = [
        (2 * d + c, 2 * (d ^ away) + (c ^ other_core)) for d in range(domains) for c in range(2)
    ]
    return lax.ppermute(value, ("dom", "dir"), pairs)


def shape(dims, dtype):
    return jax.ShapeDtypeStruct(dims, dtype)


def per_device(panel_vectors, force_blocks, bond_vectors, neighbours, boundary_low, boundary_high):
    rows, cols = panel_vectors.shape
    atoms = rows // 3
    half = cols // 2
    count = boundary_low.shape[0]
    domains, tiles = lax.axis_size("dom"), lax.axis_size("blk")
    block = cols * tiles // domains
    vmem = pl.BlockSpec(memory_space=pltpu.VMEM)
    hbm = pl.BlockSpec(memory_space=pltpu.HBM)
    anywhere = pl.BlockSpec(memory_space=pl.ANY)

    lists = [boundary_low.reshape(1, count), boundary_high.reshape(1, count)]
    forces = force_blocks.transpose(1, 0, 2)
    prepared = (
        shape((half, rows), BF16),
        shape((3 * count, half), BF16),
        shape((3 * count, half), BF16),
    )
    turned, send_low, send_high, sources, bonds = pl.pallas_call(
        prep_kernel,
        out_shape=(
            *prepared,
            shape((11, *neighbours.shape), F32),
            shape(bond_vectors.shape, F32),
        ),
        in_specs=[hbm] * 6,
        out_specs=(hbm,) * 5,
        scratch_shapes=[
            pltpu.VMEM((rows, half), BF16),
            pltpu.VMEM((1, count), jnp.int32),
            pltpu.VMEM((1, count), jnp.int32),
            pltpu.VMEM(neighbours.shape, jnp.int32),
            *[pltpu.VMEM(like.shape, like.dtype) for like in prepared],
            pltpu.VMEM((11, *neighbours.shape), F32),
            pltpu.VMEM((6 * count, rows), BF16),
            pltpu.VMEM((half // 128, rows, 128), F32),
            pltpu.SemaphoreType.DMA((4,)),
            pltpu.SemaphoreType.DMA((5,)),
            pltpu.SemaphoreType.DMA((5,)),
        ],
        compiler_params=params(58),
        name="prep",
    )(panel_vectors, *lists, forces, bond_vectors, neighbours)
    quarters = [shift(turned, "blk", j) for j in range(1, tiles)]
    turned_other = shift(turned, "dir", 1)
    other_bonds = shift(bonds, "dir", 1)
    below = shift(send_high, "dom", 1)
    above = shift(send_low, "dom", -1)

    partial_flux, hi, lo = pl.pallas_call(
        weights_kernel,
        out_shape=(
            shape((2 * rows, half), F32),
            shape((2 * rows, 6 * count), BF16),
            shape((2 * rows, 6 * count), BF16),
        ),
        in_specs=[vmem] * 3,
        out_specs=(vmem,) * 3,
        scratch_shapes=[
            pltpu.VMEM((atoms // GROUP, 24, atoms), F32),
            pltpu.VMEM((2 * rows, rows), BF16),
            pltpu.VMEM((2 * rows, rows), BF16),
        ],
        compiler_params=params(32),
        cost_estimate=pl.CostEstimate(
            flops=8*10**9, bytes_accessed=10**7, transcendentals=0
        ),
        name="weights",
    )(sources, other_bonds, turned)

    quarters = pl.pallas_call(
        relay_kernel,
        out_shape=[shape(turned.shape, BF16)] * (tiles - 1),
        in_specs=[anywhere] * 3 + [vmem] * len(quarters),
        out_specs=[vmem] * (tiles - 1),
        compiler_params=params(16),
        name="relay",
    )(partial_flux, below, above, *quarters)
    given = [turned, turned_other]
    for quarter in quarters:
        given += [quarter, shift(quarter, "dir", 1)]

    def flux_of(e):
        return pl.pallas_call(
            functools.partial(flux_kernel, e),
            out_shape=shape((rows, half), BF16),
            in_specs=[vmem] * 5,
            out_specs=vmem,
            scratch_shapes=[pltpu.VMEM((6 * count, half), BF16)],
            compiler_params=params(16),
            cost_estimate=pl.CostEstimate(
                flops=10**9, bytes_accessed=10**6, transcendentals=0
            ),
            name="flux",
        )(partial_flux, hi, lo, below, above)

    scale = (3.0 * atoms * domains) ** (-0.5)
    result = shape((1, block, cols), F32)
    if domains == 4 and block == half:
        sent, kept = shape((block, half), BF16), shape((block, half), F32)
        cost = pl.CostEstimate(flops=4 * 10**8, bytes_accessed=10**6, transcendentals=0)

        def far_of(flux, after):
            return pl.pallas_call(
                far_kernel,
                out_shape=sent,
                in_specs=[anywhere] + [vmem] * (1 + len(given)),
                out_specs=vmem,
                compiler_params=params(16),
                cost_estimate=cost,
                name="far",
            )(after, flux, *given)

        flux0, flux1 = flux_of(0), flux_of(1)
        far0 = far_of(flux0, flux1)
        far1 = far_of(flux1, far0)
        far0, far1 = swap(far0, 1, 0), swap(far1, 1, 0)
        near0, near1, add0, add1, keep, give = pl.pallas_call(
            near_kernel,
            out_shape=(sent, sent, kept, kept, kept, sent),
            in_specs=[vmem] * (2 + len(given)),
            out_specs=(vmem,) * 6,
            compiler_params=params(16),
            cost_estimate=cost,
            name="near",
        )(flux0, flux1, *given)

        def sum_of(far, add, *handed_on):
            return pl.pallas_call(
                add_kernel,
                out_shape=[sent] * (1 + len(handed_on)),
                in_specs=[vmem] * (2 + len(handed_on)),
                out_specs=[vmem] * (1 + len(handed_on)),
                compiler_params=params(16),
                name="add",
            )(far, add, *handed_on)

        near0 = swap(near0, 1, 0)
        sum0 = swap(sum_of(far0, add0)[0], 2, 0)
        sum1, near1, give = sum_of(far1, add1, near1, give)
        sum1, near1, give = swap(sum1, 2, 1), swap(near1, 1, 1), swap(give, 0, 1)
        return pl.pallas_call(
            lambda *refs: halving_sum_kernel(scale, *refs),
            out_shape=result,
            in_specs=[vmem] * 6,
            out_specs=hbm,
            scratch_shapes=[
                pltpu.VMEM((2, block, half), F32),
                pltpu.SemaphoreType.DMA((2,)),
            ],
            compiler_params=params(16),
            name="total",
        )(keep, give, near0, near1, sum0, sum1)

    terms = pl.pallas_call(
        couple_kernel,
        out_shape=shape((2 * domains, block, half), BF16),
        in_specs=[vmem] * (2 + len(given)),
        out_specs=vmem,
        compiler_params=params(16),
        name="couple",
    )(flux_of(0), flux_of(1), *given)
    terms = lax.all_to_all(terms, ("dom", "dir"), split_axis=0, concat_axis=0, tiled=True)
    return pl.pallas_call(
        lambda *refs: sum_kernel(scale, *refs),
        out_shape=result,
        in_specs=[vmem],
        out_specs=vmem,
        compiler_params=params(),
        name="total",
    )(terms)


def solution(mesh):
    in_specs = (
        P("dom", ("panel", "blk")),
        P(None, None, "dom"),
        P("dir", None, "dom"),
        P(None, "dom"),
        P("dom"),
        P("dom"),
    )
    out_specs = P("dir", ("panel", "dom"), "blk")
    return jax.shard_map(
        per_device, mesh=mesh, in_specs=in_specs, out_specs=out_specs, check_vma=False
    )
```

```python
import functools

import jax
import jax.numpy as jnp
from jax import lax
from jax.experimental import pallas as pl
from jax.experimental.pallas import tpu as pltpu
from jax.sharding import PartitionSpec as P

GROUP = 16
BF16 = jnp.bfloat16
F32 = jnp.float32


def params(mib=24):
    return pltpu.CompilerParams(vmem_limit_bytes=mib * 1024 * 1024)


def dot(a, b, contract=((1,), (0,))):
    return lax.dot_general(a, b, (contract, ((), ())), preferred_element_type=F32)


def one_hot(mask):
    return jnp.where(mask, 1.0, 0.0).astype(BF16)


def my_columns(half):
    return pl.ds(pl.multiple_of(lax.axis_index("dir") * half, 128), half)


def prep_kernel(
    v_hbm, low_hbm, high_hbm, force_hbm, bond_hbm, near_hbm,
    turned_hbm, send_low_hbm, send_high_hbm, source_hbm, bond_out_hbm,
    v_ref, low_ref, high_ref, near_ref, turned_ref, send_low_ref, send_high_ref,
    source_ref, pick_ref, wide_ref, v_sems, in_sems, out_sems,
):
    rows, half = v_ref.shape
    atoms = rows // 3
    arriving = [
        pltpu.make_async_copy(source, target, in_sems.at[i])
        for i, (source, target) in enumerate(
            (
                (low_hbm, low_ref),
                (high_hbm, high_ref),
                (near_hbm, near_ref),
                (force_hbm, source_ref.at[0:9]),
                (bond_hbm, source_ref.at[9:10]),
            )
        )
    ]
    quarter = rows // 4
    v_in = [
        pltpu.make_async_copy(
            v_hbm.at[pl.ds(at, quarter), my_columns(half)], v_ref.at[pl.ds(at, quarter)], v_sems.at[i]
        )
        for i, at in enumerate(range(0, rows, quarter))
    ]
    for copy in v_in + arriving:
        copy.start()
    leaving = []

    def leave(ref, hbm):
        copy = pltpu.make_async_copy(ref, hbm, out_sems.at[len(leaving)])
        copy.start()
        leaving.append(copy)

    for copy in arriving[:2]:
        copy.wait()
    for i, list_ref in enumerate((high_ref, low_ref)):
        count = list_ref.shape[1]
        named = jnp.broadcast_to(list_ref[...], (128, count)).T
        lane = lax.broadcasted_iota(jnp.int32, (count, 128), 1)
        for b in range(3):
            wanted = 3 * named + b
            at = (3 * i + b) * count
            for t in range(rows // 128):
                pick_ref[at : at + count, t * 128 : (t + 1) * 128] = one_hot(
                    lane + t * 128 == wanted
                )
    for copy in v_in:
        copy.wait()
    picked = dot(pick_ref[...], v_ref[...]).astype(BF16)
    send_high_ref[...] = picked[: 3 * count]
    leave(send_high_ref, send_high_hbm)
    send_low_ref[...] = picked[3 * count :]
    leave(send_low_ref, send_low_hbm)
    for copy in arriving[2:]:
        copy.wait()
    source_ref[10] = near_ref[...].astype(F32)
    leave(source_ref.at[9:10], bond_out_hbm)
    leave(source_ref, source_hbm)
    for t in range(half // 128):
        columns = slice(t * 128, (t + 1) * 128)
        wide_ref[t] = v_ref[:, columns].astype(F32)
        for b in range(3):
            part = wide_ref[t, pl.ds(b, atoms, stride=3), :]
            turned_ref[columns, b * atoms : (b + 1) * atoms] = part.astype(BF16).T
    leave(turned_ref, turned_hbm)
    for copy in leaving:
        copy.wait()


def weights_kernel(
    source_ref, other_ref, turned_ref,
    flux_ref, hi_ref, lo_ref, table_ref, own_hi_ref, own_lo_ref,
):
    _, steps, atoms = source_ref.shape
    groups = atoms // GROUP
    halo = hi_ref.shape[1] // 3
    extent = atoms + halo
    bonds = (source_ref[9], other_ref[0])
    lane = lax.broadcasted_iota(jnp.int32, (24, atoms), 1)
    rows = []
    for k in range(steps):
        force = source_ref[0:9, k, :]
        near = source_ref[10, k : k + 1, :]
        rows.append(
            jnp.concatenate(
                [force * bonds[0][k : k + 1, :], force * bonds[1][k : k + 1, :]]
                + [jnp.broadcast_to(near, (6, atoms))],
                axis=0,
            )
        )
    bit = 1
    while bit < steps:
        taken = ((lane // GROUP) & bit) != 0
        turned = list(rows)
        for p in range(steps):
            if p & bit:
                continue
            q = p | bit
            turned[p] = jnp.where(taken, pltpu.roll(rows[q], GROUP * bit, 1), rows[p])
            turned[q] = jnp.where(taken, rows[q], pltpu.roll(rows[p], atoms - GROUP * bit, 1))
        rows = turned
        bit *= 2
    for g in range(groups):
        table_ref[g] = rows[g]

    mask = (
        lax.broadcasted_iota(jnp.int32, (GROUP, atoms), 1) % GROUP
        == lax.broadcasted_iota(jnp.int32, (GROUP, atoms), 0)
    )
    target = lax.broadcasted_iota(jnp.int32, (256, atoms), 0).astype(F32).astype(BF16)

    def group(g):
        table = table_ref[g]
        named = [(table[18:19, :] - at).astype(BF16) for at in range(0, extent, 256)]
        hot = jnp.concatenate(
            [jnp.where(target == name, BF16(1), BF16(0)) for name in named], axis=0
        )
        spread = jnp.concatenate(
            [jnp.where(mask, table[r : r + 1, :], 0.0) for r in range(18)], axis=0
        )
        top = spread.astype(BF16)
        rest = (spread - top.astype(F32)).astype(BF16)
        both = ((1,), (1,))
        dense = dot(top, hot, both) + dot(rest, hot, both)
        hi = dense.astype(BF16)
        lo = (dense - hi.astype(F32)).astype(BF16)
        for e in range(2):
            for a in range(3):
                at = pl.ds(pl.multiple_of((e * 3 + a) * atoms + g * GROUP, GROUP), GROUP)
                for b in range(3):
                    r = (e * 9 + 3 * a + b) * GROUP
                    near, far = slice(b * atoms, (b + 1) * atoms), slice(b * halo, (b + 1) * halo)
                    own_hi_ref[at, near] = hi[r : r + GROUP, :atoms]
                    own_lo_ref[at, near] = lo[r : r + GROUP, :atoms]
                    hi_ref[at, far] = hi[r : r + GROUP, atoms:]
                    lo_ref[at, far] = lo[r : r + GROUP, atoms:]

    def several(step, carry):
        for g in range(4):
            group(4 * step + g)
        return carry

    lax.fori_loop(0, groups // 4, several, 0)
    turned = turned_ref[...]
    for e in range(2):
        at = slice(3 * e * atoms, 3 * (e + 1) * atoms)
        hi, lo = own_hi_ref[at, :], own_lo_ref[at, :]
        flux_ref[at, :] = dot(hi, turned, ((1,), (1,))) + dot(lo, turned, ((1,), (1,)))


def relay_kernel(part_hbm, below_hbm, above_hbm, *refs):
    for got_ref, given_ref in zip(refs[: len(refs) // 2], refs[len(refs) // 2 :]):
        given_ref[...] = got_ref[...]


def flux_kernel(e, part_ref, hi_ref, lo_ref, below_ref, above_ref, flux_ref, halo_ref):
    count = below_ref.shape[0] // 3
    for b in range(3):
        at = 2 * b * count
        halo_ref[at : at + count] = below_ref[b * count : (b + 1) * count]
        halo_ref[at + count : at + 2 * count] = above_ref[b * count : (b + 1) * count]
    atoms = flux_ref.shape[0] // 3
    halo = halo_ref[...]
    at = slice(3 * e * atoms, 3 * (e + 1) * atoms)
    flux = part_ref[at, :] + (dot(hi_ref[at, :], halo) + dot(lo_ref[at, :], halo))
    flux_ref[...] = flux.astype(BF16)


def terms_of(quarter_refs, store):
    tiles = len(quarter_refs) // 2
    me, core = lax.axis_index("blk"), lax.axis_index("dir")
    for j in range(tiles):
        tile = lax.rem(me - j + tiles, tiles)
        for s in range(2):
            store(2 * tile + (core if s == 0 else 1 - core), quarter_refs[2 * j + s])


def couple_kernel(flux0_ref, flux1_ref, *refs):
    *quarter_refs, out_ref = refs
    half = quarter_refs[0].shape[0]
    block = out_ref.shape[1]
    core = lax.axis_index("dir")

    def store(quarter, turned_ref):
        for e, flux_ref in enumerate((flux0_ref, flux1_ref)):
            term = dot(turned_ref[...], flux_ref[...]).astype(BF16)
            for t in range(half // block):
                at = 2 * (quarter * (half // block) + t) + (core if e == 0 else 1 - core)
                out_ref[at] = term[t * block : (t + 1) * block]

    terms_of(quarter_refs, store)


def sum_kernel(scale, terms_ref, out_ref):
    pairs, block, half = terms_ref.shape
    for c in range(2):
        total = terms_ref[c].astype(F32)
        for d in range(1, pairs // 2):
            total = total + terms_ref[2 * d + c].astype(F32)
        out_ref[0, :, c * half : (c + 1) * half] = total * scale


def far_kernel(after, flux_ref, *refs):
    *quarter_refs, far_ref = refs
    home = lax.axis_index("dom")

    def store(quarter, turned_ref):
        @pl.when((quarter ^ home) == 3)
        def _():
            far_ref[...] = dot(turned_ref[...], flux_ref[...]).astype(BF16)

    terms_of(quarter_refs, store)


def near_kernel(flux0_ref, flux1_ref, *refs):
    *quarter_refs, near0_ref, near1_ref, add0_ref, add1_ref, keep_ref, give_ref = refs
    home = lax.axis_index("dom")
    outs = {0: (keep_ref, give_ref), 1: (near0_ref, near1_ref), 2: (add0_ref, add1_ref)}

    def store(quarter, turned_ref):
        for away, out_refs in outs.items():

            @pl.when((quarter ^ home) == away)
            def _():
                for flux_ref, out_ref in zip((flux0_ref, flux1_ref), out_refs):
                    out_ref[...] = dot(turned_ref[...], flux_ref[...]).astype(out_ref.dtype)

    terms_of(quarter_refs, store)


def add_kernel(far_ref, add_ref, *refs):
    held_refs, (sum_ref, *given_refs) = refs[: len(refs) // 2], refs[len(refs) // 2 :]
    sum_ref[...] = (add_ref[...] + far_ref[...].astype(F32)).astype(BF16)
    for held_ref, given_ref in zip(held_refs, given_refs):
        given_ref[...] = held_ref[...]


def halving_sum_kernel(
    scale, keep_ref, give_ref, near0_ref, near1_ref, sum0_ref, sum1_ref, out_hbm, total_ref, sems
):
    half = keep_ref.shape[1]
    core = lax.axis_index("dir")
    copies = []
    for i, (owner, first, near, far) in enumerate(
        ((core, keep_ref, near0_ref, sum0_ref), (1 - core, give_ref, near1_ref, sum1_ref))
    ):
        total = first[...].astype(F32) + near[...].astype(F32) + far[...].astype(F32)
        total_ref[i] = total * scale
        columns = pl.ds(pl.multiple_of(owner * half, 128), half)
        copies.append(
            pltpu.make_async_copy(total_ref.at[i], out_hbm.at[0, :, columns], sems.at[i])
        )
        copies[i].start()
    for copy in copies:
        copy.wait()


def shift(value, axis, by):
    length = lax.axis_size(axis)
    return lax.ppermute(value, axis, [(i, (i + by) % length) for i in range(length)])


def swap(value, away, other_core):
    domains = lax.axis_size("dom")
    pairs = [
        (2 * d + c, 2 * (d ^ away) + (c ^ other_core)) for d in range(domains) for c in range(2)
    ]
    return lax.ppermute(value, ("dom", "dir"), pairs)


def shape(dims, dtype):
    return jax.ShapeDtypeStruct(dims, dtype)


def per_device(panel_vectors, force_blocks, bond_vectors, neighbours, boundary_low, boundary_high):
    rows, cols = panel_vectors.shape
    atoms = rows // 3
    half = cols // 2
    count = boundary_low.shape[0]
    domains, tiles = lax.axis_size("dom"), lax.axis_size("blk")
    block = cols * tiles // domains
    vmem = pl.BlockSpec(memory_space=pltpu.VMEM)
    hbm = pl.BlockSpec(memory_space=pltpu.HBM)
    anywhere = pl.BlockSpec(memory_space=pl.ANY)

    lists = [boundary_low.reshape(1, count), boundary_high.reshape(1, count)]
    forces = force_blocks.transpose(1, 0, 2)
    prepared = (
        shape((half, rows), BF16),
        shape((3 * count, half), BF16),
        shape((3 * count, half), BF16),
    )
    turned, send_low, send_high, sources, bonds = pl.pallas_call(
        prep_kernel,
        out_shape=(
            *prepared,
            shape((11, *neighbours.shape), F32),
            shape(bond_vectors.shape, F32),
        ),
        in_specs=[hbm] * 6,
        out_specs=(hbm,) * 5,
        scratch_shapes=[
            pltpu.VMEM((rows, half), BF16),
            pltpu.VMEM((1, count), jnp.int32),
            pltpu.VMEM((1, count), jnp.int32),
            pltpu.VMEM(neighbours.shape, jnp.int32),
            *[pltpu.VMEM(like.shape, like.dtype) for like in prepared],
            pltpu.VMEM((11, *neighbours.shape), F32),
            pltpu.VMEM((6 * count, rows), BF16),
            pltpu.VMEM((half // 128, rows, 128), F32),
            pltpu.SemaphoreType.DMA((4,)),
            pltpu.SemaphoreType.DMA((5,)),
            pltpu.SemaphoreType.DMA((5,)),
        ],
        compiler_params=params(58),
        name="prep",
    )(panel_vectors, *lists, forces, bond_vectors, neighbours)
    quarters = [shift(turned, "blk", j) for j in range(1, tiles)]
    turned_other = shift(turned, "dir", 1)
    other_bonds = shift(bonds, "dir", 1)
    below = shift(send_high, "dom", 1)
    above = shift(send_low, "dom", -1)

    partial_flux, hi, lo = pl.pallas_call(
        weights_kernel,
        out_shape=(
            shape((2 * rows, half), F32),
            shape((2 * rows, 6 * count), BF16),
            shape((2 * rows, 6 * count), BF16),
        ),
        in_specs=[vmem] * 3,
        out_specs=(vmem,) * 3,
        scratch_shapes=[
            pltpu.VMEM((atoms // GROUP, 24, atoms), F32),
            pltpu.VMEM((2 * rows, rows), BF16),
            pltpu.VMEM((2 * rows, rows), BF16),
        ],
        compiler_params=params(32),
        cost_estimate=pl.CostEstimate(
            flops=8*10**9, bytes_accessed=10**7, transcendentals=0
        ),
        name="weights",
    )(sources, other_bonds, turned)

    quarters = pl.pallas_call(
        relay_kernel,
        out_shape=[shape(turned.shape, BF16)] * (tiles - 1),
        in_specs=[anywhere] * 3 + [vmem] * len(quarters),
        out_specs=[vmem] * (tiles - 1),
        compiler_params=params(16),
        name="relay",
    )(partial_flux, below, above, *quarters)
    given = [turned, turned_other]
    for quarter in quarters:
        given += [quarter, shift(quarter, "dir", 1)]

    def flux_of(e):
        return pl.pallas_call(
            functools.partial(flux_kernel, e),
            out_shape=shape((rows, half), BF16),
            in_specs=[vmem] * 5,
            out_specs=vmem,
            scratch_shapes=[pltpu.VMEM((6 * count, half), BF16)],
            compiler_params=params(16),
            cost_estimate=pl.CostEstimate(
                flops=10**9, bytes_accessed=10**6, transcendentals=0
            ),
            name="flux",
        )(partial_flux, hi, lo, below, above)

    scale = (3.0 * atoms * domains) ** (-0.5)
    result = shape((1, block, cols), F32)
    if domains == 4 and block == half:
        sent, kept = shape((block, half), BF16), shape((block, half), F32)
        cost = pl.CostEstimate(flops=4 * 10**8, bytes_accessed=10**6, transcendentals=0)

        def far_of(flux, after):
            return pl.pallas_call(
                far_kernel,
                out_shape=sent,
                in_specs=[anywhere] + [vmem] * (1 + len(given)),
                out_specs=vmem,
                compiler_params=params(16),
                cost_estimate=cost,
                name="far",
            )(after, flux, *given)

        flux0, flux1 = flux_of(0), flux_of(1)
        far0 = far_of(flux0, flux1)
        far1 = far_of(flux1, far0)
        far0, far1 = swap(far0, 1, 0), swap(far1, 1, 0)
        near0, near1, add0, add1, keep, give = pl.pallas_call(
            near_kernel,
            out_shape=(sent, sent, kept, kept, kept, sent),
            in_specs=[vmem] * (2 + len(given)),
            out_specs=(vmem,) * 6,
            compiler_params=params(16),
            cost_estimate=cost,
            name="near",
        )(flux0, flux1, *given)

        def sum_of(far, add, *handed_on):
            return pl.pallas_call(
                add_kernel,
                out_shape=[sent] * (1 + len(handed_on)),
                in_specs=[vmem] * (2 + len(handed_on)),
                out_specs=[vmem] * (1 + len(handed_on)),
                compiler_params=params(16),
                name="add",
            )(far, add, *handed_on)

        near0 = swap(near0, 1, 0)
        sum0 = swap(sum_of(far0, add0)[0], 2, 0)
        sum1, near1, give = sum_of(far1, add1, near1, give)
        sum1, near1, give = swap(sum1, 2, 1), swap(near1, 1, 1), swap(give, 0, 1)
        return pl.pallas_call(
            lambda *refs: halving_sum_kernel(scale, *refs),
            out_shape=result,
            in_specs=[vmem] * 6,
            out_specs=hbm,
            scratch_shapes=[
                pltpu.VMEM((2, block, half), F32),
                pltpu.SemaphoreType.DMA((2,)),
            ],
            compiler_params=params(16),
            name="total",
        )(keep, give, near0, near1, sum0, sum1)

    terms = pl.pallas_call(
        couple_kernel,
        out_shape=shape((2 * domains, block, half), BF16),
        in_specs=[vmem] * (2 + len(given)),
        out_specs=vmem,
        compiler_params=params(16),
        name="couple",
    )(flux_of(0), flux_of(1), *given)
    terms = lax.all_to_all(terms, ("dom", "dir"), split_axis=0, concat_axis=0, tiled=True)
    return pl.pallas_call(
        lambda *refs: sum_kernel(scale, *refs),
        out_shape=result,
        in_specs=[vmem],
        out_specs=vmem,
        compiler_params=params(),
        name="total",
    )(terms)


def solution(mesh):
    in_specs = (
        P("dom", ("panel", "blk")),
        P(None, None, "dom"),
        P("dir", None, "dom"),
        P(None, "dom"),
        P("dom"),
        P("dom"),
    )
    out_specs = P("dir", ("panel", "dom"), "blk")
    return jax.shard_map(
        per_device, mesh=mesh, in_specs=in_specs, out_specs=out_specs, check_vma=False
    )
```

```python
import functools

import jax
import jax.numpy as jnp
from jax import lax
from jax.experimental import pallas as pl
from jax.experimental.pallas import tpu as pltpu
from jax.sharding import PartitionSpec as P

GROUP = 16
BF16 = jnp.bfloat16
F32 = jnp.float32


def params(mib=24):
    return pltpu.CompilerParams(vmem_limit_bytes=mib * 1024 * 1024)


def dot(a, b, contract=((1,), (0,))):
    return lax.dot_general(a, b, (contract, ((), ())), preferred_element_type=F32)


def one_hot(mask):
    return jnp.where(mask, 1.0, 0.0).astype(BF16)


def my_columns(half):
    return pl.ds(pl.multiple_of(lax.axis_index("dir") * half, 128), half)


def prep_kernel(
    v_hbm, low_hbm, high_hbm, force_hbm, bond_hbm, near_hbm,
    turned_hbm, send_low_hbm, send_high_hbm, source_hbm, bond_out_hbm,
    v_ref, low_ref, high_ref, near_ref, turned_ref, send_low_ref, send_high_ref,
    source_ref, pick_ref, wide_ref, v_sems, in_sems, out_sems,
):
    rows, half = v_ref.shape
    atoms = rows // 3
    arriving = [
        pltpu.make_async_copy(source, target, in_sems.at[i])
        for i, (source, target) in enumerate(
            (
                (low_hbm, low_ref),
                (high_hbm, high_ref),
                (near_hbm, near_ref),
                (force_hbm, source_ref.at[0:9]),
                (bond_hbm, source_ref.at[9:10]),
            )
        )
    ]
    quarter = rows // 4
    v_in = [
        pltpu.make_async_copy(
            v_hbm.at[pl.ds(at, quarter), my_columns(half)], v_ref.at[pl.ds(at, quarter)], v_sems.at[i]
        )
        for i, at in enumerate(range(0, rows, quarter))
    ]
    for copy in arriving + v_in:
        copy.start()
    leaving = []

    def leave(ref, hbm):
        copy = pltpu.make_async_copy(ref, hbm, out_sems.at[len(leaving)])
        copy.start()
        leaving.append(copy)

    for copy in arriving:
        copy.wait()
    source_ref[10] = near_ref[...].astype(F32)
    leave(source_ref.at[9:10], bond_out_hbm)
    leave(source_ref, source_hbm)
    for i, list_ref in enumerate((high_ref, low_ref)):
        count = list_ref.shape[1]
        named = jnp.broadcast_to(list_ref[...], (128, count)).T
        lane = lax.broadcasted_iota(jnp.int32, (count, 128), 1)
        for b in range(3):
            wanted = 3 * named + b
            at = (3 * i + b) * count
            for t in range(rows // 128):
                pick_ref[at : at + count, t * 128 : (t + 1) * 128] = one_hot(
                    lane + t * 128 == wanted
                )
    for copy in v_in:
        copy.wait()
    picked = dot(pick_ref[...], v_ref[...]).astype(BF16)
    send_high_ref[...] = picked[: 3 * count]
    leave(send_high_ref, send_high_hbm)
    send_low_ref[...] = picked[3 * count :]
    leave(send_low_ref, send_low_hbm)
    for t in range(half // 128):
        columns = slice(t * 128, (t + 1) * 128)
        wide_ref[t] = v_ref[:, columns].astype(F32)
        for b in range(3):
            part = wide_ref[t, pl.ds(b, atoms, stride=3), :]
            turned_ref[columns, b * atoms : (b + 1) * atoms] = part.astype(BF16).T
    leave(turned_ref, turned_hbm)
    for copy in leaving:
        copy.wait()


def weights_kernel(
    source_ref, other_ref, turned_ref,
    flux_ref, hi_ref, lo_ref, table_ref, own_hi_ref, own_lo_ref,
):
    _, steps, atoms = source_ref.shape
    groups = atoms // GROUP
    halo = hi_ref.shape[1] // 3
    extent = atoms + halo
    bonds = (source_ref[9], other_ref[0])
    lane = lax.broadcasted_iota(jnp.int32, (24, atoms), 1)
    rows = []
    for k in range(steps):
        force = source_ref[0:9, k, :]
        near = source_ref[10, k : k + 1, :]
        rows.append(
            jnp.concatenate(
                [force * bonds[0][k : k + 1, :], force * bonds[1][k : k + 1, :]]
                + [jnp.broadcast_to(near, (6, atoms))],
                axis=0,
            )
        )
    bit = 1
    while bit < steps:
        taken = ((lane // GROUP) & bit) != 0
        turned = list(rows)
        for p in range(steps):
            if p & bit:
                continue
            q = p | bit
            turned[p] = jnp.where(taken, pltpu.roll(rows[q], GROUP * bit, 1), rows[p])
            turned[q] = jnp.where(taken, rows[q], pltpu.roll(rows[p], atoms - GROUP * bit, 1))
        rows = turned
        bit *= 2
    for g in range(groups):
        table_ref[g] = rows[g]

    mask = (
        lax.broadcasted_iota(jnp.int32, (GROUP, atoms), 1) % GROUP
        == lax.broadcasted_iota(jnp.int32, (GROUP, atoms), 0)
    )
    target = lax.broadcasted_iota(jnp.int32, (256, atoms), 0).astype(F32).astype(BF16)

    def group(g):
        table = table_ref[g]
        named = [(table[18:19, :] - at).astype(BF16) for at in range(0, extent, 256)]
        hot = jnp.concatenate(
            [jnp.where(target == name, BF16(1), BF16(0)) for name in named], axis=0
        )
        spread = jnp.concatenate(
            [jnp.where(mask, table[r : r + 1, :], 0.0) for r in range(18)], axis=0
        )
        top = spread.astype(BF16)
        rest = (spread - top.astype(F32)).astype(BF16)
        both = ((1,), (1,))
        dense = dot(top, hot, both) + dot(rest, hot, both)
        hi = dense.astype(BF16)
        lo = (dense - hi.astype(F32)).astype(BF16)
        for e in range(2):
            for a in range(3):
                at = pl.ds(pl.multiple_of((e * 3 + a) * atoms + g * GROUP, GROUP), GROUP)
                for b in range(3):
                    r = (e * 9 + 3 * a + b) * GROUP
                    near, far = slice(b * atoms, (b + 1) * atoms), slice(b * halo, (b + 1) * halo)
                    own_hi_ref[at, near] = hi[r : r + GROUP, :atoms]
                    own_lo_ref[at, near] = lo[r : r + GROUP, :atoms]
                    hi_ref[at, far] = hi[r : r + GROUP, atoms:]
                    lo_ref[at, far] = lo[r : r + GROUP, atoms:]

    def several(step, carry):
        for g in range(4):
            group(4 * step + g)
        return carry

    lax.fori_loop(0, groups // 4, several, 0)
    turned = turned_ref[...]
    for e in range(2):
        at = slice(3 * e * atoms, 3 * (e + 1) * atoms)
        hi, lo = own_hi_ref[at, :], own_lo_ref[at, :]
        flux_ref[at, :] = dot(hi, turned, ((1,), (1,))) + dot(lo, turned, ((1,), (1,)))


def relay_kernel(part_hbm, below_hbm, above_hbm, *refs):
    for got_ref, given_ref in zip(refs[: len(refs) // 2], refs[len(refs) // 2 :]):
        given_ref[...] = got_ref[...]


def flux_kernel(e, part_ref, hi_ref, lo_ref, below_ref, above_ref, flux_ref, halo_ref):
    count = below_ref.shape[0] // 3
    for b in range(3):
        at = 2 * b * count
        halo_ref[at : at + count] = below_ref[b * count : (b + 1) * count]
        halo_ref[at + count : at + 2 * count] = above_ref[b * count : (b + 1) * count]
    atoms = flux_ref.shape[0] // 3
    halo = halo_ref[...]
    at = slice(3 * e * atoms, 3 * (e + 1) * atoms)
    flux = part_ref[at, :] + (dot(hi_ref[at, :], halo) + dot(lo_ref[at, :], halo))
    flux_ref[...] = flux.astype(BF16)


def terms_of(quarter_refs, store):
    tiles = len(quarter_refs) // 2
    me, core = lax.axis_index("blk"), lax.axis_index("dir")
    for j in range(tiles):
        tile = lax.rem(me - j + tiles, tiles)
        for s in range(2):
            store(2 * tile + (core if s == 0 else 1 - core), quarter_refs[2 * j + s])


def couple_kernel(flux0_ref, flux1_ref, *refs):
    *quarter_refs, out_ref = refs
    half = quarter_refs[0].shape[0]
    block = out_ref.shape[1]
    core = lax.axis_index("dir")

    def store(quarter, turned_ref):
        for e, flux_ref in enumerate((flux0_ref, flux1_ref)):
            term = dot(turned_ref[...], flux_ref[...]).astype(BF16)
            for t in range(half // block):
                at = 2 * (quarter * (half // block) + t) + (core if e == 0 else 1 - core)
                out_ref[at] = term[t * block : (t + 1) * block]

    terms_of(quarter_refs, store)


def sum_kernel(scale, terms_ref, out_ref):
    pairs, block, half = terms_ref.shape
    for c in range(2):
        total = terms_ref[c].astype(F32)
        for d in range(1, pairs // 2):
            total = total + terms_ref[2 * d + c].astype(F32)
        out_ref[0, :, c * half : (c + 1) * half] = total * scale


def far_kernel(after, flux_ref, *refs):
    *quarter_refs, far_ref = refs
    home = lax.axis_index("dom")

    def store(quarter, turned_ref):
        @pl.when((quarter ^ home) == 3)
        def _():
            far_ref[...] = dot(turned_ref[...], flux_ref[...]).astype(BF16)

    terms_of(quarter_refs, store)


def near_kernel(flux0_ref, flux1_ref, *refs):
    *quarter_refs, near0_ref, near1_ref, add0_ref, add1_ref, keep_ref, give_ref = refs
    home = lax.axis_index("dom")
    outs = {0: (keep_ref, give_ref), 1: (near0_ref, near1_ref), 2: (add0_ref, add1_ref)}

    def store(quarter, turned_ref):
        for away, out_refs in outs.items():

            @pl.when((quarter ^ home) == away)
            def _():
                for flux_ref, out_ref in zip((flux0_ref, flux1_ref), out_refs):
                    out_ref[...] = dot(turned_ref[...], flux_ref[...]).astype(out_ref.dtype)

    terms_of(quarter_refs, store)


def add_kernel(far_ref, add_ref, *refs):
    held_refs, (sum_ref, *given_refs) = refs[: len(refs) // 2], refs[len(refs) // 2 :]
    sum_ref[...] = (add_ref[...] + far_ref[...].astype(F32)).astype(BF16)
    for held_ref, given_ref in zip(held_refs, given_refs):
        given_ref[...] = held_ref[...]


def halving_sum_kernel(
    scale, keep_ref, give_ref, near0_ref, near1_ref, sum0_ref, sum1_ref, out_hbm, total_ref, sems
):
    half = keep_ref.shape[1]
    core = lax.axis_index("dir")
    copies = []
    for i, (owner, first, near, far) in enumerate(
        ((core, keep_ref, near0_ref, sum0_ref), (1 - core, give_ref, near1_ref, sum1_ref))
    ):
        total = first[...].astype(F32) + near[...].astype(F32) + far[...].astype(F32)
        total_ref[i] = total * scale
        columns = pl.ds(pl.multiple_of(owner * half, 128), half)
        copies.append(
            pltpu.make_async_copy(total_ref.at[i], out_hbm.at[0, :, columns], sems.at[i])
        )
        copies[i].start()
    for copy in copies:
        copy.wait()


def shift(value, axis, by):
    length = lax.axis_size(axis)
    return lax.ppermute(value, axis, [(i, (i + by) % length) for i in range(length)])


def swap(value, away, other_core):
    domains = lax.axis_size("dom")
    pairs = [
        (2 * d + c, 2 * (d ^ away) + (c ^ other_core)) for d in range(domains) for c in range(2)
    ]
    return lax.ppermute(value, ("dom", "dir"), pairs)


def shape(dims, dtype):
    return jax.ShapeDtypeStruct(dims, dtype)


def per_device(panel_vectors, force_blocks, bond_vectors, neighbours, boundary_low, boundary_high):
    rows, cols = panel_vectors.shape
    atoms = rows // 3
    half = cols // 2
    count = boundary_low.shape[0]
    domains, tiles = lax.axis_size("dom"), lax.axis_size("blk")
    block = cols * tiles // domains
    vmem = pl.BlockSpec(memory_space=pltpu.VMEM)
    hbm = pl.BlockSpec(memory_space=pltpu.HBM)
    anywhere = pl.BlockSpec(memory_space=pl.ANY)

    lists = [boundary_low.reshape(1, count), boundary_high.reshape(1, count)]
    forces = force_blocks.transpose(1, 0, 2)
    prepared = (
        shape((half, rows), BF16),
        shape((3 * count, half), BF16),
        shape((3 * count, half), BF16),
    )
    turned, send_low, send_high, sources, bonds = pl.pallas_call(
        prep_kernel,
        out_shape=(
            *prepared,
            shape((11, *neighbours.shape), F32),
            shape(bond_vectors.shape, F32),
        ),
        in_specs=[hbm] * 6,
        out_specs=(hbm,) * 5,
        scratch_shapes=[
            pltpu.VMEM((rows, half), BF16),
            pltpu.VMEM((1, count), jnp.int32),
            pltpu.VMEM((1, count), jnp.int32),
            pltpu.VMEM(neighbours.shape, jnp.int32),
            *[pltpu.VMEM(like.shape, like.dtype) for like in prepared],
            pltpu.VMEM((11, *neighbours.shape), F32),
            pltpu.VMEM((6 * count, rows), BF16),
            pltpu.VMEM((half // 128, rows, 128), F32),
            pltpu.SemaphoreType.DMA((4,)),
            pltpu.SemaphoreType.DMA((5,)),
            pltpu.SemaphoreType.DMA((5,)),
        ],
        compiler_params=params(58),
        name="prep",
    )(panel_vectors, *lists, forces, bond_vectors, neighbours)
    quarters = [shift(turned, "blk", j) for j in range(1, tiles)]
    turned_other = shift(turned, "dir", 1)
    other_bonds = shift(bonds, "dir", 1)
    below = shift(send_high, "dom", 1)
    above = shift(send_low, "dom", -1)

    partial_flux, hi, lo = pl.pallas_call(
        weights_kernel,
        out_shape=(
            shape((2 * rows, half), F32),
            shape((2 * rows, 6 * count), BF16),
            shape((2 * rows, 6 * count), BF16),
        ),
        in_specs=[vmem] * 3,
        out_specs=(vmem,) * 3,
        scratch_shapes=[
            pltpu.VMEM((atoms // GROUP, 24, atoms), F32),
            pltpu.VMEM((2 * rows, rows), BF16),
            pltpu.VMEM((2 * rows, rows), BF16),
        ],
        compiler_params=params(32),
        cost_estimate=pl.CostEstimate(
            flops=8*10**9, bytes_accessed=10**7, transcendentals=0
        ),
        name="weights",
    )(sources, other_bonds, turned)

    quarters = pl.pallas_call(
        relay_kernel,
        out_shape=[shape(turned.shape, BF16)] * (tiles - 1),
        in_specs=[anywhere] * 3 + [vmem] * len(quarters),
        out_specs=[vmem] * (tiles - 1),
        compiler_params=params(16),
        name="relay",
    )(partial_flux, below, above, *quarters)
    given = [turned, turned_other]
    for quarter in quarters:
        given += [quarter, shift(quarter, "dir", 1)]

    def flux_of(e):
        return pl.pallas_call(
            functools.partial(flux_kernel, e),
            out_shape=shape((rows, half), BF16),
            in_specs=[vmem] * 5,
            out_specs=vmem,
            scratch_shapes=[pltpu.VMEM((6 * count, half), BF16)],
            compiler_params=params(16),
            cost_estimate=pl.CostEstimate(
                flops=10**9, bytes_accessed=10**6, transcendentals=0
            ),
            name="flux",
        )(partial_flux, hi, lo, below, above)

    scale = (3.0 * atoms * domains) ** (-0.5)
    result = shape((1, block, cols), F32)
    if domains == 4 and block == half:
        sent, kept = shape((block, half), BF16), shape((block, half), F32)
        cost = pl.CostEstimate(flops=4 * 10**8, bytes_accessed=10**6, transcendentals=0)

        def far_of(flux, after):
            return pl.pallas_call(
                far_kernel,
                out_shape=sent,
                in_specs=[anywhere] + [vmem] * (1 + len(given)),
                out_specs=vmem,
                compiler_params=params(16),
                cost_estimate=cost,
                name="far",
            )(after, flux, *given)

        flux0, flux1 = flux_of(0), flux_of(1)
        far0 = far_of(flux0, flux1)
        far0 = swap(far0, 1, 0)
        near0, near1, add0, add1, keep, give = pl.pallas_call(
            near_kernel,
            out_shape=(sent, sent, kept, kept, kept, sent),
            in_specs=[vmem] * (2 + len(given)),
            out_specs=(vmem,) * 6,
            compiler_params=params(16),
            cost_estimate=cost,
            name="near",
        )(flux0, flux1, *given)
        far1 = swap(far_of(flux1, near0), 1, 0)

        def sum_of(far, add, *handed_on):
            return pl.pallas_call(
                add_kernel,
                out_shape=[sent] * (1 + len(handed_on)),
                in_specs=[vmem] * (2 + len(handed_on)),
                out_specs=[vmem] * (1 + len(handed_on)),
                compiler_params=params(16),
                name="add",
            )(far, add, *handed_on)

        near0 = swap(near0, 1, 0)
        sum0 = swap(sum_of(far0, add0)[0], 2, 0)
        sum1, near1, give = sum_of(far1, add1, near1, give)
        sum1, near1, give = swap(sum1, 2, 1), swap(near1, 1, 1), swap(give, 0, 1)
        return pl.pallas_call(
            lambda *refs: halving_sum_kernel(scale, *refs),
            out_shape=result,
            in_specs=[vmem] * 6,
            out_specs=hbm,
            scratch_shapes=[
                pltpu.VMEM((2, block, half), F32),
                pltpu.SemaphoreType.DMA((2,)),
            ],
            compiler_params=params(16),
            name="total",
        )(keep, give, near0, near1, sum0, sum1)

    terms = pl.pallas_call(
        couple_kernel,
        out_shape=shape((2 * domains, block, half), BF16),
        in_specs=[vmem] * (2 + len(given)),
        out_specs=vmem,
        compiler_params=params(16),
        name="couple",
    )(flux_of(0), flux_of(1), *given)
    terms = lax.all_to_all(terms, ("dom", "dir"), split_axis=0, concat_axis=0, tiled=True)
    return pl.pallas_call(
        lambda *refs: sum_kernel(scale, *refs),
        out_shape=result,
        in_specs=[vmem],
        out_specs=vmem,
        compiler_params=params(),
        name="total",
    )(terms)


def solution(mesh):
    in_specs = (
        P("dom", ("panel", "blk")),
        P(None, None, "dom"),
        P("dir", None, "dom"),
        P(None, "dom"),
        P("dom"),
        P("dom"),
    )
    out_specs = P("dir", ("panel", "dom"), "blk")
    return jax.shard_map(
        per_device, mesh=mesh, in_specs=in_specs, out_specs=out_specs, check_vma=False
    )
```
